128 devices in a mesh: section: 2 (over core), fsdp: 16 (over x, z), rep: 4 (over y).
Axes of the slice: x: 4, y: 4, z: 4, core: 2. Of those that a mesh axis runs over, the one named last changes fastest.
Arguments:
- layer_in: bfloat16 [2, 64, 64, 768], P(None, ('fsdp', 'rep')), may hold values from -6 to 6
- cotangent: bfloat16 [2, 64, 64, 768], P(None, ('fsdp', 'rep')), may hold values from -6 to 6
- encoder: bfloat16 [2, 64, 256, 768], P(None, ('fsdp', 'rep')), may hold values from -6 to 6
- dec_segments: int32 [2, 64, 64], P(None, ('fsdp', 'rep')), may hold values from 0 to 3, as said below
- enc_segments: int32 [2, 64, 256], P(None, ('fsdp', 'rep')), may hold values from 0 to 3, as said below
- norm_gains: bfloat16 [2, 3, 768], P('section', None, 'fsdp'), may hold values from 0.5 to 1.5
- self_query: bfloat16 [2, 768, 768], P('section', 'fsdp'), may hold values from -0.02734375 to 0.02734375
- self_kv: bfloat16 [2, 768, 2, 768], P('section', 'fsdp'), may hold values from -0.21875 to 0.21875
- self_out: bfloat16 [2, 768, 768], P('section', 'fsdp'), may hold values from -0.875 to 0.875
- rel_bias: bfloat16 [2, 32, 12], P('section', 'fsdp'), may hold values from -6 to 6
- cross_query: bfloat16 [2, 768, 768], P('section', 'fsdp'), may hold values from -0.02734375 to 0.02734375
- cross_kv: bfloat16 [2, 768, 2, 768], P('section', 'fsdp'), may hold values from -0.21875 to 0.21875
- cross_out: bfloat16 [2, 768, 768], P('section', 'fsdp'), may hold values from -1.25 to 1.25
- ffn_in: bfloat16 [2, 768, 2, 2048], P('section', 'fsdp'), may hold values from -0.21875 to 0.21875
- ffn_out: bfloat16 [2, 2048, 768], P('section', 'fsdp'), may hold values from -0.25 to 0.25
Outputs:
- layer_out: bfloat16 [2, 2, 64, 64, 768], P('section', None, ('fsdp', 'rep'))
- layer_grad: bfloat16 [2, 2, 64, 64, 768], P('section', None, ('fsdp', 'rep'))
- encoder_grad: float32 [2, 64, 256, 768], P(None, ('fsdp', 'rep'))
- grad_norm_gains: float32 [2, 3, 768], P('section', None, 'fsdp')
- grad_self_query: float32 [2, 768, 768], P('section', 'fsdp')
- grad_self_kv: float32 [2, 768, 2, 768], P('section', 'fsdp')
- grad_self_out: float32 [2, 768, 768], P('section', 'fsdp')
- grad_rel_bias: float32 [2, 32, 12], P('section', 'fsdp')
- grad_cross_query: float32 [2, 768, 768], P('section', 'fsdp')
- grad_cross_kv: float32 [2, 768, 2, 768], P('section', 'fsdp')
- grad_cross_out: float32 [2, 768, 768], P('section', 'fsdp')
- grad_ffn_in: float32 [2, 768, 2, 2048], P('section', 'fsdp')
- grad_ffn_out: float32 [2, 2048, 768], P('section', 'fsdp')
The draws below stay inside these ranges and needn't reach their ends.
Inputs may be any that keep to these rules, and one draw needn't show every extreme that they name: `dec_segments`: within each packed row the ids start at 0 and rise by one at each of 3 places, so every id of 0 to 3 is present. `enc_segments`: within each row of encoder states the ids start at 0 and rise by one at each of 3 places, so every id of 0 to 3 is present.
All inputs are finite; a program needn't handle non-finite values.
Results may differ from the reference program's by a relative error of at most 0.035.
Values may be sent and summed in bfloat16 or wider, within the bound.
No kernel may reach another device: no remote copies, remote signals or barrier semaphores. Data moves between devices by JAX's collectives and lax.ppermute only.
A program may use at most 128 MiB of HBM per device.

```python
import jax
import jax.numpy as jnp
import numpy as np
from jax import lax

D = 768
HEADS = 12
HEAD = 64
FF = 2048
BUCKETS = 32
MAX_DIST = 128
MB = 2
SEGS = 4
TOK_MB = 64
ENC_MB = 256
ROWS = 64
N_SECTION = 2


def segment_ids(key, row_count, length, count):
    scores = jax.random.randint(key, (row_count, length - 1), 0, 1 << 20) * length + jnp.arange(length - 1)
    order = jnp.argsort(scores, axis=-1, stable=True)
    cuts = jnp.sort(order[:, :count - 1], axis=-1) + 1
    places = jnp.arange(length)
    return jnp.sum((places[None, :, None] >= cuts[:, None, :]).astype(jnp.int32), axis=-1)


def draw_dec_segments(key, part):
    key = jax.random.fold_in(key, 11)
    return segment_ids(key, MB * ROWS, TOK_MB, SEGS).reshape(MB, ROWS, TOK_MB)


def draw_enc_segments(key, part):
    key = jax.random.fold_in(key, 23)
    return segment_ids(key, MB * ROWS, ENC_MB, SEGS).reshape(MB, ROWS, ENC_MB)


def level_of(stream_key, shape, split, least, largest):
    factor_of = 1.0
    for dim, blocks in split:
        heights = jax.random.uniform(jax.random.fold_in(jax.random.fold_in(stream_key, 6), dim), (blocks,), jnp.float32, least / len(split), largest / len(split))
        factor_of = factor_of * jnp.repeat(jnp.exp(heights), shape[dim] // blocks).reshape((-1,) + (1,) * (len(shape) - 1 - dim))
    return factor_of


def scatter_about(rng, extent, spread, bound, cuts=(), kind=jnp.bfloat16):
    values = jax.random.normal(rng, extent, jnp.float32) * spread
    if len(cuts) > 0:
        values = level_of(rng, extent, cuts, -0.22, 0.18) * values
    return jnp.clip(values, min=-bound, max=bound).astype(kind)


def setup_inputs(seed: int = 0) -> dict:
    arg_keys = jax.random.split(jax.random.key(seed), 16)
    layer_in = scatter_about(arg_keys[0], (MB, ROWS, TOK_MB, D), 1.0, 6.0, ((1, 64),))
    cotangent = scatter_about(arg_keys[1], (MB, ROWS, TOK_MB, D), 1.0, 6.0, ((1, 64),))
    encoder = scatter_about(arg_keys[2], (MB, ROWS, ENC_MB, D), 1.0, 6.0, ((1, 64),))
    dec_segments = draw_dec_segments(jax.random.fold_in(arg_keys[15], 71), 0)
    enc_segments = draw_enc_segments(jax.random.fold_in(arg_keys[15], 71), 0)
    norm_gains = jnp.clip(1.0 + 0.1 * jax.random.normal(arg_keys[5], (N_SECTION, 3, D), jnp.float32), 0.5, 1.5).astype(jnp.bfloat16)
    self_query = scatter_about(arg_keys[6], (N_SECTION, D, HEADS * HEAD), (D * HEAD) ** -0.5, 0.02734375, ((0, 2), (1, 16)))
    self_kv = scatter_about(arg_keys[7], (N_SECTION, D, 2, HEADS * HEAD), D ** -0.5, 0.21875, ((0, 2), (1, 16)))
    self_out = scatter_about(arg_keys[8], (N_SECTION, HEADS * HEAD, D), (D // 16) ** -0.5, 0.875, ((0, 2), (1, 16)))
    rel_bias = scatter_about(arg_keys[9], (N_SECTION, BUCKETS, HEADS), 1.0, 6.0, ((0, 2), (1, 16)))
    cross_query = scatter_about(arg_keys[10], (N_SECTION, D, HEADS * HEAD), (D * HEAD) ** -0.5, 0.02734375, ((0, 2), (1, 16)))
    cross_kv = scatter_about(arg_keys[11], (N_SECTION, D, 2, HEADS * HEAD), D ** -0.5, 0.21875, ((0, 2), (1, 16)))
    cross_out = scatter_about(arg_keys[12], (N_SECTION, HEADS * HEAD, D), (D // 32) ** -0.5, 1.25, ((0, 2), (1, 16)))
    ffn_in = scatter_about(arg_keys[13], (N_SECTION, D, 2, FF), D ** -0.5, 0.21875, ((0, 2), (1, 16)))
    ffn_out = scatter_about(arg_keys[14], (N_SECTION, FF, D), (FF // 4) ** -0.5, 0.25, ((0, 2), (1, 16)))
    return {"layer_in": layer_in, "cotangent": cotangent, "encoder": encoder, "dec_segments": dec_segments, "enc_segments": enc_segments, "norm_gains": norm_gains, "self_query": self_query, "self_kv": self_kv, "self_out": self_out, "rel_bias": rel_bias, "cross_query": cross_query, "cross_kv": cross_kv, "cross_out": cross_out, "ffn_in": ffn_in, "ffn_out": ffn_out}


epsilon = 1e-06
highest = lax.Precision.HIGHEST

@jax.custom_vjp
def low(v):
    return lax.optimization_barrier(v.astype(jnp.bfloat16)).astype(jnp.float32)

@jax.custom_vjp
def low_back(v):
    return v

def low_keep(v):
    return (low(v), None)

def low_pass(kept, grad):
    return (grad,)

def back_keep(v):
    return (v, None)

def back_low(kept, grad):
    return (low(grad),)
low.defvjp(low_keep, low_pass)
low_back.defvjp(back_keep, back_low)

def bucket_row(length):
    distance = np.arange(length)
    half_count = BUCKETS // 2
    scaled = np.log(np.maximum(distance, half_count) / half_count) / np.log(MAX_DIST / half_count) * (BUCKETS - half_count)
    far_bucket = np.minimum(half_count + np.floor(scaled).astype(np.int32), BUCKETS - 1)
    return np.where(distance < half_count, distance, far_bucket).astype(np.int32)

def normalize(value, gain):
    return value * lax.rsqrt(lax.optimization_barrier(jnp.mean(value * value, axis=-1, keepdims=True)) + epsilon) * gain

def attend(queries, key_rows, value_rows, position_bias, allowed):
    length = queries.shape[0]
    query_heads = queries.reshape(length, HEADS, HEAD)
    key_heads = key_rows.reshape(key_rows.shape[0], HEADS, HEAD)
    value_heads = value_rows.reshape(value_rows.shape[0], HEADS, HEAD)
    scores = low_back(jnp.einsum('qhe,khe->hqk', query_heads, key_heads, precision=highest) + position_bias)
    scores = jnp.where(allowed[None], scores, -jnp.inf)
    probability = low(jax.nn.softmax(scores, axis=-1))
    attended = jnp.einsum('hqk,khe->qhe', probability, value_heads, precision=highest)
    return low_back(low(attended.reshape(length, HEADS * HEAD)))

def layer(layer_input, encoder_rows, dec_ids, enc_ids, weights):
    norm_gain, w_query, w_kv, w_out, bias_table, c_query, c_kv, c_out, w_in, w_ffn = weights
    length = layer_input.shape[0]
    positions = jnp.arange(length)
    self_allowed = (dec_ids[:, None] == dec_ids[None, :]) & (positions[None, :] <= positions[:, None])
    cross_allowed = dec_ids[:, None] == enc_ids[None, :]
    distance = np.maximum(np.arange(length)[:, None] - np.arange(length)[None, :], 0)
    position_bias = jnp.transpose(bias_table[bucket_row(length)[distance]], (2, 0, 1))
    stream = low_back(layer_input)
    norm_one = low(normalize(stream, norm_gain[0]))
    queries = low_back(low(jnp.dot(norm_one, w_query, precision=highest)))
    key_value = low_back(low(jnp.einsum('ld,dcj->clj', norm_one, w_kv, precision=highest)))
    attended = attend(queries, key_value[0], key_value[1], position_bias, self_allowed)
    stream = stream + low_back(jnp.dot(attended, w_out, precision=highest))
    norm_two = low(normalize(stream, norm_gain[1]))
    cross_queries = low_back(low(jnp.dot(norm_two, c_query, precision=highest)))
    cross_pair = low_back(low(jnp.einsum('kd,dcj->ckj', encoder_rows, c_kv, precision=highest)))
    cross_attended = attend(cross_queries, cross_pair[0], cross_pair[1], 0.0, cross_allowed)
    stream = stream + low_back(jnp.dot(cross_attended, c_out, precision=highest))
    norm_three = low(normalize(stream, norm_gain[2]))
    gate_up = low_back(jnp.einsum('ld,dcf->clf', norm_three, w_in, precision=highest))
    hidden = low(jax.nn.gelu(gate_up[0], approximate=True) * gate_up[1])
    return stream + low_back(jnp.dot(hidden, w_ffn, precision=highest))

def reference(layer_in, cotangent, encoder, dec_segments, enc_segments, norm_gains, self_query, self_kv, self_out, rel_bias, cross_query, cross_kv, cross_out, ffn_in, ffn_out):
    row_count = MB * ROWS
    inputs = layer_in.astype(jnp.float32).reshape(row_count, TOK_MB, D)
    states = encoder.astype(jnp.float32).reshape(row_count, ENC_MB, D)
    zeroes = jnp.zeros_like(inputs)
    dec_ids = dec_segments.reshape(row_count, TOK_MB)
    enc_ids = enc_segments.reshape(row_count, ENC_MB)
    params = tuple((member.astype(jnp.float32) for member in (norm_gains, self_query, self_kv, self_out, rel_bias, cross_query, cross_kv, cross_out, ffn_in, ffn_out)))

    def forward(inputs, states, zeroes, params):
        first_layer = tuple((member[0] for member in params))
        second_layer = tuple((member[1] for member in params))

        def one_row(row_data):
            row_input, row_states, row_zero, row_dec, row_enc = row_data
            middle = low(layer(row_input, row_states, row_dec, row_enc, first_layer))
            final_out = low(layer(middle + row_zero, row_states, row_dec, row_enc, second_layer))
            return (middle, final_out)
        return lax.map(jax.checkpoint(one_row), (inputs, states, zeroes, dec_ids, enc_ids))
    (middle, final_out), pull = jax.vjp(forward, inputs, states, zeroes, params)
    grad_inputs, grad_states, grad_zero, grad_params = pull((jnp.zeros_like(middle), cotangent.astype(jnp.float32).reshape(row_count, TOK_MB, D)))
    shape_out = (2, MB, ROWS, TOK_MB, D)
    layer_out = jnp.stack([middle, final_out]).reshape(shape_out).astype(jnp.bfloat16)
    layer_grad = jnp.stack([grad_inputs, grad_zero]).reshape(shape_out).astype(jnp.bfloat16)
    encoder_grad = grad_states.reshape(MB, ROWS, ENC_MB, D)
    return (layer_out, layer_grad, encoder_grad, grad_params[0], grad_params[1], grad_params[2], grad_params[3], grad_params[4], grad_params[5], grad_params[6], grad_params[7], grad_params[8], grad_params[9])
```

```python
import jax
import jax.numpy as jnp
import numpy as np
from jax import lax
from jax.sharding import PartitionSpec as P

HEADS = 12
HEAD = 64
BUCKETS = 32
MAX_DIST = 128
PARTS = 16
EXTRA = 128


epsilon = 1e-06
highest = lax.Precision.HIGHEST


def bucket_row(length):
    distance = np.arange(length)
    half_count = BUCKETS // 2
    scaled = (
        np.log(np.maximum(distance, half_count) / half_count)
        / np.log(MAX_DIST / half_count)
        * (BUCKETS - half_count)
    )
    far_bucket = np.minimum(half_count + np.floor(scaled).astype(np.int32), BUCKETS - 1)
    return np.where(distance < half_count, distance, far_bucket).astype(np.int32)


def bucket_onehot(length):
    return (bucket_row(length)[None, :] == np.arange(BUCKETS)[:, None]).astype(np.float32)


def spread_distance(by_distance):
    head_count, length = by_distance.shape
    padded_row = jnp.concatenate(
        [jnp.zeros((head_count, length - 1), jnp.float32), by_distance], axis=1
    )
    tiled = jnp.tile(padded_row, (1, length))
    tiled = jnp.concatenate([tiled, jnp.zeros((head_count, length), jnp.float32)], axis=1)
    return tiled.reshape(head_count, length, 2 * length)[:, :, :length][:, :, ::-1]


def gather_distance(grid):
    head_count, length, _ = grid.shape
    flipped = jnp.concatenate(
        [grid[:, :, ::-1], jnp.zeros((head_count, length, length), jnp.float32)], axis=2
    )
    flat = flipped.reshape(head_count, 2 * length * length)[:, : length * (2 * length - 1)]
    return jnp.sum(flat.reshape(head_count, length, 2 * length - 1), axis=1)[:, length - 1 :]


def normalize(value, gain):
    return value * lax.rsqrt(jnp.mean(value * value, axis=-1, keepdims=True) + epsilon) * gain


def geglu(gate_rows, up_rows):
    return jax.nn.gelu(gate_rows, approximate=True) * up_rows


def split_heads(matrix):
    return matrix.reshape(matrix.shape[0], HEADS, HEAD)


def attend_forward(queries, key_rows, value_rows, position_bias, allowed):
    scores = (
        jnp.einsum(
            "qhe,khe->hqk",
            split_heads(queries),
            split_heads(key_rows),
            preferred_element_type=jnp.float32,
        )
        + position_bias
    )
    scores = jnp.where(allowed[None], scores, -jnp.inf)
    shifted = jnp.exp(scores - jnp.max(scores, axis=-1, keepdims=True))
    probability = shifted / jnp.sum(shifted, axis=-1, keepdims=True)
    attended = jnp.einsum(
        "hqk,khe->qhe",
        probability.astype(jnp.bfloat16),
        split_heads(value_rows),
        preferred_element_type=jnp.float32,
    )
    return (attended.reshape(queries.shape[0], HEADS * HEAD).astype(jnp.bfloat16), probability)


def attend_backward(grad_attended, queries, key_rows, value_rows, probability, allowed):
    width = HEADS * HEAD
    grad_heads = split_heads(grad_attended)
    grad_prob = jnp.einsum(
        "qhe,khe->hqk", grad_heads, split_heads(value_rows), preferred_element_type=jnp.float32
    )
    grad_values = jnp.einsum(
        "hqk,qhe->khe",
        probability.astype(jnp.bfloat16),
        grad_heads,
        preferred_element_type=jnp.float32,
    )
    grad_scores = probability * (
        grad_prob - jnp.sum(probability * grad_prob, axis=-1, keepdims=True)
    )
    grad_scores = jnp.where(allowed[None], grad_scores, 0.0).astype(jnp.bfloat16)
    grad_queries = jnp.einsum(
        "hqk,khe->qhe", grad_scores, split_heads(key_rows), preferred_element_type=jnp.float32
    )
    grad_keys = jnp.einsum(
        "hqk,qhe->khe", grad_scores, split_heads(queries), preferred_element_type=jnp.float32
    )
    return (
        grad_queries.reshape(-1, width).astype(jnp.bfloat16),
        grad_keys.reshape(-1, width).astype(jnp.bfloat16),
        grad_values.reshape(-1, width).astype(jnp.bfloat16),
        grad_scores,
    )


def layer_forward(layer_input, encoder_rows, dec_ids, enc_ids, weights):
    norm_gain, w_query, w_kv, w_out, bias_table, c_query, c_kv, c_out, w_in, w_ffn = weights
    length = layer_input.shape[0]
    positions = jnp.arange(length)
    self_allowed = (dec_ids[:, None] == dec_ids[None, :]) & (
        positions[None, :] <= positions[:, None]
    )
    cross_allowed = dec_ids[:, None] == enc_ids[None, :]
    by_distance = jnp.dot(
        bias_table.astype(jnp.float32).T, bucket_onehot(length), precision=highest
    )
    position_bias = spread_distance(by_distance)
    gain_wide = norm_gain.astype(jnp.float32)
    norm_one = normalize(layer_input, gain_wide[0]).astype(jnp.bfloat16)
    queries = jnp.dot(norm_one, w_query, preferred_element_type=jnp.float32).astype(jnp.bfloat16)
    key_value = jnp.einsum(
        "ld,dcj->clj", norm_one, w_kv, preferred_element_type=jnp.float32
    ).astype(jnp.bfloat16)
    attended, probability = attend_forward(
        queries, key_value[0], key_value[1], position_bias, self_allowed
    )
    after_self = layer_input + jnp.dot(attended, w_out, preferred_element_type=jnp.float32)
    norm_two = normalize(after_self, gain_wide[1]).astype(jnp.bfloat16)
    cross_queries = jnp.dot(norm_two, c_query, preferred_element_type=jnp.float32).astype(
        jnp.bfloat16
    )
    cross_pair = jnp.einsum(
        "kd,dcj->ckj", encoder_rows, c_kv, preferred_element_type=jnp.float32
    ).astype(jnp.bfloat16)
    cross_attended, cross_prob = attend_forward(
        cross_queries, cross_pair[0], cross_pair[1], 0.0, cross_allowed
    )
    after_cross = after_self + jnp.dot(cross_attended, c_out, preferred_element_type=jnp.float32)
    norm_three = normalize(after_cross, gain_wide[2]).astype(jnp.bfloat16)
    gate_up = jnp.einsum("ld,dcf->clf", norm_three, w_in, preferred_element_type=jnp.float32)
    hidden = geglu(gate_up[0], gate_up[1]).astype(jnp.bfloat16)
    result = after_cross + jnp.dot(hidden, w_ffn, preferred_element_type=jnp.float32)
    saved = (
        layer_input,
        encoder_rows,
        self_allowed,
        cross_allowed,
        norm_one,
        queries,
        key_value,
        probability,
        attended,
        after_self,
        norm_two,
        cross_queries,
        cross_pair,
        cross_prob,
        cross_attended,
        after_cross,
        norm_three,
        gate_up,
        hidden,
    )
    return (result, saved)


def layer_backward(grad_out, saved, weights):
    norm_gain, w_query, w_kv, w_out, bias_table, c_query, c_kv, c_out, w_in, w_ffn = weights
    (
        layer_input,
        encoder_rows,
        self_allowed,
        cross_allowed,
        norm_one,
        queries,
        key_value,
        probability,
        attended,
        after_self,
        norm_two,
        cross_queries,
        cross_pair,
        cross_prob,
        cross_attended,
        after_cross,
        norm_three,
        gate_up,
        hidden,
    ) = saved
    gain_wide = norm_gain.astype(jnp.float32)
    grad_ffn = grad_out.astype(jnp.bfloat16)
    grad_hidden = jnp.einsum("ld,fd->lf", grad_ffn, w_ffn, preferred_element_type=jnp.float32)
    _, pull_gate = jax.vjp(geglu, gate_up[0], gate_up[1])
    grad_gate, grad_up = pull_gate(grad_hidden)
    grad_gate_up = jnp.stack([grad_gate, grad_up]).astype(jnp.bfloat16)
    grad_norm = jnp.einsum("clf,dcf->ld", grad_gate_up, w_in, preferred_element_type=jnp.float32)
    _, pull_norm = jax.vjp(normalize, after_cross, gain_wide[2])
    grad_back, grad_gain_three = pull_norm(grad_norm)
    grad_stream = grad_out + grad_back
    grad_cross_branch = grad_stream.astype(jnp.bfloat16)
    grad_cross_att = jnp.einsum(
        "ld,jd->lj", grad_cross_branch, c_out, preferred_element_type=jnp.float32
    ).astype(jnp.bfloat16)
    grad_cross_q, grad_cross_k, grad_cross_v, _ = attend_backward(
        grad_cross_att, cross_queries, cross_pair[0], cross_pair[1], cross_prob, cross_allowed
    )
    grad_cross_pair = jnp.stack([grad_cross_k, grad_cross_v])
    grad_encoder = jnp.einsum(
        "ckj,dcj->kd", grad_cross_pair, c_kv, preferred_element_type=jnp.float32
    )
    grad_norm = jnp.einsum("lj,dj->ld", grad_cross_q, c_query, preferred_element_type=jnp.float32)
    _, pull_norm = jax.vjp(normalize, after_self, gain_wide[1])
    grad_back, grad_gain_two = pull_norm(grad_norm)
    grad_stream = grad_stream + grad_back
    grad_self_branch = grad_stream.astype(jnp.bfloat16)
    grad_self_att = jnp.einsum(
        "ld,jd->lj", grad_self_branch, w_out, preferred_element_type=jnp.float32
    ).astype(jnp.bfloat16)
    grad_queries, grad_keys, grad_values, grad_scores = attend_backward(
        grad_self_att, queries, key_value[0], key_value[1], probability, self_allowed
    )
    grad_pair = jnp.stack([grad_keys, grad_values])
    grad_norm = jnp.einsum(
        "lj,dj->ld", grad_queries, w_query, preferred_element_type=jnp.float32
    ) + jnp.einsum("clj,dcj->ld", grad_pair, w_kv, preferred_element_type=jnp.float32)
    _, pull_norm = jax.vjp(normalize, layer_input, gain_wide[0])
    grad_back, grad_gain_one = pull_norm(grad_norm)
    grad_input = grad_stream + grad_back
    length = layer_input.shape[0]
    diagonal_sums = gather_distance(grad_scores.astype(jnp.float32))
    grad_table = jnp.dot(bucket_onehot(length), diagonal_sums.T, precision=highest)
    grad_gains = jnp.stack([grad_gain_one, grad_gain_two, grad_gain_three])
    rows_for_weights = (
        norm_one,
        grad_queries,
        grad_pair,
        attended,
        grad_self_branch,
        norm_two,
        grad_cross_q,
        encoder_rows,
        grad_cross_pair,
        cross_attended,
        grad_cross_branch,
        norm_three,
        grad_gate_up,
        hidden,
        grad_ffn,
        grad_gains,
        grad_table,
    )
    return (grad_input, grad_encoder, rows_for_weights)


def weight_grads(records):

    def joined(slot_index, along):
        return jnp.concatenate([record[slot_index] for record in records], axis=along)

    norm_one = joined(0, 0)
    grad_query = jnp.einsum("ld,lj->dj", norm_one, joined(1, 0), preferred_element_type=jnp.float32)
    grad_kv = jnp.einsum("ld,clj->dcj", norm_one, joined(2, 1), preferred_element_type=jnp.float32)
    grad_out = jnp.einsum(
        "lj,ld->jd", joined(3, 0), joined(4, 0), preferred_element_type=jnp.float32
    )
    grad_c_query = jnp.einsum(
        "ld,lj->dj", joined(5, 0), joined(6, 0), preferred_element_type=jnp.float32
    )
    grad_c_kv = jnp.einsum(
        "kd,ckj->dcj", joined(7, 0), joined(8, 1), preferred_element_type=jnp.float32
    )
    grad_c_out = jnp.einsum(
        "lj,ld->jd", joined(9, 0), joined(10, 0), preferred_element_type=jnp.float32
    )
    grad_in = jnp.einsum(
        "ld,clf->dcf", joined(11, 0), joined(12, 1), preferred_element_type=jnp.float32
    )
    grad_ffn = jnp.einsum(
        "lf,ld->fd", joined(13, 0), joined(14, 0), preferred_element_type=jnp.float32
    )
    grad_gains = jnp.sum(jnp.stack([record[15] for record in records]), axis=0)
    grad_table = jnp.sum(jnp.stack([record[16] for record in records]), axis=0)
    return (
        grad_gains,
        grad_query,
        grad_kv,
        grad_out,
        grad_table,
        grad_c_query,
        grad_c_kv,
        grad_c_out,
        grad_in,
        grad_ffn,
    )


def pack(gains, query, kv, out, table, c_query, c_kv, c_out, w_in, w_ffn):
    rows = query.shape[0]
    extra = jnp.zeros((rows, EXTRA), query.dtype)
    extra = extra.at[:, :3].set(gains.T)
    extra = extra.at[: BUCKETS // PARTS, 16 : 16 + HEADS].set(table)
    return jnp.concatenate(
        [
            query,
            kv.reshape(rows, -1),
            out,
            c_query,
            c_kv.reshape(rows, -1),
            c_out,
            w_in.reshape(rows, -1),
            w_ffn.reshape(rows, -1),
            extra,
        ],
        axis=1,
    )


def unpack(block, parts):
    rows = block.shape[0]
    start = 0
    pieces = []
    for width in (768, 1536, 768, 768, 1536, 768, 4096, 2048, EXTRA):
        pieces.append(block[:, start : start + width])
        start += width
    query, kv, out, c_query, c_kv, c_out, w_in, w_ffn, extra = pieces
    gains = extra[:, :3].T
    table = extra.reshape(parts, rows // parts, EXTRA)[:, : BUCKETS // PARTS, 16 : 16 + HEADS]
    return (
        gains,
        query,
        kv.reshape(rows, 2, 768),
        out,
        table.reshape(-1, HEADS),
        c_query,
        c_kv.reshape(rows, 2, 768),
        c_out,
        w_in.reshape(rows, 2, 2048),
        w_ffn.reshape(-1, 768),
    )


def pack_full(gains, query, kv, out, table, c_query, c_kv, c_out, w_in, w_ffn):
    rows = query.shape[0]
    extra = jnp.zeros((PARTS, rows // PARTS, EXTRA), jnp.bfloat16)
    extra = extra.at[:, :, :3].set(gains.T.reshape(PARTS, rows // PARTS, 3).astype(jnp.bfloat16))
    extra = extra.at[:, : BUCKETS // PARTS, 16 : 16 + HEADS].set(
        table.reshape(PARTS, BUCKETS // PARTS, HEADS).astype(jnp.bfloat16)
    )
    members = [
        query,
        kv.reshape(rows, -1),
        out,
        c_query,
        c_kv.reshape(rows, -1),
        c_out,
        w_in.reshape(rows, -1),
        w_ffn.reshape(rows, -1),
        extra.reshape(rows, EXTRA),
    ]
    return jnp.concatenate([member.astype(jnp.bfloat16) for member in members], axis=1)


def shards(
    layer_in,
    cotangent,
    encoder,
    dec_segments,
    enc_segments,
    norm_gains,
    self_query,
    self_kv,
    self_out,
    rel_bias,
    cross_query,
    cross_kv,
    cross_out,
    ffn_in,
    ffn_out,
):
    section_index = lax.axis_index("section")
    batches = layer_in.shape[0]
    own = pack(
        norm_gains[0],
        self_query[0],
        self_kv[0],
        self_out[0],
        rel_bias[0],
        cross_query[0],
        cross_kv[0],
        cross_out[0],
        ffn_in[0],
        ffn_out[0],
    )
    weights = unpack(lax.all_gather(own, "fsdp", axis=0, tiled=True), PARTS)
    rows_in = layer_in[:, 0]
    states = encoder[:, 0]
    dec_ids = dec_segments[:, 0]
    enc_ids = enc_segments[:, 0]
    forward = jax.vmap(layer_forward, in_axes=(0, 0, 0, 0, None))
    backward = jax.vmap(layer_backward, in_axes=(0, 0, None))
    first, _ = forward(rows_in.astype(jnp.float32), states, dec_ids, enc_ids, weights)
    received = lax.ppermute(first.astype(jnp.bfloat16), "section", [(0, 1)])
    current = jnp.where(section_index == 0, rows_in, received)
    result, saved = forward(current.astype(jnp.float32), states, dec_ids, enc_ids, weights)
    outputs = result.astype(jnp.bfloat16)
    given = cotangent[:, 0]
    grad_first, _, _ = backward(given.astype(jnp.float32), saved, weights)
    returned = lax.ppermute(grad_first.astype(jnp.bfloat16), "section", [(1, 0)])
    incoming = jnp.where(section_index == 1, given, returned)
    grad_input, grad_encoder, records = backward(incoming.astype(jnp.float32), saved, weights)
    input_grads = grad_input.astype(jnp.bfloat16)
    encoder_total = lax.psum(grad_encoder.astype(jnp.bfloat16), "section").astype(jnp.float32)
    full_grads = weight_grads(
        [jax.tree.map(lambda member: member[slot], records) for slot in range(batches)]
    )
    owned = lax.psum_scatter(pack_full(*full_grads), "fsdp", scatter_dimension=0, tiled=True)
    summed = lax.psum(owned, "rep").astype(jnp.float32)
    grads = unpack(summed, 1)
    return (
        outputs[None, :, None],
        input_grads[None, :, None],
        encoder_total[:, None],
    ) + tuple(member[None] for member in grads)


def solution(mesh):
    return jax.shard_map(
        shards,
        mesh=mesh,
        in_specs=(
            P(None, ("fsdp", "rep"), None, None),
            P(None, ("fsdp", "rep"), None, None),
            P(None, ("fsdp", "rep"), None, None),
            P(None, ("fsdp", "rep"), None),
            P(None, ("fsdp", "rep"), None),
            P("section", None, "fsdp"),
            P("section", "fsdp", None),
            P("section", "fsdp", None, None),
            P("section", "fsdp", None),
            P("section", "fsdp", None),
            P("section", "fsdp", None),
            P("section", "fsdp", None, None),
            P("section", "fsdp", None),
            P("section", "fsdp", None, None),
            P("section", "fsdp", None),
        ),
        out_specs=(
            P("section", None, ("fsdp", "rep"), None, None),
            P("section", None, ("fsdp", "rep"), None, None),
            P(None, ("fsdp", "rep"), None, None),
            P("section", None, "fsdp"),
            P("section", "fsdp", None),
            P("section", "fsdp", None, None),
            P("section", "fsdp", None),
            P("section", "fsdp", None),
            P("section", "fsdp", None),
            P("section", "fsdp", None, None),
            P("section", "fsdp", None),
            P("section", "fsdp", None, None),
            P("section", "fsdp", None),
        ),
        check_vma=False,
    )
```

```python
import jax
import jax.numpy as jnp
import numpy as np
from jax import lax
from jax.experimental import pallas as pl
from jax.experimental.pallas import tpu as pltpu
from jax.sharding import PartitionSpec as P

HEADS = 12
HEAD = 64
BUCKETS = 32
MAX_DIST = 128
PARTS = 16
GELU_SCALE = float(np.sqrt(2.0 / np.pi))


epsilon = 1e-06
highest = lax.Precision.HIGHEST


def bucket_row(length):
    distance = np.arange(length)
    half_count = BUCKETS // 2
    scaled = (
        np.log(np.maximum(distance, half_count) / half_count)
        / np.log(MAX_DIST / half_count)
        * (BUCKETS - half_count)
    )
    far_bucket = np.minimum(half_count + np.floor(scaled).astype(np.int32), BUCKETS - 1)
    return np.where(distance < half_count, distance, far_bucket).astype(np.int32)


def bucket_onehot(length):
    return (bucket_row(length)[None, :] == np.arange(BUCKETS)[:, None]).astype(np.float32)


def spread_distance(by_distance):
    head_count, length = by_distance.shape
    padded_row = jnp.concatenate(
        [jnp.zeros((head_count, length - 1), jnp.float32), by_distance], axis=1
    )
    tiled = jnp.tile(padded_row, (1, length))
    tiled = jnp.concatenate([tiled, jnp.zeros((head_count, length), jnp.float32)], axis=1)
    return tiled.reshape(head_count, length, 2 * length)[:, :, :length][:, :, ::-1]


def gather_distance(grid):
    head_count, length, _ = grid.shape
    flipped = jnp.concatenate(
        [grid[:, :, ::-1], jnp.zeros((head_count, length, length), jnp.float32)], axis=2
    )
    flat = flipped.reshape(head_count, 2 * length * length)[:, : length * (2 * length - 1)]
    return jnp.sum(flat.reshape(head_count, length, 2 * length - 1), axis=1)[:, length - 1 :]


ROWS_OWN = 48
TOKENS = 64
WIDE = 768
FF = 2048
GROUP = 256
GROUPS = 3
BATCHES = 2
STATES = 256
CHUNK = 512
ATT = 6144
VMEM_BYTES = 60 * 1024 * 1024
FULL = (PARTS, ROWS_OWN, WIDE)
GATED = (PARTS, ROWS_OWN, FF)
DOWN = (PARTS, FF // PARTS, WIDE)
DOWN_PIECES = [(piece, block) for piece in range(GROUPS) for block in range(8)]


def product(left, right, along_left=1, along_right=0):
    return lax.dot_general(
        left,
        right,
        (((along_left,), (along_right,)), ((), ())),
        preferred_element_type=jnp.float32,
    )


def low(value):
    return value.astype(jnp.bfloat16)


def same_head():
    row = lax.broadcasted_iota(jnp.int32, (GROUP, GROUP), 0) // HEAD
    lane = lax.broadcasted_iota(jnp.int32, (GROUP, GROUP), 1) // HEAD
    return jnp.where(row == lane, 1.0, 0.0)


def spread_heads(block, own_low):
    return jnp.concatenate([block] * 4, axis=0) * own_low


def fold_heads(block, own):
    kept = block * own
    return kept[:64] + kept[64:128] + kept[128:192] + kept[192:]


def scale_of(value):
    return lax.rsqrt(jnp.mean(value * value, axis=-1, keepdims=True) + epsilon)


def norm_back(grad, value, gain):
    scale = scale_of(value)
    carried = grad * gain
    mean = jnp.mean(value * carried, axis=-1, keepdims=True)
    grad_value = carried * scale - value * (scale * scale * scale) * mean
    grad_gain = jnp.sum(grad * value * scale, axis=0, keepdims=True)
    return grad_value, grad_gain


def square(ref):
    return ref[...].reshape(WIDE, WIDE)


def down_at(ref, base, piece, block):
    return ref.at[:, pl.ds(16 * piece, 16), pl.ds(base + GROUP * block, GROUP)]


def rows_at(ref, piece, block):
    return ref.at[:, pl.ds(16 * block, 16), pl.ds(GROUP * piece, GROUP)]


def softmax_rows(scores):
    raised = jnp.exp(scores - jnp.max(scores, axis=-1, keepdims=True))
    return raised / jnp.sum(raised, axis=-1, keepdims=True)


def gelu_parts(gate):
    cube = gate * gate * gate
    bent = jnp.tanh(GELU_SCALE * (gate + 0.044715 * cube))
    half = 0.5 * (1.0 + bent)
    slope = half + 0.5 * gate * (1.0 - bent * bent) * GELU_SCALE * (
        1.0 + 3.0 * 0.044715 * gate * gate
    )
    return gate * half, slope


def weight_copies(weight, slots, sems):
    copies = {}
    for place, (name, column) in enumerate(
        (("q", 0), ("k", 1), ("v", 2), ("o", 3), ("cq", 4), ("ck", 5), ("cv", 6), ("co", 7))
    ):
        if name in slots:
            source = weight.at[:, :, pl.ds(WIDE * column, WIDE)]
            copies[name] = [pltpu.make_async_copy(source, slots[name], sems.at[place])]
    for place, (name, column) in enumerate((("gate", ATT), ("up", ATT + FF))):
        if name in slots:
            source = weight.at[:, :, pl.ds(column, FF)]
            copies[name] = [pltpu.make_async_copy(source, slots[name], sems.at[8 + place])]
    if "down" in slots:
        copies["down"] = [
            pltpu.make_async_copy(
                down_at(weight, ATT + 2 * FF, piece, block),
                rows_at(slots["down"], piece, block),
                sems.at[10 + place],
            )
            for place, (piece, block) in enumerate(DOWN_PIECES)
        ]
    return copies


def begin(copies, names):
    for name in names:
        for copy in copies[name]:
            copy.start()


def finish(copies, name):
    for copy in copies[name]:
        copy.wait()


def forward_kernel(
    x_ref,
    enc_ref,
    self_add_ref,
    cross_add_ref,
    gains_ref,
    weight,
    out_ref,
    n1_ref,
    q_ref,
    k_ref,
    v_ref,
    p_ref,
    o_ref,
    a2_ref,
    n2_ref,
    cq_ref,
    ck_ref,
    cv_ref,
    cp_ref,
    co_ref,
    a3_ref,
    n3_ref,
    gate_ref,
    up_ref,
    hid_ref,
    wq,
    wk,
    wv,
    wo,
    wcq,
    wck,
    wcv,
    wco,
    wg,
    wu,
    wd,
    sems,
):
    slots = dict(q=wq, k=wk, v=wv, o=wo, cq=wcq, ck=wck, cv=wcv, co=wco, gate=wg, up=wu, down=wd)
    copies = weight_copies(weight, slots, sems)
    begin(copies, ("ck", "cv", "q", "k", "v", "o", "cq", "co", "gate", "up", "down"))
    own = same_head()
    own_low = low(own)
    stream = x_ref[...].astype(jnp.float32)
    normed = low(stream * scale_of(stream) * gains_ref[0:1])
    n1_ref[...] = normed
    finish(copies, "ck")
    for row in range(BATCHES):
        part = pl.ds(STATES * row, STATES)
        ck_ref[part] = low(product(enc_ref[part], square(wck)))
    finish(copies, "cv")
    for row in range(BATCHES):
        part = pl.ds(STATES * row, STATES)
        cv_ref[part] = low(product(enc_ref[part], square(wcv)))
    finish(copies, "q")
    q_ref[...] = low(product(normed, square(wq)))
    finish(copies, "k")
    k_ref[...] = low(product(normed, square(wk)))
    finish(copies, "v")
    v_ref[...] = low(product(normed, square(wv)))
    for row in range(BATCHES):
        part = pl.ds(TOKENS * row, TOKENS)
        for group in range(GROUPS):
            lanes = pl.ds(GROUP * group, GROUP)
            spread = spread_heads(q_ref[part, lanes], own_low)
            scores = product(spread, k_ref[part, lanes], 1, 1) + self_add_ref[row, lanes]
            chance = softmax_rows(scores)
            p_ref[row, lanes] = chance
            mixed = product(low(chance), v_ref[part, lanes])
            o_ref[part, lanes] = low(fold_heads(mixed, own))
    finish(copies, "o")
    stream = stream + product(o_ref[...], square(wo))
    a2_ref[...] = stream
    normed = low(stream * scale_of(stream) * gains_ref[1:2])
    n2_ref[...] = normed
    finish(copies, "cq")
    cq_ref[...] = low(product(normed, square(wcq)))
    for row in range(BATCHES):
        part = pl.ds(TOKENS * row, TOKENS)
        keys = pl.ds(STATES * row, STATES)
        add = jnp.concatenate([cross_add_ref[row]] * 4, axis=0)
        for group in range(GROUPS):
            lanes = pl.ds(GROUP * group, GROUP)
            spread = spread_heads(cq_ref[part, lanes], own_low)
            scores = product(spread, ck_ref[keys, lanes], 1, 1) + add
            chance = softmax_rows(scores)
            cp_ref[row, lanes] = chance
            mixed = product(low(chance), cv_ref[keys, lanes])
            co_ref[part, lanes] = low(fold_heads(mixed, own))
    finish(copies, "co")
    stream = a2_ref[...] + product(co_ref[...], square(wco))
    a3_ref[...] = stream
    n3_ref[...] = low(stream * scale_of(stream) * gains_ref[2:3])
    finish(copies, "gate")
    finish(copies, "up")
    finish(copies, "down")

    def step(index, total):
        lanes = pl.ds(pl.multiple_of(index * CHUNK, CHUNK), CHUNK)
        rows = n3_ref[...]
        gate = product(rows, wg[:, :, lanes].reshape(WIDE, CHUNK))
        up = product(rows, wu[:, :, lanes].reshape(WIDE, CHUNK))
        gate_ref[:, lanes] = gate
        up_ref[:, lanes] = up
        bent = 0.5 * (1.0 + jnp.tanh(GELU_SCALE * (gate + 0.044715 * (gate * gate * gate))))
        hidden = low(gate * bent * up)
        hid_ref[:, lanes] = hidden
        return total + product(hidden, wd[pl.ds(4 * index, 4)].reshape(CHUNK, WIDE))

    total = lax.fori_loop(0, FF // CHUNK, step, jnp.zeros((BATCHES * TOKENS, WIDE), jnp.float32))
    out_ref[...] = low(a3_ref[...] + total)


def backward_kernel(
    c_ref,
    x_ref,
    gains_ref,
    q_ref,
    k_ref,
    v_ref,
    p_ref,
    a2_ref,
    cq_ref,
    ck_ref,
    cv_ref,
    cp_ref,
    a3_ref,
    gate_ref,
    up_ref,
    weight,
    da_ref,
    dgate_ref,
    dup_ref,
    dc_ref,
    dcq_ref,
    dck_ref,
    dcv_ref,
    dself_ref,
    dq_ref,
    dk_ref,
    dv_ref,
    dgain_ref,
    dscore_ref,
    wq,
    wk,
    wv,
    wo,
    wcq,
    wco,
    wg,
    wu,
    wd,
    sems,
):
    slots = dict(q=wq, k=wk, v=wv, o=wo, cq=wcq, co=wco, gate=wg, up=wu, down=wd)
    copies = weight_copies(weight, slots, sems)
    begin(copies, ("down", "gate", "up", "co", "cq", "o", "q", "k", "v"))
    own = same_head()
    own_low = low(own)
    finish(copies, "down")
    finish(copies, "gate")
    finish(copies, "up")

    def step(index, total):
        lanes = pl.ds(pl.multiple_of(index * CHUNK, CHUNK), CHUNK)
        grad = product(c_ref[...], wd[pl.ds(4 * index, 4)].reshape(CHUNK, WIDE), 1, 1)
        bent, slope = gelu_parts(gate_ref[:, lanes])
        dgate = low(grad * up_ref[:, lanes] * slope)
        dup = low(grad * bent)
        dgate_ref[:, lanes] = dgate
        dup_ref[:, lanes] = dup
        total = total + product(dgate, wg[:, :, lanes].reshape(WIDE, CHUNK), 1, 1)
        return total + product(dup, wu[:, :, lanes].reshape(WIDE, CHUNK), 1, 1)

    grad = lax.fori_loop(0, FF // CHUNK, step, jnp.zeros((BATCHES * TOKENS, WIDE), jnp.float32))
    back, dgain = norm_back(grad, a3_ref[...], gains_ref[2:3])
    dgain_ref[2:3] = dgain
    stream = c_ref[...].astype(jnp.float32) + back
    dc_ref[...] = low(stream)
    finish(copies, "co")
    datt = low(product(dc_ref[...], square(wco), 1, 1))
    for row in range(BATCHES):
        part = pl.ds(TOKENS * row, TOKENS)
        keys = pl.ds(STATES * row, STATES)
        for group in range(GROUPS):
            lanes = pl.ds(GROUP * group, GROUP)
            left = GROUP * group
            dout = spread_heads(
                datt[TOKENS * row : TOKENS * (row + 1), left : left + GROUP], own_low
            )
            spread = spread_heads(cq_ref[part, lanes], own_low)
            chance = cp_ref[row, lanes]
            dchance = product(dout, cv_ref[keys, lanes], 1, 1)
            dcv_ref[keys, lanes] = low(product(low(chance), dout, 0, 0))
            inner = jnp.sum(chance * dchance, axis=-1, keepdims=True)
            dscore = low(chance * (dchance - inner))
            dcq_ref[part, lanes] = low(fold_heads(product(dscore, ck_ref[keys, lanes]), own))
            dck_ref[keys, lanes] = low(product(dscore, spread, 0, 0))
    finish(copies, "cq")
    grad = product(dcq_ref[...], square(wcq), 1, 1)
    back, dgain = norm_back(grad, a2_ref[...], gains_ref[1:2])
    dgain_ref[1:2] = dgain
    stream = stream + back
    dself_ref[...] = low(stream)
    finish(copies, "o")
    datt = low(product(dself_ref[...], square(wo), 1, 1))
    for row in range(BATCHES):
        part = pl.ds(TOKENS * row, TOKENS)
        for group in range(GROUPS):
            lanes = pl.ds(GROUP * group, GROUP)
            left = GROUP * group
            dout = spread_heads(
                datt[TOKENS * row : TOKENS * (row + 1), left : left + GROUP], own_low
            )
            spread = spread_heads(q_ref[part, lanes], own_low)
            chance = p_ref[row, lanes]
            dchance = product(dout, v_ref[part, lanes], 1, 1)
            dv_ref[part, lanes] = low(product(low(chance), dout, 0, 0))
            inner = jnp.sum(chance * dchance, axis=-1, keepdims=True)
            dscore = low(chance * (dchance - inner))
            if row == 0:
                dscore_ref[lanes] = dscore.astype(jnp.float32)
            else:
                dscore_ref[lanes] += dscore.astype(jnp.float32)
            dq_ref[part, lanes] = low(fold_heads(product(dscore, k_ref[part, lanes]), own))
            dk_ref[part, lanes] = low(product(dscore, spread, 0, 0))
    finish(copies, "q")
    grad = product(dq_ref[...], square(wq), 1, 1)
    finish(copies, "k")
    grad = grad + product(dk_ref[...], square(wk), 1, 1)
    finish(copies, "v")
    grad = grad + product(dv_ref[...], square(wv), 1, 1)
    back, dgain = norm_back(grad, x_ref[...].astype(jnp.float32), gains_ref[0:1])
    dgain_ref[0:1] = dgain
    da_ref[...] = low(stream + back)


def weight_kernel(
    c_ref,
    enc_ref,
    n1_ref,
    o_ref,
    n2_ref,
    co_ref,
    n3_ref,
    hid_ref,
    dgate_ref,
    dup_ref,
    dc_ref,
    dcq_ref,
    dck_ref,
    dcv_ref,
    dself_ref,
    dq_ref,
    dk_ref,
    dv_ref,
    weight,
    grads,
    denc_ref,
    wck,
    wcv,
    gq,
    gk,
    gv,
    go,
    gcq,
    gck,
    gcv,
    gco,
    gg,
    gu,
    gd,
    sems,
    out_sems,
):
    copies = weight_copies(weight, dict(ck=wck, cv=wcv), sems)
    begin(copies, ("ck", "cv"))
    slots = dict(q=gq, k=gk, v=gv, o=go, cq=gcq, ck=gck, cv=gcv, co=gco, gate=gg, up=gu, down=gd)
    outward = {
        name: [pltpu.make_async_copy(slots[name], grads.at[:, :, pl.ds(WIDE * place, WIDE)], out_sems.at[place])]
        for place, name in enumerate(("q", "k", "v", "o", "cq", "ck", "cv", "co"))
    }
    for place, name in enumerate(("gate", "up")):
        target = grads.at[:, :, pl.ds(ATT + FF * place, FF)]
        outward[name] = [pltpu.make_async_copy(slots[name], target, out_sems.at[8 + place])]
    outward["down"] = [
        pltpu.make_async_copy(
            rows_at(gd, piece, block),
            down_at(grads, ATT + 2 * FF, piece, block),
            out_sems.at[10 + place],
        )
        for place, (piece, block) in enumerate(DOWN_PIECES)
    ]

    def down_step(index, carry):
        lanes = pl.ds(pl.multiple_of(index * CHUNK, CHUNK), CHUNK)
        grad = low(product(hid_ref[:, lanes], c_ref[...], 0, 0))
        gd[pl.ds(4 * index, 4)] = grad.reshape(4, FF // PARTS, WIDE)
        return carry

    lax.fori_loop(0, FF // CHUNK, down_step, 0)
    begin(outward, ("down",))

    def up_step(index, carry):
        lanes = pl.ds(pl.multiple_of(index * CHUNK, CHUNK), CHUNK)
        rows = n3_ref[...]
        shape = (PARTS, ROWS_OWN, CHUNK)
        gg[:, :, lanes] = low(product(rows, dgate_ref[:, lanes], 0, 0)).reshape(shape)
        gu[:, :, lanes] = low(product(rows, dup_ref[:, lanes], 0, 0)).reshape(shape)
        return carry

    lax.fori_loop(0, FF // CHUNK, up_step, 0)
    begin(outward, ("gate", "up"))
    for name, left, right in (
        ("co", co_ref, dc_ref),
        ("cq", n2_ref, dcq_ref),
        ("ck", enc_ref, dck_ref),
        ("cv", enc_ref, dcv_ref),
        ("o", o_ref, dself_ref),
        ("q", n1_ref, dq_ref),
        ("k", n1_ref, dk_ref),
        ("v", n1_ref, dv_ref),
    ):
        slots[name][...] = low(product(left[...], right[...], 0, 0)).reshape(FULL)
        begin(outward, (name,))
    finish(copies, "ck")
    finish(copies, "cv")
    for row in range(BATCHES):
        keys = pl.ds(STATES * row, STATES)
        denc_ref[keys] = low(
            product(dck_ref[keys], square(wck), 1, 1) + product(dcv_ref[keys], square(wcv), 1, 1)
        )
    for name in ("down", "gate", "up", "co", "cq", "ck", "cv", "o", "q", "k", "v"):
        finish(outward, name)


def in_vmem(count):
    return [pl.BlockSpec(memory_space=pltpu.VMEM)] * count


def held(*shapes):
    return [pltpu.VMEM(shape, jnp.bfloat16) for shape in shapes]


def shape_of(dims, kind=jnp.bfloat16):
    return jax.ShapeDtypeStruct(dims, kind)


ALL_TOKENS = (BATCHES * TOKENS, WIDE)
ALL_STATES = (BATCHES * STATES, WIDE)
HIDDEN = (BATCHES * TOKENS, FF)
params = pltpu.CompilerParams(vmem_limit_bytes=VMEM_BYTES)


def run_forward(x, enc, self_add, cross_add, gains, weight):
    wide = jnp.float32
    outs = [
        shape_of(ALL_TOKENS),
        shape_of(ALL_TOKENS),
        shape_of(ALL_TOKENS),
        shape_of(ALL_TOKENS),
        shape_of(ALL_TOKENS),
        shape_of((BATCHES, WIDE, TOKENS), wide),
        shape_of(ALL_TOKENS),
        shape_of(ALL_TOKENS, wide),
        shape_of(ALL_TOKENS),
        shape_of(ALL_TOKENS),
        shape_of(ALL_STATES),
        shape_of(ALL_STATES),
        shape_of((BATCHES, WIDE, STATES), wide),
        shape_of(ALL_TOKENS),
        shape_of(ALL_TOKENS, wide),
        shape_of(ALL_TOKENS),
        shape_of(HIDDEN, wide),
        shape_of(HIDDEN, wide),
        shape_of(HIDDEN),
    ]
    return pl.pallas_call(
        forward_kernel,
        out_shape=outs,
        in_specs=in_vmem(5) + [pl.BlockSpec(memory_space=pl.ANY)],
        out_specs=in_vmem(len(outs)),
        scratch_shapes=held(*[FULL] * 8, GATED, GATED, DOWN) + [pltpu.SemaphoreType.DMA((34,))],
        compiler_params=params,
        name="layer_forward",
    )(x, enc, self_add, cross_add, gains, weight)


def run_backward(cotangent, x, gains, saved, weight):
    (n1, q, k, v, p, o, a2, n2, cq, ck, cv, cp, co, a3, n3, gate, up, hid) = saved
    outs = [
        shape_of(ALL_TOKENS),
        shape_of(HIDDEN),
        shape_of(HIDDEN),
        shape_of(ALL_TOKENS),
        shape_of(ALL_TOKENS),
        shape_of(ALL_STATES),
        shape_of(ALL_STATES),
        shape_of(ALL_TOKENS),
        shape_of(ALL_TOKENS),
        shape_of(ALL_TOKENS),
        shape_of(ALL_TOKENS),
        shape_of((3, WIDE), jnp.float32),
        shape_of((WIDE, TOKENS), jnp.float32),
    ]
    return pl.pallas_call(
        backward_kernel,
        out_shape=outs,
        in_specs=in_vmem(15) + [pl.BlockSpec(memory_space=pl.ANY)],
        out_specs=in_vmem(len(outs)),
        scratch_shapes=held(*[FULL] * 6, GATED, GATED, DOWN) + [pltpu.SemaphoreType.DMA((34,))],
        compiler_params=params,
        name="layer_backward",
    )(cotangent, x, gains, q, k, v, p, a2, cq, ck, cv, cp, a3, gate, up, weight)


def run_weights(cotangent, enc, saved, records, weight):
    (n1, q, k, v, p, o, a2, n2, cq, ck, cv, cp, co, a3, n3, gate, up, hid) = saved
    (dgate, dup, dc, dcq, dck, dcv, dself, dq, dk, dv) = records
    return pl.pallas_call(
        weight_kernel,
        out_shape=[shape_of((PARTS, ROWS_OWN, 2 * ATT)), shape_of(ALL_STATES)],
        in_specs=in_vmem(18) + [pl.BlockSpec(memory_space=pl.ANY)],
        out_specs=[pl.BlockSpec(memory_space=pl.ANY)] + in_vmem(1),
        scratch_shapes=held(FULL, FULL, *[FULL] * 8, GATED, GATED, DOWN)
        + [pltpu.SemaphoreType.DMA((34,)), pltpu.SemaphoreType.DMA((34,))],
        compiler_params=params,
        name="weight_gradients",
    )(
        cotangent, enc, n1, o, n2, co, n3, hid, dgate, dup, dc, dcq, dck, dcv, dself, dq, dk, dv, weight
    )


def pack(query, kv, out, c_query, c_kv, c_out, w_in, w_ffn):
    rows = query.shape[0]
    pieces = w_ffn.reshape(8, 16, GROUPS, GROUP).transpose(2, 1, 0, 3)
    return jnp.concatenate(
        [
            query,
            kv.reshape(rows, -1),
            out,
            c_query,
            c_kv.reshape(rows, -1),
            c_out,
            w_in.reshape(rows, -1),
            pieces.reshape(rows, FF),
        ],
        axis=1,
    )


def unpack(block):
    rows = block.shape[0]
    start = 0
    pieces = []
    for width in (768, 1536, 768, 768, 1536, 768, 4096, 2048):
        pieces.append(block[:, start : start + width])
        start += width
    query, kv, out, c_query, c_kv, c_out, w_in, w_ffn = pieces
    return (
        query,
        kv.reshape(rows, 2, WIDE),
        out,
        c_query,
        c_kv.reshape(rows, 2, WIDE),
        c_out,
        w_in.reshape(rows, 2, FF),
        w_ffn.reshape(GROUPS, 16, 8, GROUP).transpose(2, 1, 0, 3).reshape(FF // PARTS, WIDE),
    )


def score_terms(table, dec_ids, enc_ids):
    positions = jnp.arange(TOKENS)
    by_distance = jnp.dot(table.astype(jnp.float32).T, bucket_onehot(TOKENS), precision=highest)
    bias = spread_distance(by_distance)
    allowed = (dec_ids[:, :, None] == dec_ids[:, None, :]) & (
        positions[None, :] <= positions[:, None]
    )
    self_add = jnp.where(allowed[:, None], bias[None], -jnp.inf)
    cross_add = jnp.where(dec_ids[:, :, None] == enc_ids[:, None, :], 0.0, -jnp.inf)
    return self_add.reshape(BATCHES, WIDE, TOKENS), cross_add


def shards(
    layer_in,
    cotangent,
    encoder,
    dec_segments,
    enc_segments,
    norm_gains,
    self_query,
    self_kv,
    self_out,
    rel_bias,
    cross_query,
    cross_kv,
    cross_out,
    ffn_in,
    ffn_out,
):
    section_index = lax.axis_index("section")
    part_index = lax.axis_index("fsdp")
    own = pack(
        self_query[0],
        self_kv[0],
        self_out[0],
        cross_query[0],
        cross_kv[0],
        cross_out[0],
        ffn_in[0],
        ffn_out[0],
    )
    weight = lax.all_gather(own, "fsdp", axis=0, tiled=True).reshape(PARTS, ROWS_OWN, 2 * ATT)
    small = jnp.zeros((8, 128), jnp.bfloat16)
    small = small.at[:3, :ROWS_OWN].set(norm_gains[0])
    small = small.at[3:5, :HEADS].set(rel_bias[0])
    small = lax.all_gather(small, "fsdp", axis=0, tiled=False)
    gains = small[:, :3, :ROWS_OWN].transpose(1, 0, 2).reshape(3, WIDE).astype(jnp.float32)
    table = small[:, 3:5, :HEADS].reshape(BUCKETS, HEADS)
    self_add, cross_add = score_terms(table, dec_segments[:, 0], enc_segments[:, 0])
    rows_in = layer_in[:, 0].reshape(ALL_TOKENS)
    given = cotangent[:, 0].reshape(ALL_TOKENS)
    enc = encoder[:, 0].reshape(ALL_STATES)
    first = run_forward(rows_in, enc, self_add, cross_add, gains, weight)[0]
    received = lax.ppermute(first, "section", [(0, 1)])
    current = jnp.where(section_index == 0, rows_in, received)
    result, *saved = run_forward(current, enc, self_add, cross_add, gains, weight)
    grad_first = run_backward(given, current, gains, saved, weight)[0]
    returned = lax.ppermute(grad_first, "section", [(1, 0)])
    incoming = jnp.where(section_index == 1, given, returned)
    grad_input, *records, grad_gains, grad_scores = run_backward(
        incoming, current, gains, saved, weight
    )
    grads, grad_enc = run_weights(incoming, enc, saved, records, weight)
    owned = lax.psum_scatter(
        grads.reshape(WIDE, 2 * ATT), "fsdp", scatter_dimension=0, tiled=True
    )
    other_enc = lax.ppermute(grad_enc, "section", [(0, 1), (1, 0)])
    encoder_total = grad_enc.astype(jnp.float32) + other_enc.astype(jnp.float32)
    diagonal_sums = gather_distance(grad_scores.reshape(HEADS, TOKENS, TOKENS))
    grad_table = jnp.dot(bucket_onehot(TOKENS), diagonal_sums.T, precision=highest)
    little = jnp.zeros((8, WIDE), jnp.float32)
    little = little.at[:3].set(grad_gains)
    little = little.at[3, : BUCKETS * HEADS].set(grad_table.reshape(-1))
    little = lax.psum(little, ("fsdp", "rep"))
    own_gains = lax.dynamic_slice(little, (0, part_index * ROWS_OWN), (3, ROWS_OWN))
    own_table = lax.dynamic_slice(little, (3, part_index * 2 * HEADS), (1, 2 * HEADS))
    quarters = owned.reshape(ROWS_OWN, 4, 2 * ATT // 4)
    quarters = lax.all_to_all(quarters, "rep", split_axis=1, concat_axis=1, tiled=True)
    quarter = low(jnp.sum(quarters.astype(jnp.float32), axis=1))
    summed = lax.all_gather(quarter, "rep", axis=1, tiled=True).astype(jnp.float32)
    query, kv, out, c_query, c_kv, c_out, w_in, w_ffn = unpack(summed)
    ordered = (
        own_gains,
        query,
        kv,
        out,
        own_table.reshape(2, HEADS),
        c_query,
        c_kv,
        c_out,
        w_in,
        w_ffn,
    )
    return (
        result.reshape(1, BATCHES, 1, TOKENS, WIDE),
        grad_input.reshape(1, BATCHES, 1, TOKENS, WIDE),
        encoder_total.reshape(BATCHES, 1, STATES, WIDE),
    ) + tuple(member[None] for member in ordered)


def solution(mesh):
    return jax.shard_map(
        shards,
        mesh=mesh,
        in_specs=(
            P(None, ("fsdp", "rep"), None, None),
            P(None, ("fsdp", "rep"), None, None),
            P(None, ("fsdp", "rep"), None, None),
            P(None, ("fsdp", "rep"), None),
            P(None, ("fsdp", "rep"), None),
            P("section", None, "fsdp"),
            P("section", "fsdp", None),
            P("section", "fsdp", None, None),
            P("section", "fsdp", None),
            P("section", "fsdp", None),
            P("section", "fsdp", None),
            P("section", "fsdp", None, None),
            P("section", "fsdp", None),
            P("section", "fsdp", None, None),
            P("section", "fsdp", None),
        ),
        out_specs=(
            P("section", None, ("fsdp", "rep"), None, None),
            P("section", None, ("fsdp", "rep"), None, None),
            P(None, ("fsdp", "rep"), None, None),
            P("section", None, "fsdp"),
            P("section", "fsdp", None),
            P("section", "fsdp", None, None),
            P("section", "fsdp", None),
            P("section", "fsdp", None),
            P("section", "fsdp", None),
            P("section", "fsdp", None, None),
            P("section", "fsdp", None),
            P("section", "fsdp", None, None),
            P("section", "fsdp", None),
        ),
        check_vma=False,
    )
```

```python
import jax
import jax.numpy as jnp
import numpy as np
from jax import lax
from jax.experimental import pallas as pl
from jax.experimental.pallas import tpu as pltpu
from jax.sharding import PartitionSpec as P

HEADS = 12
HEAD = 64
BUCKETS = 32
MAX_DIST = 128
PARTS = 16
GELU_SCALE = float(np.sqrt(2.0 / np.pi))


epsilon = 1e-06
highest = lax.Precision.HIGHEST


def bucket_row(length):
    distance = np.arange(length)
    half_count = BUCKETS // 2
    scaled = (
        np.log(np.maximum(distance, half_count) / half_count)
        / np.log(MAX_DIST / half_count)
        * (BUCKETS - half_count)
    )
    far_bucket = np.minimum(half_count + np.floor(scaled).astype(np.int32), BUCKETS - 1)
    return np.where(distance < half_count, distance, far_bucket).astype(np.int32)


def bucket_onehot(length):
    return (bucket_row(length)[None, :] == np.arange(BUCKETS)[:, None]).astype(np.float32)


def spread_distance(by_distance):
    head_count, length = by_distance.shape
    padded_row = jnp.concatenate(
        [jnp.zeros((head_count, length - 1), jnp.float32), by_distance], axis=1
    )
    tiled = jnp.tile(padded_row, (1, length))
    tiled = jnp.concatenate([tiled, jnp.zeros((head_count, length), jnp.float32)], axis=1)
    return tiled.reshape(head_count, length, 2 * length)[:, :, :length][:, :, ::-1]


def gather_distance(grid):
    head_count, length, _ = grid.shape
    flipped = jnp.concatenate(
        [grid[:, :, ::-1], jnp.zeros((head_count, length, length), jnp.float32)], axis=2
    )
    flat = flipped.reshape(head_count, 2 * length * length)[:, : length * (2 * length - 1)]
    return jnp.sum(flat.reshape(head_count, length, 2 * length - 1), axis=1)[:, length - 1 :]


ROWS_OWN = 48
TOKENS = 64
WIDE = 768
FF = 2048
GROUP = 256
GROUPS = 3
BATCHES = 2
STATES = 256
CHUNK = 512
ATT = 6144
VMEM_BYTES = 60 * 1024 * 1024
FULL = (PARTS, ROWS_OWN, WIDE)
GATED = (PARTS, ROWS_OWN, FF)
DOWN = (PARTS, FF // PARTS, WIDE)
DOWN_PIECES = [(piece, block) for piece in range(GROUPS) for block in range(8)]


def product(left, right, along_left=1, along_right=0):
    return lax.dot_general(
        left,
        right,
        (((along_left,), (along_right,)), ((), ())),
        preferred_element_type=jnp.float32,
    )


def low(value):
    return value.astype(jnp.bfloat16)


def same_head():
    row = lax.broadcasted_iota(jnp.int32, (GROUP, GROUP), 0) // HEAD
    lane = lax.broadcasted_iota(jnp.int32, (GROUP, GROUP), 1) // HEAD
    return jnp.where(row == lane, 1.0, 0.0)


def spread_heads(block, own_low):
    return jnp.concatenate([block] * 4, axis=0) * own_low


def fold_heads(block, own):
    kept = block * own
    return kept[:64] + kept[64:128] + kept[128:192] + kept[192:]


def scale_of(value):
    return lax.rsqrt(jnp.mean(value * value, axis=-1, keepdims=True) + epsilon)


def norm_back(grad, value, gain):
    scale = scale_of(value)
    carried = grad * gain
    mean = jnp.mean(value * carried, axis=-1, keepdims=True)
    grad_value = carried * scale - value * (scale * scale * scale) * mean
    grad_gain = jnp.sum(grad * value * scale, axis=0, keepdims=True)
    return grad_value, grad_gain


def square(ref):
    return ref[...].reshape(WIDE, WIDE)


def down_at(ref, piece, block):
    return ref.at[:, 1, pl.ds(16 * piece, 16), pl.ds(2 * FF + GROUP * block, GROUP)]


def rows_at(ref, piece, block):
    return ref.at[:, pl.ds(16 * block, 16), pl.ds(GROUP * piece, GROUP)]


def softmax_rows(scores):
    raised = jnp.exp(scores - jnp.max(scores, axis=-1, keepdims=True))
    return raised / jnp.sum(raised, axis=-1, keepdims=True)


def gelu_parts(gate):
    cube = gate * gate * gate
    bent = jnp.tanh(GELU_SCALE * (gate + 0.044715 * cube))
    half = 0.5 * (1.0 + bent)
    slope = half + 0.5 * gate * (1.0 - bent * bent) * GELU_SCALE * (
        1.0 + 3.0 * 0.044715 * gate * gate
    )
    return gate * half, slope


def weight_copies(weight, slots, sems):
    copies = {}
    for place, (name, column) in enumerate(
        (("q", 0), ("k", 1), ("v", 2), ("o", 3), ("cq", 4), ("ck", 5), ("cv", 6), ("co", 7))
    ):
        if name in slots:
            source = weight.at[:, 0, :, pl.ds(WIDE * column, WIDE)]
            copies[name] = [pltpu.make_async_copy(source, slots[name], sems.at[place])]
    for place, (name, column) in enumerate((("gate", 0), ("up", FF))):
        if name in slots:
            source = weight.at[:, 1, :, pl.ds(column, FF)]
            copies[name] = [pltpu.make_async_copy(source, slots[name], sems.at[8 + place])]
    if "down" in slots:
        copies["down"] = [
            pltpu.make_async_copy(
                down_at(weight, piece, block),
                rows_at(slots["down"], piece, block),
                sems.at[10 + place],
            )
            for place, (piece, block) in enumerate(DOWN_PIECES)
        ]
    return copies


def begin(copies, names):
    for name in names:
        for copy in copies[name]:
            copy.start()


def finish(copies, name):
    for copy in copies[name]:
        copy.wait()


def forward_body(
    keys_given,
    x_ref,
    enc_ref,
    self_add_ref,
    cross_add_ref,
    gains_ref,
    weight,
    out_ref,
    n1_ref,
    q_ref,
    k_ref,
    v_ref,
    p_ref,
    o_ref,
    a2_ref,
    n2_ref,
    cq_ref,
    ck_ref,
    cv_ref,
    cp_ref,
    co_ref,
    a3_ref,
    n3_ref,
    gate_ref,
    up_ref,
    hid_ref,
    wq,
    wk,
    wv,
    wo,
    wcq,
    wck,
    wcv,
    wco,
    wg,
    wu,
    wd,
    sems,
):
    slots = dict(q=wq, k=wk, v=wv, o=wo, cq=wcq, co=wco, gate=wg, up=wu, down=wd)
    if not keys_given:
        slots.update(ck=wck, cv=wcv)
    copies = weight_copies(weight, slots, sems)
    if not keys_given:
        begin(copies, ("ck", "cv"))
    begin(copies, ("q", "k", "v", "o", "cq", "co", "gate", "up", "down"))
    own = same_head()
    own_low = low(own)
    stream = x_ref[...].astype(jnp.float32)
    normed = low(stream * scale_of(stream) * gains_ref[0:1])
    n1_ref[...] = normed
    if not keys_given:
        for name, held_weight, target in (("ck", wck, ck_ref), ("cv", wcv, cv_ref)):
            finish(copies, name)
            for row in range(BATCHES):
                part = pl.ds(STATES * row, STATES)
                target[part] = low(product(enc_ref[part], square(held_weight)))
    finish(copies, "q")
    q_ref[...] = low(product(normed, square(wq)))
    finish(copies, "k")
    k_ref[...] = low(product(normed, square(wk)))
    finish(copies, "v")
    v_ref[...] = low(product(normed, square(wv)))
    for row in range(BATCHES):
        part = pl.ds(TOKENS * row, TOKENS)
        for group in range(GROUPS):
            lanes = pl.ds(GROUP * group, GROUP)
            spread = spread_heads(q_ref[part, lanes], own_low)
            scores = product(spread, k_ref[part, lanes], 1, 1) + self_add_ref[row, lanes]
            chance = softmax_rows(scores)
            p_ref[row, lanes] = chance
            mixed = product(low(chance), v_ref[part, lanes])
            o_ref[part, lanes] = low(fold_heads(mixed, own))
    finish(copies, "o")
    stream = stream + product(o_ref[...], square(wo))
    a2_ref[...] = stream
    normed = low(stream * scale_of(stream) * gains_ref[1:2])
    n2_ref[...] = normed
    finish(copies, "cq")
    cq_ref[...] = low(product(normed, square(wcq)))
    for row in range(BATCHES):
        part = pl.ds(TOKENS * row, TOKENS)
        keys = pl.ds(STATES * row, STATES)
        add = jnp.concatenate([cross_add_ref[row]] * 4, axis=0)
        for group in range(GROUPS):
            lanes = pl.ds(GROUP * group, GROUP)
            spread = spread_heads(cq_ref[part, lanes], own_low)
            scores = product(spread, ck_ref[keys, lanes], 1, 1) + add
            chance = softmax_rows(scores)
            cp_ref[row, lanes] = chance
            mixed = product(low(chance), cv_ref[keys, lanes])
            co_ref[part, lanes] = low(fold_heads(mixed, own))
    finish(copies, "co")
    stream = a2_ref[...] + product(co_ref[...], square(wco))
    a3_ref[...] = stream
    n3_ref[...] = low(stream * scale_of(stream) * gains_ref[2:3])
    finish(copies, "gate")
    finish(copies, "up")
    finish(copies, "down")

    def step(index, total):
        lanes = pl.ds(pl.multiple_of(index * CHUNK, CHUNK), CHUNK)
        rows = n3_ref[...]
        gate = product(rows, wg[:, :, lanes].reshape(WIDE, CHUNK))
        up = product(rows, wu[:, :, lanes].reshape(WIDE, CHUNK))
        gate_ref[:, lanes] = gate
        up_ref[:, lanes] = up
        bent = 0.5 * (1.0 + jnp.tanh(GELU_SCALE * (gate + 0.044715 * (gate * gate * gate))))
        hidden = low(gate * bent * up)
        hid_ref[:, lanes] = hidden
        return total + product(hidden, wd[pl.ds(4 * index, 4)].reshape(CHUNK, WIDE))

    total = lax.fori_loop(0, FF // CHUNK, step, jnp.zeros((BATCHES * TOKENS, WIDE), jnp.float32))
    out_ref[...] = low(a3_ref[...] + total)


def first_kernel(
    x_ref, enc_ref, self_add_ref, cross_add_ref, gains_ref, weight, out_ref, ck_ref, cv_ref, *rest
):
    (n1, q, k, v, p, o, a2, n2, cq, cp, co, a3, n3, gate, up, hid, *scratch) = rest
    forward_body(
        False,
        x_ref, enc_ref, self_add_ref, cross_add_ref, gains_ref, weight, out_ref,
        n1, q, k, v, p, o, a2, n2, cq, ck_ref, cv_ref, cp, co, a3, n3, gate, up, hid, *scratch,
    )


def second_kernel(
    x_ref, ck_ref, cv_ref, self_add_ref, cross_add_ref, gains_ref, weight, out_ref, *rest
):
    (n1, q, k, v, p, o, a2, n2, cq, cp, co, a3, n3, gate, up, hid, *scratch) = rest
    (wq, wk, wv, wo, wcq, wco, wg, wu, wd, sems) = scratch
    forward_body(
        True,
        x_ref, None, self_add_ref, cross_add_ref, gains_ref, weight, out_ref,
        n1, q, k, v, p, o, a2, n2, cq, ck_ref, cv_ref, cp, co, a3, n3, gate, up, hid,
        wq, wk, wv, wo, wcq, None, None, wco, wg, wu, wd, sems,
    )


def backward_kernel(
    c_ref,
    x_ref,
    gains_ref,
    q_ref,
    k_ref,
    v_ref,
    p_ref,
    a2_ref,
    cq_ref,
    ck_ref,
    cv_ref,
    cp_ref,
    a3_ref,
    gate_ref,
    up_ref,
    weight,
    da_ref,
    dgate_ref,
    dup_ref,
    dc_ref,
    dcq_ref,
    dck_ref,
    dcv_ref,
    dself_ref,
    dq_ref,
    dk_ref,
    dv_ref,
    dgain_ref,
    dscore_ref,
    wq,
    wk,
    wv,
    wo,
    wcq,
    wco,
    wg,
    wu,
    wd,
    sems,
):
    slots = dict(q=wq, k=wk, v=wv, o=wo, cq=wcq, co=wco, gate=wg, up=wu, down=wd)
    copies = weight_copies(weight, slots, sems)
    begin(copies, ("down", "gate", "up", "co", "cq", "o", "q", "k", "v"))
    own = same_head()
    own_low = low(own)
    finish(copies, "down")
    finish(copies, "gate")
    finish(copies, "up")

    def step(index, total):
        lanes = pl.ds(pl.multiple_of(index * CHUNK, CHUNK), CHUNK)
        grad = product(c_ref[...], wd[pl.ds(4 * index, 4)].reshape(CHUNK, WIDE), 1, 1)
        bent, slope = gelu_parts(gate_ref[:, lanes])
        dgate = low(grad * up_ref[:, lanes] * slope)
        dup = low(grad * bent)
        dgate_ref[:, lanes] = dgate
        dup_ref[:, lanes] = dup
        total = total + product(dgate, wg[:, :, lanes].reshape(WIDE, CHUNK), 1, 1)
        return total + product(dup, wu[:, :, lanes].reshape(WIDE, CHUNK), 1, 1)

    grad = lax.fori_loop(0, FF // CHUNK, step, jnp.zeros((BATCHES * TOKENS, WIDE), jnp.float32))
    back, dgain = norm_back(grad, a3_ref[...], gains_ref[2:3])
    dgain_ref[2:3] = dgain
    stream = c_ref[...].astype(jnp.float32) + back
    dc_ref[...] = low(stream)
    finish(copies, "co")
    datt = low(product(dc_ref[...], square(wco), 1, 1))
    for row in range(BATCHES):
        part = pl.ds(TOKENS * row, TOKENS)
        keys = pl.ds(STATES * row, STATES)
        for group in range(GROUPS):
            lanes = pl.ds(GROUP * group, GROUP)
            left = GROUP * group
            dout = spread_heads(
                datt[TOKENS * row : TOKENS * (row + 1), left : left + GROUP], own_low
            )
            spread = spread_heads(cq_ref[part, lanes], own_low)
            chance = cp_ref[row, lanes]
            dchance = product(dout, cv_ref[keys, lanes], 1, 1)
            dcv_ref[keys, lanes] = low(product(low(chance), dout, 0, 0))
            inner = jnp.sum(chance * dchance, axis=-1, keepdims=True)
            dscore = low(chance * (dchance - inner))
            dcq_ref[part, lanes] = low(fold_heads(product(dscore, ck_ref[keys, lanes]), own))
            dck_ref[keys, lanes] = low(product(dscore, spread, 0, 0))
    finish(copies, "cq")
    grad = product(dcq_ref[...], square(wcq), 1, 1)
    back, dgain = norm_back(grad, a2_ref[...], gains_ref[1:2])
    dgain_ref[1:2] = dgain
    stream = stream + back
    dself_ref[...] = low(stream)
    finish(copies, "o")
    datt = low(product(dself_ref[...], square(wo), 1, 1))
    for row in range(BATCHES):
        part = pl.ds(TOKENS * row, TOKENS)
        for group in range(GROUPS):
            lanes = pl.ds(GROUP * group, GROUP)
            left = GROUP * group
            dout = spread_heads(
                datt[TOKENS * row : TOKENS * (row + 1), left : left + GROUP], own_low
            )
            spread = spread_heads(q_ref[part, lanes], own_low)
            chance = p_ref[row, lanes]
            dchance = product(dout, v_ref[part, lanes], 1, 1)
            dv_ref[part, lanes] = low(product(low(chance), dout, 0, 0))
            inner = jnp.sum(chance * dchance, axis=-1, keepdims=True)
            dscore = low(chance * (dchance - inner))
            if row == 0:
                dscore_ref[lanes] = dscore.astype(jnp.float32)
            else:
                dscore_ref[lanes] += dscore.astype(jnp.float32)
            dq_ref[part, lanes] = low(fold_heads(product(dscore, k_ref[part, lanes]), own))
            dk_ref[part, lanes] = low(product(dscore, spread, 0, 0))
    finish(copies, "q")
    grad = product(dq_ref[...], square(wq), 1, 1)
    finish(copies, "k")
    grad = grad + product(dk_ref[...], square(wk), 1, 1)
    finish(copies, "v")
    grad = grad + product(dv_ref[...], square(wv), 1, 1)
    back, dgain = norm_back(grad, x_ref[...].astype(jnp.float32), gains_ref[0:1])
    dgain_ref[0:1] = dgain
    da_ref[...] = low(stream + back)


def weight_kernel(
    c_ref,
    enc_ref,
    n1_ref,
    o_ref,
    n2_ref,
    co_ref,
    n3_ref,
    hid_ref,
    dgate_ref,
    dup_ref,
    dc_ref,
    dcq_ref,
    dck_ref,
    dcv_ref,
    dself_ref,
    dq_ref,
    dk_ref,
    dv_ref,
    weight,
    grads,
    denc_ref,
    wck,
    wcv,
    gq,
    gk,
    gv,
    go,
    gcq,
    gck,
    gcv,
    gco,
    gg,
    gu,
    gd,
    sems,
    out_sems,
):
    copies = weight_copies(weight, dict(ck=wck, cv=wcv), sems)
    begin(copies, ("ck", "cv"))
    slots = dict(q=gq, k=gk, v=gv, o=go, cq=gcq, ck=gck, cv=gcv, co=gco, gate=gg, up=gu, down=gd)
    outward = {
        name: [
            pltpu.make_async_copy(
                slots[name], grads.at[:, 0, :, pl.ds(WIDE * place, WIDE)], out_sems.at[place]
            )
        ]
        for place, name in enumerate(("q", "k", "v", "o", "cq", "ck", "cv", "co"))
    }
    for place, name in enumerate(("gate", "up")):
        target = grads.at[:, 1, :, pl.ds(FF * place, FF)]
        outward[name] = [pltpu.make_async_copy(slots[name], target, out_sems.at[8 + place])]
    outward["down"] = [
        pltpu.make_async_copy(
            rows_at(gd, piece, block),
            down_at(grads, piece, block),
            out_sems.at[10 + place],
        )
        for place, (piece, block) in enumerate(DOWN_PIECES)
    ]

    def down_step(index, carry):
        lanes = pl.ds(pl.multiple_of(index * CHUNK, CHUNK), CHUNK)
        grad = low(product(hid_ref[:, lanes], c_ref[...], 0, 0))
        gd[pl.ds(4 * index, 4)] = grad.reshape(4, FF // PARTS, WIDE)
        return carry

    lax.fori_loop(0, FF // CHUNK, down_step, 0)
    begin(outward, ("down",))

    def up_step(index, carry):
        lanes = pl.ds(pl.multiple_of(index * CHUNK, CHUNK), CHUNK)
        rows = n3_ref[...]
        shape = (PARTS, ROWS_OWN, CHUNK)
        gg[:, :, lanes] = low(product(rows, dgate_ref[:, lanes], 0, 0)).reshape(shape)
        gu[:, :, lanes] = low(product(rows, dup_ref[:, lanes], 0, 0)).reshape(shape)
        return carry

    lax.fori_loop(0, FF // CHUNK, up_step, 0)
    begin(outward, ("gate", "up"))
    for name, left, right in (
        ("co", co_ref, dc_ref),
        ("cq", n2_ref, dcq_ref),
        ("ck", enc_ref, dck_ref),
        ("cv", enc_ref, dcv_ref),
        ("o", o_ref, dself_ref),
        ("q", n1_ref, dq_ref),
        ("k", n1_ref, dk_ref),
        ("v", n1_ref, dv_ref),
    ):
        slots[name][...] = low(product(left[...], right[...], 0, 0)).reshape(FULL)
        begin(outward, (name,))
    finish(copies, "ck")
    finish(copies, "cv")
    for row in range(BATCHES):
        keys = pl.ds(STATES * row, STATES)
        denc_ref[keys] = low(
            product(dck_ref[keys], square(wck), 1, 1) + product(dcv_ref[keys], square(wcv), 1, 1)
        )
    for name in ("down", "gate", "up", "co", "cq", "ck", "cv", "o", "q", "k", "v"):
        finish(outward, name)


def in_vmem(count):
    return [pl.BlockSpec(memory_space=pltpu.VMEM)] * count


def held(*shapes):
    return [pltpu.VMEM(shape, jnp.bfloat16) for shape in shapes]


def shape_of(dims, kind=jnp.bfloat16):
    return jax.ShapeDtypeStruct(dims, kind)


ALL_TOKENS = (BATCHES * TOKENS, WIDE)
ALL_STATES = (BATCHES * STATES, WIDE)
HIDDEN = (BATCHES * TOKENS, FF)
params = pltpu.CompilerParams(vmem_limit_bytes=VMEM_BYTES)


SAVED = (
    (ALL_TOKENS, jnp.bfloat16),
    (ALL_TOKENS, jnp.bfloat16),
    (ALL_TOKENS, jnp.bfloat16),
    (ALL_TOKENS, jnp.bfloat16),
    ((BATCHES, WIDE, TOKENS), jnp.float32),
    (ALL_TOKENS, jnp.bfloat16),
    (ALL_TOKENS, jnp.float32),
    (ALL_TOKENS, jnp.bfloat16),
    (ALL_TOKENS, jnp.bfloat16),
    ((BATCHES, WIDE, STATES), jnp.float32),
    (ALL_TOKENS, jnp.bfloat16),
    (ALL_TOKENS, jnp.float32),
    (ALL_TOKENS, jnp.bfloat16),
    (HIDDEN, jnp.float32),
    (HIDDEN, jnp.float32),
    (HIDDEN, jnp.bfloat16),
)


def run_first(x, enc, self_add, cross_add, gains, weight):
    outs = [shape_of(ALL_TOKENS), shape_of(ALL_STATES), shape_of(ALL_STATES)]
    return pl.pallas_call(
        first_kernel,
        out_shape=outs,
        in_specs=in_vmem(5) + [pl.BlockSpec(memory_space=pl.ANY)],
        out_specs=in_vmem(len(outs)),
        scratch_shapes=[pltpu.VMEM(dims, kind) for dims, kind in SAVED]
        + held(*[FULL] * 8, GATED, GATED, DOWN)
        + [pltpu.SemaphoreType.DMA((34,))],
        compiler_params=params,
        name="first_forward",
    )(x, enc, self_add, cross_add, gains, weight)


def run_second(x, ck, cv, self_add, cross_add, gains, weight):
    outs = [shape_of(ALL_TOKENS)] + [shape_of(dims, kind) for dims, kind in SAVED]
    return pl.pallas_call(
        second_kernel,
        out_shape=outs,
        in_specs=in_vmem(6) + [pl.BlockSpec(memory_space=pl.ANY)],
        out_specs=in_vmem(len(outs)),
        scratch_shapes=held(*[FULL] * 6, GATED, GATED, DOWN) + [pltpu.SemaphoreType.DMA((34,))],
        compiler_params=params,
        name="second_forward",
    )(x, ck, cv, self_add, cross_add, gains, weight)


def run_backward(cotangent, x, gains, saved, weight):
    (ck, cv, n1, q, k, v, p, o, a2, n2, cq, cp, co, a3, n3, gate, up, hid) = saved
    outs = [
        shape_of(ALL_TOKENS),
        shape_of(HIDDEN),
        shape_of(HIDDEN),
        shape_of(ALL_TOKENS),
        shape_of(ALL_TOKENS),
        shape_of(ALL_STATES),
        shape_of(ALL_STATES),
        shape_of(ALL_TOKENS),
        shape_of(ALL_TOKENS),
        shape_of(ALL_TOKENS),
        shape_of(ALL_TOKENS),
        shape_of((3, WIDE), jnp.float32),
        shape_of((WIDE, TOKENS), jnp.float32),
    ]
    return pl.pallas_call(
        backward_kernel,
        out_shape=outs,
        in_specs=in_vmem(15) + [pl.BlockSpec(memory_space=pl.ANY)],
        out_specs=in_vmem(len(outs)),
        scratch_shapes=held(*[FULL] * 6, GATED, GATED, DOWN) + [pltpu.SemaphoreType.DMA((34,))],
        compiler_params=params,
        name="layer_backward",
    )(cotangent, x, gains, q, k, v, p, a2, cq, ck, cv, cp, a3, gate, up, weight)


def run_weights(cotangent, enc, saved, records, weight):
    (ck, cv, n1, q, k, v, p, o, a2, n2, cq, cp, co, a3, n3, gate, up, hid) = saved
    (dgate, dup, dc, dcq, dck, dcv, dself, dq, dk, dv) = records
    return pl.pallas_call(
        weight_kernel,
        out_shape=[shape_of((PARTS, 2, ROWS_OWN, ATT)), shape_of(ALL_STATES)],
        in_specs=in_vmem(18) + [pl.BlockSpec(memory_space=pl.ANY)],
        out_specs=[pl.BlockSpec(memory_space=pl.ANY)] + in_vmem(1),
        scratch_shapes=held(FULL, FULL, *[FULL] * 8, GATED, GATED, DOWN)
        + [pltpu.SemaphoreType.DMA((34,)), pltpu.SemaphoreType.DMA((34,))],
        compiler_params=params,
        name="weight_gradients",
    )(
        cotangent, enc, n1, o, n2, co, n3, hid, dgate, dup, dc, dcq, dck, dcv, dself, dq, dk, dv, weight
    )


def pack_attention(query, kv, out, c_query, c_kv, c_out):
    rows = query.shape[0]
    return jnp.concatenate(
        [query, kv.reshape(rows, -1), out, c_query, c_kv.reshape(rows, -1), c_out], axis=1
    )


def pack_hidden(w_in, w_ffn):
    rows = w_in.shape[0]
    pieces = w_ffn.reshape(8, 16, GROUPS, GROUP).transpose(2, 1, 0, 3)
    return jnp.concatenate([w_in.reshape(rows, -1), pieces.reshape(rows, FF)], axis=1)


def unpack(attention, hidden):
    rows = attention.shape[0]
    start = 0
    pieces = []
    for width in (768, 1536, 768, 768, 1536, 768):
        pieces.append(attention[:, start : start + width])
        start += width
    query, kv, out, c_query, c_kv, c_out = pieces
    w_ffn = hidden[:, 2 * FF :].reshape(GROUPS, 16, 8, GROUP).transpose(2, 1, 0, 3)
    return (
        query,
        kv.reshape(rows, 2, WIDE),
        out,
        c_query,
        c_kv.reshape(rows, 2, WIDE),
        c_out,
        hidden[:, : 2 * FF].reshape(rows, 2, FF),
        w_ffn.reshape(FF // PARTS, WIDE),
    )


def score_terms(table, dec_ids, enc_ids):
    positions = jnp.arange(TOKENS)
    by_distance = jnp.dot(table.astype(jnp.float32).T, bucket_onehot(TOKENS), precision=highest)
    bias = spread_distance(by_distance)
    allowed = (dec_ids[:, :, None] == dec_ids[:, None, :]) & (
        positions[None, :] <= positions[:, None]
    )
    self_add = jnp.where(allowed[:, None], bias[None], -jnp.inf)
    cross_add = jnp.where(dec_ids[:, :, None] == enc_ids[:, None, :], 0.0, -jnp.inf)
    return self_add.reshape(BATCHES, WIDE, TOKENS), cross_add


def shards(
    layer_in,
    cotangent,
    encoder,
    dec_segments,
    enc_segments,
    norm_gains,
    self_query,
    self_kv,
    self_out,
    rel_bias,
    cross_query,
    cross_kv,
    cross_out,
    ffn_in,
    ffn_out,
):
    core = lax.axis_index("section")
    part_index = lax.axis_index("fsdp")
    plane = lax.axis_index("rep")
    planes = lax.axis_size("rep")
    layer = lax.rem(plane, 2)
    first_core = core == 0
    at_home = core == layer

    def place(core_index, plane_index):
        return core_index * planes + plane_index

    def flip_core(value):
        return lax.ppermute(value, "section", [(0, 1), (1, 0)])

    def from_home(value):
        pairs = [(place(p % 2, p), place(1 - p % 2, p)) for p in range(planes)]
        return jnp.where(at_home, value, lax.ppermute(value, ("section", "rep"), pairs))

    def beside(value):
        return lax.ppermute(value, "rep", [(p, p ^ 1) for p in range(planes)])

    def rows_for_layer(value):
        pairs = [(place(p % 2, p), place(p % 2, p ^ 1)) for p in range(planes)]
        return jnp.where(at_home, value, lax.ppermute(value, ("section", "rep"), pairs))

    def rows_back(value):
        pairs = [(place(1 - p % 2, p), place(p % 2, p ^ 1)) for p in range(planes)]
        return jnp.where(at_home, value, lax.ppermute(value, ("section", "rep"), pairs))

    def between_layers(value, steps):
        pairs = [(p, p + steps) for p in range(planes) if p % 2 == (steps < 0)]
        return lax.ppermute(value, "rep", pairs)

    attention = pack_attention(
        self_query[0], self_kv[0], self_out[0], cross_query[0], cross_kv[0], cross_out[0]
    )
    hidden = pack_hidden(ffn_in[0], ffn_out[0])
    kept = jnp.where(first_core, attention, hidden)
    given_away = jnp.where(first_core, hidden, attention)
    half = jnp.where(at_home, kept, flip_core(given_away))
    weight = lax.all_gather(half, ("fsdp", "section"), axis=0, tiled=True)
    weight = weight.reshape(PARTS, 2, ROWS_OWN, ATT)
    small = jnp.zeros((8, 128), jnp.bfloat16)
    small = small.at[:3, :ROWS_OWN].set(norm_gains[0])
    small = small.at[3:5, :HEADS].set(rel_bias[0])
    small = lax.all_gather(from_home(small), "fsdp", axis=0, tiled=False)
    gains = small[:, :3, :ROWS_OWN].transpose(1, 0, 2).reshape(3, WIDE).astype(jnp.float32)
    table = small[:, 3:5, :HEADS].reshape(BUCKETS, HEADS)
    ids = jnp.concatenate([dec_segments[:, 0], enc_segments[:, 0]], axis=1)
    ids = rows_for_layer(ids)
    self_add, cross_add = score_terms(table, ids[:, :TOKENS], ids[:, TOKENS:])
    ends = jnp.stack([layer_in[:, 0].reshape(ALL_TOKENS), cotangent[:, 0].reshape(ALL_TOKENS)])
    ends = rows_for_layer(ends)
    rows_in, given = ends[0], ends[1]
    enc = rows_for_layer(encoder[:, 0].reshape(ALL_STATES))
    weight, rows_in, given, enc, self_add, cross_add, gains = lax.optimization_barrier(
        (weight, rows_in, given, enc, self_add, cross_add, gains)
    )
    first, ck, cv = run_first(rows_in, enc, self_add, cross_add, gains, weight)
    current = jnp.where(layer == 0, rows_in, between_layers(first, 1))
    result, *saved = run_second(current, ck, cv, self_add, cross_add, gains, weight)
    saved = [ck, cv] + saved
    grad_first = run_backward(given, current, gains, saved, weight)[0]
    incoming = jnp.where(layer == 1, given, between_layers(grad_first, -1))
    grad_input, *records, grad_gains, grad_scores = run_backward(
        incoming, current, gains, saved, weight
    )
    grads, grad_enc = run_weights(incoming, enc, saved, records, weight)
    partial = lax.psum_scatter(
        grads.reshape(2 * WIDE, ATT), ("fsdp", "section"), scatter_dimension=0, tiled=True
    )
    outs = rows_back(jnp.stack([result, grad_input]))
    encoder_total = grad_enc.astype(jnp.float32) + beside(grad_enc).astype(jnp.float32)
    encoder_total = from_home(encoder_total)
    diagonal_sums = gather_distance(grad_scores.reshape(HEADS, TOKENS, TOKENS))
    grad_table = jnp.dot(bucket_onehot(TOKENS), diagonal_sums.T, precision=highest)
    little = jnp.zeros((8, WIDE), jnp.float32)
    little = little.at[:3].set(grad_gains)
    little = little.at[3, : BUCKETS * HEADS].set(grad_table.reshape(-1))
    for axis, bits in (("section", (1,)), ("fsdp", (1, 2, 4, 8)), ("rep", (2,))):
        for bit in bits:
            pairs = [(index, index ^ bit) for index in range(lax.axis_size(axis))]
            little = little + lax.ppermute(little, axis, pairs)
    little = jnp.where(at_home, little, beside(little))
    own_gains = lax.dynamic_slice(little, (0, part_index * ROWS_OWN), (3, ROWS_OWN))
    own_table = lax.dynamic_slice(little, (3, part_index * 2 * HEADS), (1, 2 * HEADS))
    partial, own_gains, own_table, encoder_total, outs = lax.optimization_barrier(
        (partial, own_gains, own_table, encoder_total, outs)
    )
    up = [(p, (p + 1) % planes) for p in range(planes)]
    down = [(p, (p - 1) % planes) for p in range(planes)]
    above = lax.ppermute(partial, "rep", down).astype(jnp.float32)
    below = lax.ppermute(partial, "rep", up).astype(jnp.float32)
    other_layer = low(above + below)
    cut = ATT // 2
    own_layer = jnp.concatenate(
        [
            lax.ppermute(other_layer[:, :cut], "rep", down),
            lax.ppermute(other_layer[:, cut:], "rep", up),
        ],
        axis=1,
    )
    mine = jnp.where(at_home, own_layer, other_layer)
    theirs = flip_core(jnp.where(at_home, other_layer, own_layer))
    attention = jnp.where(first_core, mine, theirs).astype(jnp.float32)
    hidden = jnp.where(first_core, theirs, mine).astype(jnp.float32)
    query, kv, out, c_query, c_kv, c_out, w_in, w_ffn = unpack(attention, hidden)
    ordered = (
        own_gains,
        query,
        kv,
        out,
        own_table.reshape(2, HEADS),
        c_query,
        c_kv,
        c_out,
        w_in,
        w_ffn,
    )
    return (
        outs[0].reshape(1, BATCHES, 1, TOKENS, WIDE),
        outs[1].reshape(1, BATCHES, 1, TOKENS, WIDE),
        encoder_total.reshape(BATCHES, 1, STATES, WIDE),
    ) + tuple(member[None] for member in ordered)


def solution(mesh):
    return jax.shard_map(
        shards,
        mesh=mesh,
        in_specs=(
            P(None, ("fsdp", "rep"), None, None),
            P(None, ("fsdp", "rep"), None, None),
            P(None, ("fsdp", "rep"), None, None),
            P(None, ("fsdp", "rep"), None),
            P(None, ("fsdp", "rep"), None),
            P("section", None, "fsdp"),
            P("section", "fsdp", None),
            P("section", "fsdp", None, None),
            P("section", "fsdp", None),
            P("section", "fsdp", None),
            P("section", "fsdp", None),
            P("section", "fsdp", None, None),
            P("section", "fsdp", None),
            P("section", "fsdp", None, None),
            P("section", "fsdp", None),
        ),
        out_specs=(
            P("section", None, ("fsdp", "rep"), None, None),
            P("section", None, ("fsdp", "rep"), None, None),
            P(None, ("fsdp", "rep"), None, None),
            P("section", None, "fsdp"),
            P("section", "fsdp", None),
            P("section", "fsdp", None, None),
            P("section", "fsdp", None),
            P("section", "fsdp", None),
            P("section", "fsdp", None),
            P("section", "fsdp", None, None),
            P("section", "fsdp", None),
            P("section", "fsdp", None, None),
            P("section", "fsdp", None),
        ),
        check_vma=False,
    )
```

```python
import jax
import jax.numpy as jnp
import numpy as np
from jax import lax
from jax.experimental import pallas as pl
from jax.experimental.pallas import tpu as pltpu
from jax.sharding import PartitionSpec as P

HEADS = 12
HEAD = 64
BUCKETS = 32
MAX_DIST = 128
PARTS = 16
GELU_SCALE = float(np.sqrt(2.0 / np.pi))


epsilon = 1e-06
highest = lax.Precision.HIGHEST


def bucket_row(length):
    distance = np.arange(length)
    half_count = BUCKETS // 2
    scaled = (
        np.log(np.maximum(distance, half_count) / half_count)
        / np.log(MAX_DIST / half_count)
        * (BUCKETS - half_count)
    )
    far_bucket = np.minimum(half_count + np.floor(scaled).astype(np.int32), BUCKETS - 1)
    return np.where(distance < half_count, distance, far_bucket).astype(np.int32)


def bucket_onehot(length):
    return (bucket_row(length)[None, :] == np.arange(BUCKETS)[:, None]).astype(np.float32)


def spread_distance(by_distance):
    head_count, length = by_distance.shape
    padded_row = jnp.concatenate(
        [jnp.zeros((head_count, length - 1), jnp.float32), by_distance], axis=1
    )
    tiled = jnp.tile(padded_row, (1, length))
    tiled = jnp.concatenate([tiled, jnp.zeros((head_count, length), jnp.float32)], axis=1)
    return tiled.reshape(head_count, length, 2 * length)[:, :, :length][:, :, ::-1]


def gather_distance(grid):
    head_count, length, _ = grid.shape
    flipped = jnp.concatenate(
        [grid[:, :, ::-1], jnp.zeros((head_count, length, length), jnp.float32)], axis=2
    )
    flat = flipped.reshape(head_count, 2 * length * length)[:, : length * (2 * length - 1)]
    return jnp.sum(flat.reshape(head_count, length, 2 * length - 1), axis=1)[:, length - 1 :]


ROWS_OWN = 48
TOKENS = 64
WIDE = 768
FF = 2048
GROUP = 256
GROUPS = 3
BATCHES = 2
STATES = 256
CHUNK = 512
ATT = 6144
ALL_TOKENS = (BATCHES * TOKENS, WIDE)
ALL_STATES = (BATCHES * STATES, WIDE)
HIDDEN = (BATCHES * TOKENS, FF)
VMEM_BYTES = 60 * 1024 * 1024
FULL = (PARTS, ROWS_OWN, WIDE)
GATED = (PARTS, ROWS_OWN, FF)
DOWN = (PARTS, FF // PARTS, WIDE)
RING = 4
DOWN_PIECES = [(piece, block) for piece in range(GROUPS) for block in range(8)]


def product(left, right, along_left=1, along_right=0):
    return lax.dot_general(
        left,
        right,
        (((along_left,), (along_right,)), ((), ())),
        preferred_element_type=jnp.float32,
    )


def low(value):
    return value.astype(jnp.bfloat16)


def same_head():
    row = lax.broadcasted_iota(jnp.int32, (GROUP, GROUP), 0) // HEAD
    lane = lax.broadcasted_iota(jnp.int32, (GROUP, GROUP), 1) // HEAD
    return jnp.where(row == lane, 1.0, 0.0)


def spread_heads(block, own_low):
    return jnp.concatenate([block] * 4, axis=0) * own_low


def fold_heads(block, own):
    kept = block * own
    return kept[:64] + kept[64:128] + kept[128:192] + kept[192:]


def scale_of(value):
    return lax.rsqrt(jnp.mean(value * value, axis=-1, keepdims=True) + epsilon)


def norm_back(grad, value, gain):
    scale = scale_of(value)
    carried = grad * gain
    mean = jnp.mean(value * carried, axis=-1, keepdims=True)
    grad_value = carried * scale - value * (scale * scale * scale) * mean
    grad_gain = jnp.sum(grad * value * scale, axis=0, keepdims=True)
    return grad_value, grad_gain


def square(ref):
    return ref[...].reshape(WIDE, WIDE)


def down_at(ref, piece, block):
    return ref.at[:, 1, pl.ds(16 * piece, 16), pl.ds(2 * FF + GROUP * block, GROUP)]


def rows_at(ref, piece, block):
    return ref.at[:, pl.ds(16 * block, 16), pl.ds(GROUP * piece, GROUP)]


def softmax_rows(scores):
    raised = jnp.exp(scores - jnp.max(scores, axis=-1, keepdims=True))
    return raised / jnp.sum(raised, axis=-1, keepdims=True)


def gelu_parts(gate):
    cube = gate * gate * gate
    bent = jnp.tanh(GELU_SCALE * (gate + 0.044715 * cube))
    half = 0.5 * (1.0 + bent)
    slope = half + 0.5 * gate * (1.0 - bent * bent) * GELU_SCALE * (
        1.0 + 3.0 * 0.044715 * gate * gate
    )
    return gate * half, slope


def weight_copies(weight, slots, sems):
    copies = {}
    for place, (name, column) in enumerate(
        (("q", 0), ("k", 1), ("v", 2), ("o", 3), ("cq", 4), ("ck", 5), ("cv", 6), ("co", 7))
    ):
        if name in slots:
            source = weight.at[:, 0, :, pl.ds(WIDE * column, WIDE)]
            copies[name] = [pltpu.make_async_copy(source, slots[name], sems.at[place])]
    for place, (name, column) in enumerate((("gate", 0), ("up", FF))):
        if name in slots:
            source = weight.at[:, 1, :, pl.ds(column, FF)]
            copies[name] = [pltpu.make_async_copy(source, slots[name], sems.at[8 + place])]
    if "down" in slots:
        copies["down"] = [
            pltpu.make_async_copy(
                down_at(weight, piece, block),
                rows_at(slots["down"], piece, block),
                sems.at[10 + place],
            )
            for place, (piece, block) in enumerate(DOWN_PIECES)
        ]
    return copies


def begin(copies, names):
    for name in names:
        for copy in copies[name]:
            copy.start()


def finish(copies, name):
    for copy in copies[name]:
        copy.wait()


def forward_body(
    keys_given,
    x_ref,
    enc_ref,
    self_add_ref,
    cross_add_ref,
    gains_ref,
    weight,
    out_ref,
    n1_ref,
    q_ref,
    k_ref,
    v_ref,
    p_ref,
    o_ref,
    a2_ref,
    n2_ref,
    cq_ref,
    ck_ref,
    cv_ref,
    cp_ref,
    co_ref,
    a3_ref,
    n3_ref,
    gate_ref,
    up_ref,
    hid_ref,
    wq,
    wk,
    wv,
    wo,
    wcq,
    wck,
    wcv,
    wco,
    wg,
    wu,
    wd,
    sems,
):
    slots = dict(q=wq, k=wk, v=wv, o=wo, cq=wcq, co=wco, gate=wg, up=wu, down=wd)
    if not keys_given:
        slots.update(ck=wck, cv=wcv)
    copies = weight_copies(weight, slots, sems)
    if not keys_given:
        begin(copies, ("ck", "cv"))
    begin(copies, ("q", "k", "v", "o", "cq", "co", "gate", "up", "down"))
    own = same_head()
    own_low = low(own)
    stream = x_ref[...].astype(jnp.float32)
    normed = low(stream * scale_of(stream) * gains_ref[0:1])
    n1_ref[...] = normed
    if not keys_given:
        for name, held_weight, target in (("ck", wck, ck_ref), ("cv", wcv, cv_ref)):
            finish(copies, name)
            for row in range(BATCHES):
                part = pl.ds(STATES * row, STATES)
                target[part] = low(product(enc_ref[part], square(held_weight)))
    finish(copies, "q")
    q_ref[...] = low(product(normed, square(wq)))
    finish(copies, "k")
    k_ref[...] = low(product(normed, square(wk)))
    finish(copies, "v")
    v_ref[...] = low(product(normed, square(wv)))
    for row in range(BATCHES):
        part = pl.ds(TOKENS * row, TOKENS)
        for group in range(GROUPS):
            lanes = pl.ds(GROUP * group, GROUP)
            spread = spread_heads(q_ref[part, lanes], own_low)
            scores = product(spread, k_ref[part, lanes], 1, 1) + self_add_ref[row, lanes]
            chance = softmax_rows(scores)
            p_ref[row, lanes] = chance
            mixed = product(low(chance), v_ref[part, lanes])
            o_ref[part, lanes] = low(fold_heads(mixed, own))
    finish(copies, "o")
    stream = stream + product(o_ref[...], square(wo))
    a2_ref[...] = stream
    normed = low(stream * scale_of(stream) * gains_ref[1:2])
    n2_ref[...] = normed
    finish(copies, "cq")
    cq_ref[...] = low(product(normed, square(wcq)))
    for row in range(BATCHES):
        part = pl.ds(TOKENS * row, TOKENS)
        keys = pl.ds(STATES * row, STATES)
        add = jnp.concatenate([cross_add_ref[row]] * 4, axis=0)
        for group in range(GROUPS):
            lanes = pl.ds(GROUP * group, GROUP)
            spread = spread_heads(cq_ref[part, lanes], own_low)
            scores = product(spread, ck_ref[keys, lanes], 1, 1) + add
            chance = softmax_rows(scores)
            cp_ref[row, lanes] = chance
            mixed = product(low(chance), cv_ref[keys, lanes])
            co_ref[part, lanes] = low(fold_heads(mixed, own))
    finish(copies, "co")
    stream = a2_ref[...] + product(co_ref[...], square(wco))
    a3_ref[...] = stream
    n3_ref[...] = low(stream * scale_of(stream) * gains_ref[2:3])
    finish(copies, "gate")
    finish(copies, "up")
    finish(copies, "down")

    def step(index, total):
        lanes = pl.ds(pl.multiple_of(index * CHUNK, CHUNK), CHUNK)
        rows = n3_ref[...]
        gate = product(rows, wg[:, :, lanes].reshape(WIDE, CHUNK))
        up = product(rows, wu[:, :, lanes].reshape(WIDE, CHUNK))
        gate_ref[:, lanes] = gate
        up_ref[:, lanes] = up
        bent = 0.5 * (1.0 + jnp.tanh(GELU_SCALE * (gate + 0.044715 * (gate * gate * gate))))
        hidden = low(gate * bent * up)
        hid_ref[:, lanes] = hidden
        return total + product(hidden, wd[pl.ds(4 * index, 4)].reshape(CHUNK, WIDE))

    total = lax.fori_loop(0, FF // CHUNK, step, jnp.zeros((BATCHES * TOKENS, WIDE), jnp.float32))
    out_ref[...] = low(a3_ref[...] + total)


def first_kernel(
    x_ref, enc_ref, self_add_ref, cross_add_ref, gains_ref, weight, out_ref, ck_ref, cv_ref, *rest
):
    (n1, q, k, v, p, o, a2, n2, cq, cp, co, a3, n3, gate, up, hid, *scratch) = rest
    forward_body(
        False,
        x_ref, enc_ref, self_add_ref, cross_add_ref, gains_ref, weight, out_ref,
        n1, q, k, v, p, o, a2, n2, cq, ck_ref, cv_ref, cp, co, a3, n3, gate, up, hid, *scratch,
    )


def second_kernel(
    x_ref, ck_ref, cv_ref, self_add_ref, cross_add_ref, gains_ref, weight, out_ref, *rest
):
    (n1, q, k, v, p, o, a2, n2, cq, cp, co, a3, n3, gate, up, hid, *scratch) = rest
    (wq, wk, wv, wo, wcq, wco, wg, wu, wd, sems) = scratch
    forward_body(
        True,
        x_ref, None, self_add_ref, cross_add_ref, gains_ref, weight, out_ref,
        n1, q, k, v, p, o, a2, n2, cq, ck_ref, cv_ref, cp, co, a3, n3, gate, up, hid,
        wq, wk, wv, wo, wcq, None, None, wco, wg, wu, wd, sems,
    )


def core_is(part):
    return lax.axis_index("section") == part


def push(source, keep, send, part, window, sem):
    @pl.when(core_is(part))
    def _():
        pltpu.make_async_copy(source, keep.at[window], sem).start()

    @pl.when(jnp.logical_not(core_is(part)))
    def _():
        pltpu.make_async_copy(source, send.at[window], sem).start()

    return pltpu.make_async_copy(source, keep.at[window], sem)


def columns(start, width):
    return (slice(None), slice(None), slice(None), pl.ds(start, width))


def put_square(slot, part, lanes, value):
    value = value.reshape(RING, RING, ROWS_OWN, value.shape[-1])
    if part == 1:
        slot[:, :, :, lanes] = value
    else:
        for place in range(RING):
            slot[:, place, :, lanes] = value[place]


def hidden_back(with_grads, c_ref, a3_ref, gains_ref, gate_ref, up_ref, wg, wu, wd, extra):
    def step(index, total):
        lanes = pl.ds(pl.multiple_of(index * CHUNK, CHUNK), CHUNK)
        grad = product(c_ref[...], wd[pl.ds(4 * index, 4)].reshape(CHUNK, WIDE), 1, 1)
        bent, slope = gelu_parts(gate_ref[:, lanes])
        dgate = low(grad * up_ref[:, lanes] * slope)
        dup = low(grad * bent)
        total = total + product(dgate, wg[:, :, lanes].reshape(WIDE, CHUNK), 1, 1)
        total = total + product(dup, wu[:, :, lanes].reshape(WIDE, CHUNK), 1, 1)
        if with_grads:
            n3_ref, hid_ref, gg, gu, gd0, gd1 = extra
            rows = n3_ref[...]
            put_square(gg, 0, lanes, low(product(rows, dgate, 0, 0)))
            put_square(gu, 1, lanes, low(product(rows, dup, 0, 0)))
            grad = low(product(hid_ref[:, lanes], c_ref[...], 0, 0))
            grad = grad.reshape(RING, FF // PARTS, WIDE)
            gd0[:, pl.ds(index, 1)] = grad[:, : FF // PARTS // 2][:, None]
            gd1[pl.ds(index, 1)] = grad[:, FF // PARTS // 2 :][None]
        return total

    grad = lax.fori_loop(0, FF // CHUNK, step, jnp.zeros(ALL_TOKENS, jnp.float32))
    back, dgain = norm_back(grad, a3_ref[...], gains_ref[2:3])
    return c_ref[...].astype(jnp.float32) + back, dgain


def cross_back(
    stream, finish_weight, gains_ref, a2_ref, cq_ref, ck_ref, cv_ref, cp_ref, wcq, wco,
    dc_ref, dcq_ref, dck_ref, dcv_ref,
):
    own = same_head()
    own_low = low(own)
    dc_ref[...] = low(stream)
    finish_weight("co")
    datt = low(product(dc_ref[...], square(wco), 1, 1))
    for row in range(BATCHES):
        part = pl.ds(TOKENS * row, TOKENS)
        keys = pl.ds(STATES * row, STATES)
        for group in range(GROUPS):
            lanes = pl.ds(GROUP * group, GROUP)
            left = GROUP * group
            dout = spread_heads(
                datt[TOKENS * row : TOKENS * (row + 1), left : left + GROUP], own_low
            )
            spread = spread_heads(cq_ref[part, lanes], own_low)
            chance = cp_ref[row, lanes]
            dchance = product(dout, cv_ref[keys, lanes], 1, 1)
            dcv_ref[keys, lanes] = low(product(low(chance), dout, 0, 0))
            inner = jnp.sum(chance * dchance, axis=-1, keepdims=True)
            dscore = low(chance * (dchance - inner))
            dcq_ref[part, lanes] = low(fold_heads(product(dscore, ck_ref[keys, lanes]), own))
            dck_ref[keys, lanes] = low(product(dscore, spread, 0, 0))
    finish_weight("cq")
    grad = product(dcq_ref[...], square(wcq), 1, 1)
    back, dgain = norm_back(grad, a2_ref[...], gains_ref[1:2])
    return stream + back, dgain


def self_back(
    stream, finish_weight, gains_ref, x_ref, q_ref, k_ref, v_ref, p_ref, wq, wk, wv, wo,
    dself_ref, dq_ref, dk_ref, dv_ref, dscore_ref,
):
    own = same_head()
    own_low = low(own)
    dself_ref[...] = low(stream)
    finish_weight("o")
    datt = low(product(dself_ref[...], square(wo), 1, 1))
    for row in range(BATCHES):
        part = pl.ds(TOKENS * row, TOKENS)
        for group in range(GROUPS):
            lanes = pl.ds(GROUP * group, GROUP)
            left = GROUP * group
            dout = spread_heads(
                datt[TOKENS * row : TOKENS * (row + 1), left : left + GROUP], own_low
            )
            spread = spread_heads(q_ref[part, lanes], own_low)
            chance = p_ref[row, lanes]
            dchance = product(dout, v_ref[part, lanes], 1, 1)
            dv_ref[part, lanes] = low(product(low(chance), dout, 0, 0))
            inner = jnp.sum(chance * dchance, axis=-1, keepdims=True)
            dscore = low(chance * (dchance - inner))
            if dscore_ref is not None:
                if row == 0:
                    dscore_ref[lanes] = dscore.astype(jnp.float32)
                else:
                    dscore_ref[lanes] += dscore.astype(jnp.float32)
            dq_ref[part, lanes] = low(fold_heads(product(dscore, k_ref[part, lanes]), own))
            dk_ref[part, lanes] = low(product(dscore, spread, 0, 0))
    finish_weight("q")
    grad = product(dq_ref[...], square(wq), 1, 1)
    finish_weight("k")
    grad = grad + product(dk_ref[...], square(wk), 1, 1)
    finish_weight("v")
    grad = grad + product(dv_ref[...], square(wv), 1, 1)
    back, dgain = norm_back(grad, x_ref[...].astype(jnp.float32), gains_ref[0:1])
    return stream + back, dgain


def chain_kernel(
    c_ref, x_ref, gains_ref, q_ref, k_ref, v_ref, p_ref, a2_ref, cq_ref, ck_ref, cv_ref, cp_ref,
    a3_ref, gate_ref, up_ref, weight,
    da_ref,
    dc_ref, dcq_ref, dck_ref, dcv_ref, dself_ref, dq_ref, dk_ref, dv_ref,
    wq, wk, wv, wo, wcq, wco, wg, wu, wd, sems,
):
    slots = dict(q=wq, k=wk, v=wv, o=wo, cq=wcq, co=wco, gate=wg, up=wu, down=wd)
    copies = weight_copies(weight, slots, sems)
    begin(copies, ("down", "gate", "up", "co", "cq", "o", "q", "k", "v"))
    for name in ("down", "gate", "up"):
        finish(copies, name)

    def finish_weight(name):
        finish(copies, name)

    stream, _ = hidden_back(False, c_ref, a3_ref, gains_ref, gate_ref, up_ref, wg, wu, wd, None)
    stream, _ = cross_back(
        stream, finish_weight, gains_ref, a2_ref, cq_ref, ck_ref, cv_ref, cp_ref, wcq, wco,
        dc_ref, dcq_ref, dck_ref, dcv_ref,
    )
    stream, _ = self_back(
        stream, finish_weight, gains_ref, x_ref, q_ref, k_ref, v_ref, p_ref, wq, wk, wv, wo,
        dself_ref, dq_ref, dk_ref, dv_ref, None,
    )
    da_ref[...] = low(stream)


def hidden_kernel(
    c_ref, a3_ref, gains_ref, gate_ref, up_ref, n3_ref, hid_ref, weight,
    stream_ref, dgain_ref, keep, send,
    wg, wu, wd, gg, gu, gd0, gd1, sems, out_sems,
):
    copies = weight_copies(weight, dict(gate=wg, up=wu, down=wd), sems)
    begin(copies, ("down", "gate", "up"))
    for name in ("down", "gate", "up"):
        finish(copies, name)
    stream, dgain = hidden_back(
        True, c_ref, a3_ref, gains_ref, gate_ref, up_ref, wg, wu, wd,
        (n3_ref, hid_ref, gg, gu, gd0, gd1),
    )
    sent = []
    for part, (wide, tall) in enumerate(((gg, gd0), (gu, gd1))):
        sent.append(push(wide, keep, send, part, columns(0, FF), out_sems.at[part]))
        for piece in range(GROUPS):
            for block in range(4):
                source = tall.at[:, :, pl.ds(16 * block, 16), pl.ds(GROUP * piece, GROUP)]
                window = (
                    slice(None),
                    slice(None),
                    pl.ds(16 * piece, 16),
                    pl.ds(FF + GROUP * block, GROUP),
                )
                place = 2 + 12 * part + 4 * piece + block
                sent.append(push(source, keep, send, part, window, out_sems.at[place]))
    stream_ref[...] = stream
    dgain_ref[...] = dgain
    for copy in sent:
        copy.wait()


def cross_kernel(
    stream_ref, gains_ref, a2_ref, cq_ref, ck_ref, cv_ref, cp_ref, weight,
    next_ref, dgain_ref, dc_ref, dcq_ref, dck_ref, dcv_ref,
    wcq, wco, sems,
):
    copies = weight_copies(weight, dict(cq=wcq, co=wco), sems)
    begin(copies, ("co", "cq"))

    def finish_weight(name):
        finish(copies, name)

    stream, dgain = cross_back(
        stream_ref[...], finish_weight, gains_ref, a2_ref, cq_ref, ck_ref, cv_ref, cp_ref,
        wcq, wco, dc_ref, dcq_ref, dck_ref, dcv_ref,
    )
    next_ref[...] = stream
    dgain_ref[...] = dgain


def self_kernel(
    stream_ref, x_ref, gains_ref, q_ref, k_ref, v_ref, p_ref,
    enc_ref, n1_ref, o_ref, n2_ref, co_ref, dc_ref, dcq_ref, dck_ref, dcv_ref, weight,
    da_ref, dgain_ref, dscore_ref, denc_ref, keep, send,
    dself_ref, dq_ref, dk_ref, dv_ref,
    wq, wk, wv, wo, wck, wcv, g0, g1, g2, g3, g4, g5, g6, g7, sems, out_sems,
):
    slots = dict(q=wq, k=wk, v=wv, o=wo, ck=wck, cv=wcv)
    copies = weight_copies(weight, slots, sems)
    begin(copies, ("o", "q", "k", "v", "ck", "cv"))

    def finish_weight(name):
        finish(copies, name)

    sent = []

    def emit(slot, part, column, left, right):
        put_square(slot, part, slice(None), low(product(left[...], right[...], 0, 0)))
        window = columns(WIDE * column, WIDE)
        sent.append(push(slot, keep, send, part, window, out_sems.at[len(sent)]))

    emit(g0, 0, 0, co_ref, dc_ref)
    emit(g1, 0, 1, n2_ref, dcq_ref)
    emit(g2, 1, 0, enc_ref, dck_ref)
    emit(g3, 1, 1, enc_ref, dcv_ref)
    stream, dgain = self_back(
        stream_ref[...], finish_weight, gains_ref, x_ref, q_ref, k_ref, v_ref, p_ref,
        wq, wk, wv, wo, dself_ref, dq_ref, dk_ref, dv_ref, dscore_ref,
    )
    da_ref[...] = low(stream)
    dgain_ref[...] = dgain
    emit(g4, 0, 2, o_ref, dself_ref)
    emit(g5, 0, 3, n1_ref, dq_ref)
    emit(g6, 1, 2, n1_ref, dk_ref)
    emit(g7, 1, 3, n1_ref, dv_ref)
    finish(copies, "ck")
    finish(copies, "cv")
    for row in range(BATCHES):
        keys = pl.ds(STATES * row, STATES)
        denc_ref[keys] = low(
            product(dck_ref[keys], square(wck), 1, 1) + product(dcv_ref[keys], square(wcv), 1, 1)
        )
    for copy in sent:
        copy.wait()


def in_vmem(count):
    return [pl.BlockSpec(memory_space=pltpu.VMEM)] * count


def held(*shapes):
    return [pltpu.VMEM(shape, jnp.bfloat16) for shape in shapes]


def shape_of(dims, kind=jnp.bfloat16):
    return jax.ShapeDtypeStruct(dims, kind)


params = pltpu.CompilerParams(vmem_limit_bytes=VMEM_BYTES)


SAVED = (
    (ALL_TOKENS, jnp.bfloat16),
    (ALL_TOKENS, jnp.bfloat16),
    (ALL_TOKENS, jnp.bfloat16),
    (ALL_TOKENS, jnp.bfloat16),
    ((BATCHES, WIDE, TOKENS), jnp.float32),
    (ALL_TOKENS, jnp.bfloat16),
    (ALL_TOKENS, jnp.float32),
    (ALL_TOKENS, jnp.bfloat16),
    (ALL_TOKENS, jnp.bfloat16),
    ((BATCHES, WIDE, STATES), jnp.float32),
    (ALL_TOKENS, jnp.bfloat16),
    (ALL_TOKENS, jnp.float32),
    (ALL_TOKENS, jnp.bfloat16),
    (HIDDEN, jnp.float32),
    (HIDDEN, jnp.float32),
    (HIDDEN, jnp.bfloat16),
)


def run_first(x, enc, self_add, cross_add, gains, weight):
    outs = [shape_of(ALL_TOKENS), shape_of(ALL_STATES), shape_of(ALL_STATES)]
    return pl.pallas_call(
        first_kernel,
        out_shape=outs,
        in_specs=in_vmem(5) + [pl.BlockSpec(memory_space=pl.ANY)],
        out_specs=in_vmem(len(outs)),
        scratch_shapes=[pltpu.VMEM(dims, kind) for dims, kind in SAVED]
        + held(*[FULL] * 8, GATED, GATED, DOWN)
        + [pltpu.SemaphoreType.DMA((34,))],
        compiler_params=params,
        name="first_forward",
    )(x, enc, self_add, cross_add, gains, weight)


def run_second(x, ck, cv, self_add, cross_add, gains, weight):
    outs = [shape_of(ALL_TOKENS)] + [shape_of(dims, kind) for dims, kind in SAVED]
    return pl.pallas_call(
        second_kernel,
        out_shape=outs,
        in_specs=in_vmem(6) + [pl.BlockSpec(memory_space=pl.ANY)],
        out_specs=in_vmem(len(outs)),
        scratch_shapes=held(*[FULL] * 6, GATED, GATED, DOWN) + [pltpu.SemaphoreType.DMA((34,))],
        compiler_params=params,
        name="second_forward",
    )(x, ck, cv, self_add, cross_add, gains, weight)


HALF = (RING, RING, ROWS_OWN, ATT // 2)
RINGED = (RING, RING, ROWS_OWN, WIDE)
RINGED_WIDE = (RING, RING, ROWS_OWN, FF)
RINGED_TALL = (RING, RING, FF // PARTS // 2, WIDE)
ANYWHERE = pl.BlockSpec(memory_space=pl.ANY)
DMAS = pltpu.SemaphoreType.DMA((34,))


def run_chain(cotangent, x, gains, saved, weight):
    (ck, cv, n1, q, k, v, p, o, a2, n2, cq, cp, co, a3, n3, gate, up, hid) = saved
    return pl.pallas_call(
        chain_kernel,
        out_shape=shape_of(ALL_TOKENS),
        in_specs=in_vmem(15) + [ANYWHERE],
        out_specs=in_vmem(1)[0],
        scratch_shapes=held(
            ALL_TOKENS, ALL_TOKENS, ALL_STATES, ALL_STATES, *[ALL_TOKENS] * 4,
            *[FULL] * 6, GATED, GATED, DOWN,
        )
        + [DMAS],
        compiler_params=params,
        name="backward_chain",
    )(cotangent, x, gains, q, k, v, p, a2, cq, ck, cv, cp, a3, gate, up, weight)


def run_hidden(cotangent, gains, saved, weight):
    (ck, cv, n1, q, k, v, p, o, a2, n2, cq, cp, co, a3, n3, gate, up, hid) = saved
    return pl.pallas_call(
        hidden_kernel,
        out_shape=[
            shape_of(ALL_TOKENS, jnp.float32),
            shape_of((1, WIDE), jnp.float32),
            shape_of(HALF),
            shape_of(HALF),
        ],
        in_specs=in_vmem(7) + [ANYWHERE],
        out_specs=in_vmem(2) + [ANYWHERE, ANYWHERE],
        scratch_shapes=held(
            GATED, GATED, DOWN, RINGED_WIDE, RINGED_WIDE, RINGED_TALL, RINGED_TALL
        )
        + [DMAS, DMAS],
        compiler_params=params,
        name="hidden_backward",
    )(cotangent, a3, gains, gate, up, n3, hid, weight)


def run_cross(stream, gains, saved, weight):
    (ck, cv, n1, q, k, v, p, o, a2, n2, cq, cp, co, a3, n3, gate, up, hid) = saved
    return pl.pallas_call(
        cross_kernel,
        out_shape=[
            shape_of(ALL_TOKENS, jnp.float32),
            shape_of((1, WIDE), jnp.float32),
            shape_of(ALL_TOKENS),
            shape_of(ALL_TOKENS),
            shape_of(ALL_STATES),
            shape_of(ALL_STATES),
        ],
        in_specs=in_vmem(7) + [ANYWHERE],
        out_specs=in_vmem(6),
        scratch_shapes=held(FULL, FULL) + [DMAS],
        compiler_params=params,
        name="cross_backward",
    )(stream, gains, a2, cq, ck, cv, cp, weight)


def run_self(stream, x, gains, enc, saved, records, weight):
    (ck, cv, n1, q, k, v, p, o, a2, n2, cq, cp, co, a3, n3, gate, up, hid) = saved
    return pl.pallas_call(
        self_kernel,
        out_shape=[
            shape_of(ALL_TOKENS),
            shape_of((1, WIDE), jnp.float32),
            shape_of((WIDE, TOKENS), jnp.float32),
            shape_of(ALL_STATES),
            shape_of(HALF),
            shape_of(HALF),
        ],
        in_specs=in_vmem(16) + [ANYWHERE],
        out_specs=in_vmem(4) + [ANYWHERE, ANYWHERE],
        scratch_shapes=held(*[ALL_TOKENS] * 4, *[FULL] * 6, *[RINGED] * 8) + [DMAS, DMAS],
        compiler_params=params,
        name="self_backward",
    )(stream, x, gains, q, k, v, p, enc, n1, o, n2, co, *records, weight)


def pack_attention(query, kv, out, c_query, c_kv, c_out):
    rows = query.shape[0]
    return jnp.concatenate(
        [query, kv.reshape(rows, -1), out, c_query, c_kv.reshape(rows, -1), c_out], axis=1
    )


def pack_hidden(w_in, w_ffn):
    rows = w_in.shape[0]
    pieces = w_ffn.reshape(8, 16, GROUPS, GROUP).transpose(2, 1, 0, 3)
    return jnp.concatenate([w_in.reshape(rows, -1), pieces.reshape(rows, FF)], axis=1)


def unpack(first, second):
    rows = first.shape[0]
    squares = [
        part[:, ATT // 2 + WIDE * place : ATT // 2 + WIDE * (place + 1)]
        for part in (first, second)
        for place in range(4)
    ]
    c_out, c_query, out, query, c_key, c_value, key, value = squares
    tall = [
        part[:, FF : FF + 1024].reshape(GROUPS, 16, 4, GROUP).transpose(2, 1, 0, 3)
        for part in (first, second)
    ]
    tall = [part.reshape(FF // PARTS // 2, WIDE) for part in tall]
    return (
        query,
        jnp.stack([key, value], axis=1),
        out,
        c_query,
        jnp.stack([c_key, c_value], axis=1),
        c_out,
        jnp.stack([first[:, :FF], second[:, :FF]], axis=1),
        jnp.concatenate(tall, axis=0),
    )


def score_terms(table, dec_ids, enc_ids):
    positions = jnp.arange(TOKENS)
    by_distance = jnp.dot(table.astype(jnp.float32).T, bucket_onehot(TOKENS), precision=highest)
    bias = spread_distance(by_distance)
    allowed = (dec_ids[:, :, None] == dec_ids[:, None, :]) & (
        positions[None, :] <= positions[:, None]
    )
    self_add = jnp.where(allowed[:, None], bias[None], -jnp.inf)
    cross_add = jnp.where(dec_ids[:, :, None] == enc_ids[:, None, :], 0.0, -jnp.inf)
    return self_add.reshape(BATCHES, WIDE, TOKENS), cross_add


def shards(
    layer_in,
    cotangent,
    encoder,
    dec_segments,
    enc_segments,
    norm_gains,
    self_query,
    self_kv,
    self_out,
    rel_bias,
    cross_query,
    cross_kv,
    cross_out,
    ffn_in,
    ffn_out,
):
    core = lax.axis_index("section")
    part_index = lax.axis_index("fsdp")
    plane = lax.axis_index("rep")
    planes = lax.axis_size("rep")
    layer = lax.rem(plane, 2)
    first_core = core == 0
    at_home = core == layer

    def place(core_index, plane_index):
        return core_index * planes + plane_index

    def flip_core(value):
        return lax.ppermute(value, "section", [(0, 1), (1, 0)])

    def from_home(value):
        pairs = [(place(p % 2, p), place(1 - p % 2, p)) for p in range(planes)]
        return jnp.where(at_home, value, lax.ppermute(value, ("section", "rep"), pairs))

    def beside(value):
        return lax.ppermute(value, "rep", [(p, p ^ 1) for p in range(planes)])

    def rows_for_layer(value):
        pairs = [(place(p % 2, p), place(p % 2, p ^ 1)) for p in range(planes)]
        return jnp.where(at_home, value, lax.ppermute(value, ("section", "rep"), pairs))

    def rows_back(value):
        pairs = [(place(1 - p % 2, p), place(p % 2, p ^ 1)) for p in range(planes)]
        return jnp.where(at_home, value, lax.ppermute(value, ("section", "rep"), pairs))

    def between_layers(value, steps):
        pairs = [(p, p + steps) for p in range(planes) if p % 2 == (steps < 0)]
        return lax.ppermute(value, "rep", pairs)

    along_z = [[RING * x + z for z in range(RING)] for x in range(RING)]
    along_x = [[RING * x + z for x in range(RING)] for z in range(RING)]
    first_rings = along_z + [[PARTS + d for d in ring] for ring in along_x]
    second_rings = along_x + [[PARTS + d for d in ring] for ring in along_z]

    def add_halves(keep, received):
        total = low(keep.astype(jnp.float32) + received.astype(jnp.float32))
        return total.reshape(WIDE, ATT // 2)

    def scatter(value, rings):
        return lax.psum_scatter(
            value, ("section", "fsdp"), scatter_dimension=0, axis_index_groups=rings, tiled=True
        )

    attention = pack_attention(
        self_query[0], self_kv[0], self_out[0], cross_query[0], cross_kv[0], cross_out[0]
    )
    hidden = pack_hidden(ffn_in[0], ffn_out[0])
    kept = jnp.where(first_core, attention, hidden)
    given_away = jnp.where(first_core, hidden, attention)
    half = jnp.where(at_home, kept, flip_core(given_away))
    weight = lax.all_gather(half, ("fsdp", "section"), axis=0, tiled=True)
    weight = weight.reshape(PARTS, 2, ROWS_OWN, ATT)
    small = jnp.zeros((8, 128), jnp.bfloat16)
    small = small.at[:3, :ROWS_OWN].set(norm_gains[0])
    small = small.at[3:5, :HEADS].set(rel_bias[0])
    small = lax.all_gather(from_home(small), "fsdp", axis=0, tiled=False)
    gains = small[:, :3, :ROWS_OWN].transpose(1, 0, 2).reshape(3, WIDE).astype(jnp.float32)
    table = small[:, 3:5, :HEADS].reshape(BUCKETS, HEADS)
    ids = jnp.concatenate([dec_segments[:, 0], enc_segments[:, 0]], axis=1)
    ids = rows_for_layer(ids)
    self_add, cross_add = score_terms(table, ids[:, :TOKENS], ids[:, TOKENS:])
    ends = jnp.stack([layer_in[:, 0].reshape(ALL_TOKENS), cotangent[:, 0].reshape(ALL_TOKENS)])
    ends = rows_for_layer(ends)
    rows_in, given = ends[0], ends[1]
    enc = rows_for_layer(encoder[:, 0].reshape(ALL_STATES))
    weight, rows_in, given, enc, self_add, cross_add, gains = lax.optimization_barrier(
        (weight, rows_in, given, enc, self_add, cross_add, gains)
    )
    first, ck, cv = run_first(rows_in, enc, self_add, cross_add, gains, weight)
    current = jnp.where(layer == 0, rows_in, between_layers(first, 1))
    result, *saved = run_second(current, ck, cv, self_add, cross_add, gains, weight)
    saved = [ck, cv] + saved
    grad_first = run_chain(given, current, gains, saved, weight)
    incoming = jnp.where(layer == 1, given, between_layers(grad_first, -1))
    stream, gain_three, keep, send = run_hidden(incoming, gains, saved, weight)
    received = flip_core(send)
    stream, gain_two, *records = run_cross(stream, gains, saved, weight)
    wide_sum = add_halves(keep, received)
    wide_sum, stream = lax.optimization_barrier((wide_sum, stream))
    wide_part = scatter(wide_sum, first_rings)
    grad_input, gain_one, grad_scores, grad_enc, keep, send = run_self(
        stream, current, gains, enc, saved, records, weight
    )
    square_part = scatter(add_halves(keep, flip_core(send)), first_rings)
    partial = scatter(jnp.concatenate([wide_part, square_part], axis=1), second_rings)
    grad_gains = jnp.concatenate([gain_one, gain_two, gain_three], axis=0)
    outs = rows_back(jnp.stack([result, grad_input]))
    encoder_total = grad_enc.astype(jnp.float32) + beside(grad_enc).astype(jnp.float32)
    encoder_total = from_home(encoder_total)
    diagonal_sums = gather_distance(grad_scores.reshape(HEADS, TOKENS, TOKENS))
    grad_table = jnp.dot(bucket_onehot(TOKENS), diagonal_sums.T, precision=highest)
    little = jnp.zeros((8, WIDE), jnp.float32)
    little = little.at[:3].set(grad_gains)
    little = little.at[3, : BUCKETS * HEADS].set(grad_table.reshape(-1))
    for axis, bits in (("section", (1,)), ("fsdp", (1, 2, 4, 8)), ("rep", (2,))):
        for bit in bits:
            pairs = [(index, index ^ bit) for index in range(lax.axis_size(axis))]
            little = little + lax.ppermute(little, axis, pairs)
    little = jnp.where(at_home, little, beside(little))
    own_gains = lax.dynamic_slice(little, (0, part_index * ROWS_OWN), (3, ROWS_OWN))
    own_table = lax.dynamic_slice(little, (3, part_index * 2 * HEADS), (1, 2 * HEADS))
    own_table = own_table.reshape(2, HEADS)
    results = (
        outs[0].reshape(1, BATCHES, 1, TOKENS, WIDE),
        outs[1].reshape(1, BATCHES, 1, TOKENS, WIDE),
        encoder_total.reshape(BATCHES, 1, STATES, WIDE),
        own_gains[None],
        own_table[None],
    )
    partial, results = lax.optimization_barrier((partial, results))
    up = [(p, (p + 1) % planes) for p in range(planes)]
    down = [(p, (p - 1) % planes) for p in range(planes)]
    above = lax.ppermute(partial, "rep", down).astype(jnp.float32)
    below = lax.ppermute(partial, "rep", up).astype(jnp.float32)
    other_layer = low(above + below)
    cut = ATT // 2
    own_layer = jnp.concatenate(
        [
            lax.ppermute(other_layer[:, :cut], "rep", down),
            lax.ppermute(other_layer[:, cut:], "rep", up),
        ],
        axis=1,
    )
    mine = jnp.where(at_home, own_layer, other_layer)
    theirs = flip_core(jnp.where(at_home, other_layer, own_layer))
    first_part = jnp.where(first_core, mine, theirs).astype(jnp.float32)
    second_part = jnp.where(first_core, theirs, mine).astype(jnp.float32)
    query, kv, out, *others = [member[None] for member in unpack(first_part, second_part)]
    return (*results[:4], query, kv, out, results[4], *others)


def solution(mesh):
    return jax.shard_map(
        shards,
        mesh=mesh,
        in_specs=(
            P(None, ("fsdp", "rep"), None, None),
            P(None, ("fsdp", "rep"), None, None),
            P(None, ("fsdp", "rep"), None, None),
            P(None, ("fsdp", "rep"), None),
            P(None, ("fsdp", "rep"), None),
            P("section", None, "fsdp"),
            P("section", "fsdp", None),
            P("section", "fsdp", None, None),
            P("section", "fsdp", None),
            P("section", "fsdp", None),
            P("section", "fsdp", None),
            P("section", "fsdp", None, None),
            P("section", "fsdp", None),
            P("section", "fsdp", None, None),
            P("section", "fsdp", None),
        ),
        out_specs=(
            P("section", None, ("fsdp", "rep"), None, None),
            P("section", None, ("fsdp", "rep"), None, None),
            P(None, ("fsdp", "rep"), None, None),
            P("section", None, "fsdp"),
            P("section", "fsdp", None),
            P("section", "fsdp", None, None),
            P("section", "fsdp", None),
            P("section", "fsdp", None),
            P("section", "fsdp", None),
            P("section", "fsdp", None, None),
            P("section", "fsdp", None),
            P("section", "fsdp", None, None),
            P("section", "fsdp", None),
        ),
        check_vma=False,
    )
```

```python
import jax
import jax.numpy as jnp
import numpy as np
from jax import lax
from jax.experimental import pallas as pl
from jax.experimental.pallas import tpu as pltpu
from jax.sharding import PartitionSpec as P

HEADS = 12
HEAD = 64
BUCKETS = 32
MAX_DIST = 128
PARTS = 16
GELU_SCALE = float(np.sqrt(2.0 / np.pi))


epsilon = 1e-06
highest = lax.Precision.HIGHEST


def bucket_row(length):
    distance = np.arange(length)
    half_count = BUCKETS // 2
    scaled = (
        np.log(np.maximum(distance, half_count) / half_count)
        / np.log(MAX_DIST / half_count)
        * (BUCKETS - half_count)
    )
    far_bucket = np.minimum(half_count + np.floor(scaled).astype(np.int32), BUCKETS - 1)
    return np.where(distance < half_count, distance, far_bucket).astype(np.int32)


def bucket_onehot(length):
    return (bucket_row(length)[None, :] == np.arange(BUCKETS)[:, None]).astype(np.float32)


def spread_distance(by_distance):
    head_count, length = by_distance.shape
    padded_row = jnp.concatenate(
        [jnp.zeros((head_count, length - 1), jnp.float32), by_distance], axis=1
    )
    tiled = jnp.tile(padded_row, (1, length))
    tiled = jnp.concatenate([tiled, jnp.zeros((head_count, length), jnp.float32)], axis=1)
    return tiled.reshape(head_count, length, 2 * length)[:, :, :length][:, :, ::-1]


def gather_distance(grid):
    head_count, length, _ = grid.shape
    flipped = jnp.concatenate(
        [grid[:, :, ::-1], jnp.zeros((head_count, length, length), jnp.float32)], axis=2
    )
    flat = flipped.reshape(head_count, 2 * length * length)[:, : length * (2 * length - 1)]
    return jnp.sum(flat.reshape(head_count, length, 2 * length - 1), axis=1)[:, length - 1 :]


ROWS_OWN = 48
TOKENS = 64
WIDE = 768
FF = 2048
GROUP = 256
GROUPS = 3
BATCHES = 2
STATES = 256
CHUNK = 512
CHUNKS = FF // CHUNK
ATT = 6144
ALL_TOKENS = (BATCHES * TOKENS, WIDE)
ALL_STATES = (BATCHES * STATES, WIDE)
HIDDEN = (BATCHES * TOKENS, FF)
VMEM_BYTES = 60 * 1024 * 1024
FULL = (PARTS, ROWS_OWN, WIDE)
GATED = (PARTS, ROWS_OWN, FF)
DOWN = (PARTS, FF // PARTS, WIDE)
RING = 4
LATE_HIDDEN = [name + str(index) for index in range(1, CHUNKS) for name in ("gate", "up")]
DOWN_PIECES = [(piece, block) for piece in range(GROUPS) for block in range(8)]


def product(left, right, along_left=1, along_right=0):
    return lax.dot_general(
        left,
        right,
        (((along_left,), (along_right,)), ((), ())),
        preferred_element_type=jnp.float32,
    )


def low(value):
    return value.astype(jnp.bfloat16)


def same_head():
    row = lax.broadcasted_iota(jnp.int32, (GROUP, GROUP), 0) // HEAD
    lane = lax.broadcasted_iota(jnp.int32, (GROUP, GROUP), 1) // HEAD
    return jnp.where(row == lane, 1.0, 0.0)


def spread_heads(block, own_low):
    return jnp.concatenate([block] * 4, axis=0) * own_low


def fold_heads(block, own):
    kept = block * own
    return kept[:64] + kept[64:128] + kept[128:192] + kept[192:]


def scale_of(value):
    return lax.rsqrt(jnp.mean(value * value, axis=-1, keepdims=True) + epsilon)


def norm_back(grad, value, gain):
    scale = scale_of(value)
    carried = grad * gain
    mean = jnp.mean(value * carried, axis=-1, keepdims=True)
    grad_value = carried * scale - value * (scale * scale * scale) * mean
    grad_gain = jnp.sum(grad * value * scale, axis=0, keepdims=True)
    return grad_value, grad_gain


def square(ref):
    return ref[...].reshape(WIDE, WIDE)


def down_at(ref, piece, block):
    return ref.at[:, 1, pl.ds(16 * piece, 16), pl.ds(2 * FF + GROUP * block, GROUP)]


def rows_at(ref, piece, block):
    return ref.at[:, pl.ds(16 * block, 16), pl.ds(GROUP * piece, GROUP)]


def softmax_rows(scores):
    raised = jnp.exp(scores - jnp.max(scores, axis=-1, keepdims=True))
    return raised / jnp.sum(raised, axis=-1, keepdims=True)


def gelu_parts(gate):
    cube = gate * gate * gate
    bent = jnp.tanh(GELU_SCALE * (gate + 0.044715 * cube))
    half = 0.5 * (1.0 + bent)
    slope = half + 0.5 * gate * (1.0 - bent * bent) * GELU_SCALE * (
        1.0 + 3.0 * 0.044715 * gate * gate
    )
    return gate * half, slope


def weight_copies(weight, slots, sems):
    copies = {}
    for place, (name, column) in enumerate(
        (("q", 0), ("k", 1), ("v", 2), ("o", 3), ("cq", 4), ("ck", 5), ("cv", 6), ("co", 7))
    ):
        if name in slots:
            source = weight.at[:, 0, :, pl.ds(WIDE * column, WIDE)]
            copies[name] = [pltpu.make_async_copy(source, slots[name], sems.at[place])]
    for place, (name, column) in enumerate((("gate", 0), ("up", FF))):
        if name in slots:
            for index in range(CHUNKS):
                start = CHUNK * index
                source = weight.at[:, 1, :, pl.ds(column + start, CHUNK)]
                target = slots[name].at[:, :, pl.ds(start, CHUNK)]
                sem = sems.at[8 + CHUNKS * place + index]
                copies[name + str(index)] = [pltpu.make_async_copy(source, target, sem)]
    if "down" in slots:
        copies["down"] = [
            pltpu.make_async_copy(
                down_at(weight, piece, block),
                rows_at(slots["down"], piece, block),
                sems.at[8 + 2 * CHUNKS + place],
            )
            for place, (piece, block) in enumerate(DOWN_PIECES)
        ]
    return copies


def begin(copies, names):
    for name in names:
        for copy in copies[name]:
            copy.start()


def finish(copies, name):
    for copy in copies[name]:
        copy.wait()


def forward_body(
    keys_given,
    x_ref,
    enc_ref,
    self_add_ref,
    cross_add_ref,
    gains_ref,
    weight,
    out_ref,
    n1_ref,
    q_ref,
    k_ref,
    v_ref,
    p_ref,
    o_ref,
    a2_ref,
    n2_ref,
    cq_ref,
    ck_ref,
    cv_ref,
    cp_ref,
    co_ref,
    a3_ref,
    n3_ref,
    gate_ref,
    up_ref,
    hid_ref,
    wq,
    wk,
    wv,
    wo,
    wcq,
    wck,
    wcv,
    wco,
    wg,
    wu,
    wd,
    sems,
):
    slots = dict(q=wq, k=wk, v=wv, o=wo, cq=wcq, co=wco, gate=wg, up=wu, down=wd)
    if not keys_given:
        slots.update(ck=wck, cv=wcv)
    copies = weight_copies(weight, slots, sems)
    if not keys_given:
        begin(copies, ("ck", "cv"))
    begin(copies, ("q", "k", "v", "o", "cq", "co", "gate0", "up0", "down", *LATE_HIDDEN))
    own = same_head()
    own_low = low(own)
    stream = x_ref[...].astype(jnp.float32)
    normed = low(stream * scale_of(stream) * gains_ref[0:1])
    n1_ref[...] = normed
    if not keys_given:
        for name, held_weight, target in (("ck", wck, ck_ref), ("cv", wcv, cv_ref)):
            finish(copies, name)
            for row in range(BATCHES):
                part = pl.ds(STATES * row, STATES)
                target[part] = low(product(enc_ref[part], square(held_weight)))
    finish(copies, "q")
    q_ref[...] = low(product(normed, square(wq)))
    finish(copies, "k")
    k_ref[...] = low(product(normed, square(wk)))
    finish(copies, "v")
    v_ref[...] = low(product(normed, square(wv)))
    for row in range(BATCHES):
        part = pl.ds(TOKENS * row, TOKENS)
        for group in range(GROUPS):
            lanes = pl.ds(GROUP * group, GROUP)
            spread = spread_heads(q_ref[part, lanes], own_low)
            scores = product(spread, k_ref[part, lanes], 1, 1) + self_add_ref[row, lanes]
            chance = softmax_rows(scores)
            p_ref[row, lanes] = chance
            mixed = product(low(chance), v_ref[part, lanes])
            o_ref[part, lanes] = low(fold_heads(mixed, own))
    finish(copies, "o")
    stream = stream + product(o_ref[...], square(wo))
    a2_ref[...] = stream
    normed = low(stream * scale_of(stream) * gains_ref[1:2])
    n2_ref[...] = normed
    finish(copies, "cq")
    cq_ref[...] = low(product(normed, square(wcq)))
    for row in range(BATCHES):
        part = pl.ds(TOKENS * row, TOKENS)
        keys = pl.ds(STATES * row, STATES)
        add = jnp.concatenate([cross_add_ref[row]] * 4, axis=0)
        for group in range(GROUPS):
            lanes = pl.ds(GROUP * group, GROUP)
            spread = spread_heads(cq_ref[part, lanes], own_low)
            scores = product(spread, ck_ref[keys, lanes], 1, 1) + add
            chance = softmax_rows(scores)
            cp_ref[row, lanes] = chance
            mixed = product(low(chance), cv_ref[keys, lanes])
            co_ref[part, lanes] = low(fold_heads(mixed, own))
    finish(copies, "co")
    stream = a2_ref[...] + product(co_ref[...], square(wco))
    a3_ref[...] = stream
    n3_ref[...] = low(stream * scale_of(stream) * gains_ref[2:3])
    total = a3_ref[...]
    for index in range(CHUNKS):
        lanes = pl.ds(index * CHUNK, CHUNK)
        rows = n3_ref[...]
        finish(copies, "gate" + str(index))
        gate = product(rows, wg[:, :, lanes].reshape(WIDE, CHUNK))
        finish(copies, "up" + str(index))
        up = product(rows, wu[:, :, lanes].reshape(WIDE, CHUNK))
        gate_ref[:, lanes] = gate
        up_ref[:, lanes] = up
        bent = 0.5 * (1.0 + jnp.tanh(GELU_SCALE * (gate + 0.044715 * (gate * gate * gate))))
        hidden = low(gate * bent * up)
        hid_ref[:, lanes] = hidden
        if index == 0:
            finish(copies, "down")
        total = total + product(hidden, wd[pl.ds(4 * index, 4)].reshape(CHUNK, WIDE))
    out_ref[...] = low(total)


def first_kernel(
    x_ref, enc_ref, self_add_ref, cross_add_ref, gains_ref, weight, out_ref, ck_ref, cv_ref, *rest
):
    (n1, q, k, v, p, o, a2, n2, cq, cp, co, a3, n3, gate, up, hid, *scratch) = rest
    forward_body(
        False,
        x_ref, enc_ref, self_add_ref, cross_add_ref, gains_ref, weight, out_ref,
        n1, q, k, v, p, o, a2, n2, cq, ck_ref, cv_ref, cp, co, a3, n3, gate, up, hid, *scratch,
    )


def second_kernel(
    x_ref, ck_ref, cv_ref, self_add_ref, cross_add_ref, gains_ref, weight, out_ref, *rest
):
    (n1, q, k, v, p, o, a2, n2, cq, cp, co, a3, n3, gate, up, hid, *scratch) = rest
    (wq, wk, wv, wo, wcq, wco, wg, wu, wd, sems) = scratch
    forward_body(
        True,
        x_ref, None, self_add_ref, cross_add_ref, gains_ref, weight, out_ref,
        n1, q, k, v, p, o, a2, n2, cq, ck_ref, cv_ref, cp, co, a3, n3, gate, up, hid,
        wq, wk, wv, wo, wcq, None, None, wco, wg, wu, wd, sems,
    )


def core_is(part):
    return lax.axis_index("section") == part


def push(source, keep, send, part, window, sem):
    @pl.when(core_is(part))
    def _():
        pltpu.make_async_copy(source, keep.at[window], sem).start()

    @pl.when(jnp.logical_not(core_is(part)))
    def _():
        pltpu.make_async_copy(source, send.at[window], sem).start()

    return pltpu.make_async_copy(source, keep.at[window], sem)


def columns(start, width):
    return (slice(None), slice(None), slice(None), pl.ds(start, width))


def put_square(slot, part, lanes, value):
    value = value.reshape(RING, RING, ROWS_OWN, value.shape[-1])
    if part == 1:
        slot[:, :, :, lanes] = value
    else:
        for place in range(RING):
            slot[:, place, :, lanes] = value[place]


def hidden_back(finish_weight, emit, c_ref, a3_ref, gains_ref, gate_ref, up_ref, wg, wu, wd):
    total = jnp.zeros(ALL_TOKENS, jnp.float32)
    finish_weight("down")
    for index in range(CHUNKS):
        lanes = pl.ds(index * CHUNK, CHUNK)
        grad = product(c_ref[...], wd[pl.ds(4 * index, 4)].reshape(CHUNK, WIDE), 1, 1)
        bent, slope = gelu_parts(gate_ref[:, lanes])
        dgate = low(grad * up_ref[:, lanes] * slope)
        dup = low(grad * bent)
        finish_weight("gate" + str(index))
        total = total + product(dgate, wg[:, :, lanes].reshape(WIDE, CHUNK), 1, 1)
        finish_weight("up" + str(index))
        total = total + product(dup, wu[:, :, lanes].reshape(WIDE, CHUNK), 1, 1)
        emit(index, lanes, dgate, dup)
    back, dgain = norm_back(total, a3_ref[...], gains_ref[2:3])
    return c_ref[...].astype(jnp.float32) + back, dgain


def cross_back(
    stream, finish_weight, gains_ref, a2_ref, cq_ref, ck_ref, cv_ref, cp_ref, wcq, wco,
    dc_ref, dcq_ref, dck_ref, dcv_ref,
):
    own = same_head()
    own_low = low(own)
    dc_ref[...] = low(stream)
    finish_weight("co")
    datt = low(product(dc_ref[...], square(wco), 1, 1))
    for row in range(BATCHES):
        part = pl.ds(TOKENS * row, TOKENS)
        keys = pl.ds(STATES * row, STATES)
        for group in range(GROUPS):
            lanes = pl.ds(GROUP * group, GROUP)
            left = GROUP * group
            dout = spread_heads(
                datt[TOKENS * row : TOKENS * (row + 1), left : left + GROUP], own_low
            )
            spread = spread_heads(cq_ref[part, lanes], own_low)
            chance = cp_ref[row, lanes]
            dchance = product(dout, cv_ref[keys, lanes], 1, 1)
            dcv_ref[keys, lanes] = low(product(low(chance), dout, 0, 0))
            inner = jnp.sum(chance * dchance, axis=-1, keepdims=True)
            dscore = low(chance * (dchance - inner))
            dcq_ref[part, lanes] = low(fold_heads(product(dscore, ck_ref[keys, lanes]), own))
            dck_ref[keys, lanes] = low(product(dscore, spread, 0, 0))
    finish_weight("cq")
    grad = product(dcq_ref[...], square(wcq), 1, 1)
    back, dgain = norm_back(grad, a2_ref[...], gains_ref[1:2])
    return stream + back, dgain


def self_back(
    stream, finish_weight, gains_ref, x_ref, q_ref, k_ref, v_ref, p_ref, wq, wk, wv, wo,
    dself_ref, dq_ref, dk_ref, dv_ref, dscore_ref,
):
    own = same_head()
    own_low = low(own)
    dself_ref[...] = low(stream)
    finish_weight("o")
    datt = low(product(dself_ref[...], square(wo), 1, 1))
    for row in range(BATCHES):
        part = pl.ds(TOKENS * row, TOKENS)
        for group in range(GROUPS):
            lanes = pl.ds(GROUP * group, GROUP)
            left = GROUP * group
            dout = spread_heads(
                datt[TOKENS * row : TOKENS * (row + 1), left : left + GROUP], own_low
            )
            spread = spread_heads(q_ref[part, lanes], own_low)
            chance = p_ref[row, lanes]
            dchance = product(dout, v_ref[part, lanes], 1, 1)
            dv_ref[part, lanes] = low(product(low(chance), dout, 0, 0))
            inner = jnp.sum(chance * dchance, axis=-1, keepdims=True)
            dscore = low(chance * (dchance - inner))
            if dscore_ref is not None:
                if row == 0:
                    dscore_ref[lanes] = dscore.astype(jnp.float32)
                else:
                    dscore_ref[lanes] += dscore.astype(jnp.float32)
            dq_ref[part, lanes] = low(fold_heads(product(dscore, k_ref[part, lanes]), own))
            dk_ref[part, lanes] = low(product(dscore, spread, 0, 0))
    finish_weight("q")
    grad = product(dq_ref[...], square(wq), 1, 1)
    finish_weight("k")
    grad = grad + product(dk_ref[...], square(wk), 1, 1)
    finish_weight("v")
    grad = grad + product(dv_ref[...], square(wv), 1, 1)
    back, dgain = norm_back(grad, x_ref[...].astype(jnp.float32), gains_ref[0:1])
    return stream + back, dgain


def chain_kernel(
    c_ref, a3_ref, gains_ref, gate_ref, up_ref,
    x_any, q_any, k_any, v_any, p_any, a2_any, cq_any, ck_any, cv_any, cp_any, weight,
    da_ref,
    x_ref, q_ref, k_ref, v_ref, p_ref, a2_ref, cq_ref, ck_ref, cv_ref, cp_ref,
    dc_ref, dcq_ref, dck_ref, dcv_ref, dself_ref, dq_ref, dk_ref, dv_ref,
    wq, wk, wv, wo, wcq, wco, wg, wu, wd, sems, late_sems,
):
    slots = dict(q=wq, k=wk, v=wv, o=wo, cq=wcq, co=wco, gate=wg, up=wu, down=wd)
    copies = weight_copies(weight, slots, sems)
    late = (
        (cq_any, cq_ref), (ck_any, ck_ref), (cv_any, cv_ref), (cp_any, cp_ref), (a2_any, a2_ref),
        (q_any, q_ref), (k_any, k_ref), (v_any, v_ref), (p_any, p_ref), (x_any, x_ref),
    )
    late = [
        pltpu.make_async_copy(source, target, late_sems.at[place])
        for place, (source, target) in enumerate(late)
    ]
    begin(copies, ("down", "gate0", "up0", *LATE_HIDDEN, "co"))
    for copy in late[:5]:
        copy.start()
    begin(copies, ("cq", "o"))
    for copy in late[5:]:
        copy.start()
    begin(copies, ("q", "k", "v"))

    def finish_weight(name):
        finish(copies, name)

    def emit(index, lanes, dgate, dup):
        return None

    stream, _ = hidden_back(
        finish_weight, emit, c_ref, a3_ref, gains_ref, gate_ref, up_ref, wg, wu, wd
    )
    for copy in late[:5]:
        copy.wait()
    stream, _ = cross_back(
        stream, finish_weight, gains_ref, a2_ref, cq_ref, ck_ref, cv_ref, cp_ref, wcq, wco,
        dc_ref, dcq_ref, dck_ref, dcv_ref,
    )
    for copy in late[5:]:
        copy.wait()
    stream, _ = self_back(
        stream, finish_weight, gains_ref, x_ref, q_ref, k_ref, v_ref, p_ref, wq, wk, wv, wo,
        dself_ref, dq_ref, dk_ref, dv_ref, None,
    )
    da_ref[...] = low(stream)


def hidden_kernel(
    c_ref, a3_ref, gains_ref, gate_ref, up_ref, n3_ref, hid_ref, weight,
    stream_ref, dgain_ref, keep, send,
    wg, wu, wd, gg, gu, gd0, gd1, sems, out_sems,
):
    copies = weight_copies(weight, dict(gate=wg, up=wu, down=wd), sems)
    begin(copies, ("down", "gate0", "up0", *LATE_HIDDEN))
    sent = []

    def finish_weight(name):
        finish(copies, name)

    for index in range(RING):
        lanes = pl.ds(index * CHUNK, CHUNK)
        grad = low(product(hid_ref[:, lanes], c_ref[...], 0, 0))
        grad = grad.reshape(RING, FF // PARTS, WIDE)
        gd0[:, index] = grad[:, : FF // PARTS // 2]
        gd1[index] = grad[:, FF // PARTS // 2 :]
    for part, tall in enumerate((gd0, gd1)):
        for piece in range(GROUPS):
            for block in range(4):
                source = tall.at[:, :, pl.ds(16 * block, 16), pl.ds(GROUP * piece, GROUP)]
                window = (
                    slice(None),
                    slice(None),
                    pl.ds(16 * piece, 16),
                    pl.ds(FF + GROUP * block, GROUP),
                )
                sent.append(push(source, keep, send, part, window, out_sems.at[len(sent)]))

    def emit(index, lanes, dgate, dup):
        for part, slot, grad in ((0, gg, dgate), (1, gu, dup)):
            put_square(slot, part, lanes, low(product(n3_ref[...], grad, 0, 0)))
            window = columns(index * CHUNK, CHUNK)
            sent.append(
                push(slot.at[window], keep, send, part, window, out_sems.at[len(sent)])
            )

    stream, dgain = hidden_back(
        finish_weight, emit, c_ref, a3_ref, gains_ref, gate_ref, up_ref, wg, wu, wd
    )
    stream_ref[...] = stream
    dgain_ref[...] = dgain
    for copy in sent:
        copy.wait()


def cross_kernel(
    stream_ref, gains_ref, a2_ref, cq_ref, ck_ref, cv_ref, cp_ref, weight,
    next_ref, dgain_ref, dc_ref, dcq_ref, dck_ref, dcv_ref,
    wcq, wco, sems,
):
    copies = weight_copies(weight, dict(cq=wcq, co=wco), sems)
    begin(copies, ("co", "cq"))

    def finish_weight(name):
        finish(copies, name)

    stream, dgain = cross_back(
        stream_ref[...], finish_weight, gains_ref, a2_ref, cq_ref, ck_ref, cv_ref, cp_ref,
        wcq, wco, dc_ref, dcq_ref, dck_ref, dcv_ref,
    )
    next_ref[...] = stream
    dgain_ref[...] = dgain


def self_kernel(
    stream_ref, x_ref, gains_ref, q_ref, k_ref, v_ref, p_ref,
    enc_ref, n1_ref, o_ref, n2_ref, co_ref, dc_ref, dcq_ref, dck_ref, dcv_ref, weight,
    da_ref, dgain_ref, dscore_ref, denc_ref, keep, send,
    dself_ref, dq_ref, dk_ref, dv_ref,
    wq, wk, wv, wo, wck, wcv, g0, g1, g2, g3, g4, g5, g6, g7, sems, out_sems,
):
    slots = dict(q=wq, k=wk, v=wv, o=wo, ck=wck, cv=wcv)
    copies = weight_copies(weight, slots, sems)
    begin(copies, ("o", "q", "k", "v", "ck", "cv"))

    def finish_weight(name):
        finish(copies, name)

    sent = []

    def emit(slot, part, column, left, right):
        put_square(slot, part, slice(None), low(product(left[...], right[...], 0, 0)))
        window = columns(WIDE * column, WIDE)
        sent.append(push(slot, keep, send, part, window, out_sems.at[len(sent)]))

    emit(g0, 0, 0, co_ref, dc_ref)
    emit(g1, 0, 1, n2_ref, dcq_ref)
    emit(g2, 1, 0, enc_ref, dck_ref)
    emit(g3, 1, 1, enc_ref, dcv_ref)
    stream, dgain = self_back(
        stream_ref[...], finish_weight, gains_ref, x_ref, q_ref, k_ref, v_ref, p_ref,
        wq, wk, wv, wo, dself_ref, dq_ref, dk_ref, dv_ref, dscore_ref,
    )
    da_ref[...] = low(stream)
    dgain_ref[...] = dgain
    emit(g4, 0, 2, o_ref, dself_ref)
    emit(g5, 0, 3, n1_ref, dq_ref)
    emit(g6, 1, 2, n1_ref, dk_ref)
    emit(g7, 1, 3, n1_ref, dv_ref)
    finish(copies, "ck")
    finish(copies, "cv")
    for row in range(BATCHES):
        keys = pl.ds(STATES * row, STATES)
        denc_ref[keys] = low(
            product(dck_ref[keys], square(wck), 1, 1) + product(dcv_ref[keys], square(wcv), 1, 1)
        )
    for copy in sent:
        copy.wait()


def in_vmem(count):
    return [pl.BlockSpec(memory_space=pltpu.VMEM)] * count


def held(*shapes):
    return [pltpu.VMEM(shape, jnp.bfloat16) for shape in shapes]


def shape_of(dims, kind=jnp.bfloat16):
    return jax.ShapeDtypeStruct(dims, kind)


params = pltpu.CompilerParams(vmem_limit_bytes=VMEM_BYTES)


SAVED = (
    (ALL_TOKENS, jnp.bfloat16),
    (ALL_TOKENS, jnp.bfloat16),
    (ALL_TOKENS, jnp.bfloat16),
    (ALL_TOKENS, jnp.bfloat16),
    ((BATCHES, WIDE, TOKENS), jnp.float32),
    (ALL_TOKENS, jnp.bfloat16),
    (ALL_TOKENS, jnp.float32),
    (ALL_TOKENS, jnp.bfloat16),
    (ALL_TOKENS, jnp.bfloat16),
    ((BATCHES, WIDE, STATES), jnp.float32),
    (ALL_TOKENS, jnp.bfloat16),
    (ALL_TOKENS, jnp.float32),
    (ALL_TOKENS, jnp.bfloat16),
    (HIDDEN, jnp.float32),
    (HIDDEN, jnp.float32),
    (HIDDEN, jnp.bfloat16),
)


def run_first(x, enc, self_add, cross_add, gains, weight):
    outs = [shape_of(ALL_TOKENS), shape_of(ALL_STATES), shape_of(ALL_STATES)]
    return pl.pallas_call(
        first_kernel,
        out_shape=outs,
        in_specs=in_vmem(5) + [pl.BlockSpec(memory_space=pl.ANY)],
        out_specs=in_vmem(len(outs)),
        scratch_shapes=[pltpu.VMEM(dims, kind) for dims, kind in SAVED]
        + held(*[FULL] * 8, GATED, GATED, DOWN)
        + [pltpu.SemaphoreType.DMA((40,))],
        compiler_params=params,
        name="first_forward",
    )(x, enc, self_add, cross_add, gains, weight)


def run_second(x, ck, cv, self_add, cross_add, gains, weight):
    outs = [shape_of(ALL_TOKENS)] + [shape_of(dims, kind) for dims, kind in SAVED]
    return pl.pallas_call(
        second_kernel,
        out_shape=outs,
        in_specs=in_vmem(6) + [pl.BlockSpec(memory_space=pl.ANY)],
        out_specs=in_vmem(len(outs)),
        scratch_shapes=held(*[FULL] * 6, GATED, GATED, DOWN) + [pltpu.SemaphoreType.DMA((40,))],
        compiler_params=params,
        name="second_forward",
    )(x, ck, cv, self_add, cross_add, gains, weight)


HALF = (RING, RING, ROWS_OWN, ATT // 2)
RINGED = (RING, RING, ROWS_OWN, WIDE)
RINGED_WIDE = (RING, RING, ROWS_OWN, FF)
RINGED_TALL = (RING, RING, FF // PARTS // 2, WIDE)
ANYWHERE = pl.BlockSpec(memory_space=pl.ANY)
DMAS = pltpu.SemaphoreType.DMA((40,))


def run_chain(cotangent, x, gains, saved, weight):
    (ck, cv, n1, q, k, v, p, o, a2, n2, cq, cp, co, a3, n3, gate, up, hid) = saved
    return pl.pallas_call(
        chain_kernel,
        out_shape=shape_of(ALL_TOKENS),
        in_specs=in_vmem(5) + [ANYWHERE] * 11,
        out_specs=in_vmem(1)[0],
        scratch_shapes=held(*[ALL_TOKENS] * 4)
        + [pltpu.VMEM((BATCHES, WIDE, TOKENS), jnp.float32), pltpu.VMEM(ALL_TOKENS, jnp.float32)]
        + held(ALL_TOKENS, ALL_STATES, ALL_STATES)
        + [pltpu.VMEM((BATCHES, WIDE, STATES), jnp.float32)]
        + held(
            ALL_TOKENS, ALL_TOKENS, ALL_STATES, ALL_STATES, *[ALL_TOKENS] * 4,
            *[FULL] * 6, GATED, GATED, DOWN,
        )
        + [DMAS, DMAS],
        compiler_params=params,
        name="backward_chain",
    )(cotangent, a3, gains, gate, up, x, q, k, v, p, a2, cq, ck, cv, cp, weight)


def run_hidden(cotangent, gains, saved, weight):
    (ck, cv, n1, q, k, v, p, o, a2, n2, cq, cp, co, a3, n3, gate, up, hid) = saved
    return pl.pallas_call(
        hidden_kernel,
        out_shape=[
            shape_of(ALL_TOKENS, jnp.float32),
            shape_of((1, WIDE), jnp.float32),
            shape_of(HALF),
            shape_of(HALF),
        ],
        in_specs=in_vmem(7) + [ANYWHERE],
        out_specs=in_vmem(2) + [ANYWHERE, ANYWHERE],
        scratch_shapes=held(
            GATED, GATED, DOWN, RINGED_WIDE, RINGED_WIDE, RINGED_TALL, RINGED_TALL
        )
        + [DMAS, DMAS],
        compiler_params=params,
        name="hidden_backward",
    )(cotangent, a3, gains, gate, up, n3, hid, weight)


def run_cross(stream, gains, saved, weight):
    (ck, cv, n1, q, k, v, p, o, a2, n2, cq, cp, co, a3, n3, gate, up, hid) = saved
    return pl.pallas_call(
        cross_kernel,
        out_shape=[
            shape_of(ALL_TOKENS, jnp.float32),
            shape_of((1, WIDE), jnp.float32),
            shape_of(ALL_TOKENS),
            shape_of(ALL_TOKENS),
            shape_of(ALL_STATES),
            shape_of(ALL_STATES),
        ],
        in_specs=in_vmem(7) + [ANYWHERE],
        out_specs=in_vmem(6),
        scratch_shapes=held(FULL, FULL) + [DMAS],
        compiler_params=params,
        name="cross_backward",
    )(stream, gains, a2, cq, ck, cv, cp, weight)


def run_self(stream, x, gains, enc, saved, records, weight):
    (ck, cv, n1, q, k, v, p, o, a2, n2, cq, cp, co, a3, n3, gate, up, hid) = saved
    return pl.pallas_call(
        self_kernel,
        out_shape=[
            shape_of(ALL_TOKENS),
            shape_of((1, WIDE), jnp.float32),
            shape_of((WIDE, TOKENS), jnp.float32),
            shape_of(ALL_STATES),
            shape_of(HALF),
            shape_of(HALF),
        ],
        in_specs=in_vmem(16) + [ANYWHERE],
        out_specs=in_vmem(4) + [ANYWHERE, ANYWHERE],
        scratch_shapes=held(*[ALL_TOKENS] * 4, *[FULL] * 6, *[RINGED] * 8) + [DMAS, DMAS],
        compiler_params=params,
        name="self_backward",
    )(stream, x, gains, q, k, v, p, enc, n1, o, n2, co, *records, weight)


def pack_attention(query, kv, out, c_query, c_kv, c_out):
    rows = query.shape[0]
    return jnp.concatenate(
        [query, kv.reshape(rows, -1), out, c_query, c_kv.reshape(rows, -1), c_out], axis=1
    )


def pack_hidden(w_in, w_ffn):
    rows = w_in.shape[0]
    pieces = w_ffn.reshape(8, 16, GROUPS, GROUP).transpose(2, 1, 0, 3)
    return jnp.concatenate([w_in.reshape(rows, -1), pieces.reshape(rows, FF)], axis=1)


def unpack(first, second):
    rows = first.shape[0]
    squares = [
        part[:, ATT // 2 + WIDE * place : ATT // 2 + WIDE * (place + 1)]
        for part in (first, second)
        for place in range(4)
    ]
    c_out, c_query, out, query, c_key, c_value, key, value = squares
    tall = [
        part[:, FF : FF + 1024].reshape(GROUPS, 16, 4, GROUP).transpose(2, 1, 0, 3)
        for part in (first, second)
    ]
    tall = [part.reshape(FF // PARTS // 2, WIDE) for part in tall]
    return (
        query,
        jnp.stack([key, value], axis=1),
        out,
        c_query,
        jnp.stack([c_key, c_value], axis=1),
        c_out,
        jnp.stack([first[:, :FF], second[:, :FF]], axis=1),
        jnp.concatenate(tall, axis=0),
    )


def score_terms(table, dec_ids, enc_ids):
    positions = jnp.arange(TOKENS)
    by_distance = jnp.dot(table.astype(jnp.float32).T, bucket_onehot(TOKENS), precision=highest)
    bias = spread_distance(by_distance)
    allowed = (dec_ids[:, :, None] == dec_ids[:, None, :]) & (
        positions[None, :] <= positions[:, None]
    )
    self_add = jnp.where(allowed[:, None], bias[None], -jnp.inf)
    cross_add = jnp.where(dec_ids[:, :, None] == enc_ids[:, None, :], 0.0, -jnp.inf)
    return self_add.reshape(BATCHES, WIDE, TOKENS), cross_add


def shards(
    layer_in,
    cotangent,
    encoder,
    dec_segments,
    enc_segments,
    norm_gains,
    self_query,
    self_kv,
    self_out,
    rel_bias,
    cross_query,
    cross_kv,
    cross_out,
    ffn_in,
    ffn_out,
):
    core = lax.axis_index("section")
    part_index = lax.axis_index("fsdp")
    plane = lax.axis_index("rep")
    planes = lax.axis_size("rep")
    layer = lax.rem(plane, 2)
    first_core = core == 0
    at_home = core == layer

    def place(core_index, plane_index):
        return core_index * planes + plane_index

    def flip_core(value):
        return lax.ppermute(value, "section", [(0, 1), (1, 0)])

    def from_home(value):
        pairs = [(place(p % 2, p), place(1 - p % 2, p)) for p in range(planes)]
        return jnp.where(at_home, value, lax.ppermute(value, ("section", "rep"), pairs))

    def beside(value):
        return lax.ppermute(value, "rep", [(p, p ^ 1) for p in range(planes)])

    def rows_for_layer(value):
        pairs = [(place(p % 2, p), place(p % 2, p ^ 1)) for p in range(planes)]
        return jnp.where(at_home, value, lax.ppermute(value, ("section", "rep"), pairs))

    def rows_back(value):
        pairs = [(place(1 - p % 2, p), place(p % 2, p ^ 1)) for p in range(planes)]
        return jnp.where(at_home, value, lax.ppermute(value, ("section", "rep"), pairs))

    def between_layers(value, steps):
        pairs = [(p, p + steps) for p in range(planes) if p % 2 == (steps < 0)]
        return lax.ppermute(value, "rep", pairs)

    along_z = [[RING * x + z for z in range(RING)] for x in range(RING)]
    along_x = [[RING * x + z for x in range(RING)] for z in range(RING)]
    first_rings = along_z + [[PARTS + d for d in ring] for ring in along_x]
    second_rings = along_x + [[PARTS + d for d in ring] for ring in along_z]

    def add_halves(keep, received):
        total = low(keep.astype(jnp.float32) + received.astype(jnp.float32))
        return total.reshape(WIDE, ATT // 2)

    def scatter(value, rings):
        return lax.psum_scatter(
            value, ("section", "fsdp"), scatter_dimension=0, axis_index_groups=rings, tiled=True
        )

    attention = pack_attention(
        self_query[0], self_kv[0], self_out[0], cross_query[0], cross_kv[0], cross_out[0]
    )
    hidden = pack_hidden(ffn_in[0], ffn_out[0])
    kept = jnp.where(first_core, attention, hidden)
    given_away = jnp.where(first_core, hidden, attention)
    half = jnp.where(at_home, kept, flip_core(given_away))
    weight = lax.all_gather(half, ("fsdp", "section"), axis=0, tiled=True)
    weight = weight.reshape(PARTS, 2, ROWS_OWN, ATT)
    small = jnp.zeros((8, 128), jnp.bfloat16)
    small = small.at[:3, :ROWS_OWN].set(norm_gains[0])
    small = small.at[3:5, :HEADS].set(rel_bias[0])
    small = lax.all_gather(from_home(small), "fsdp", axis=0, tiled=False)
    gains = small[:, :3, :ROWS_OWN].transpose(1, 0, 2).reshape(3, WIDE).astype(jnp.float32)
    table = small[:, 3:5, :HEADS].reshape(BUCKETS, HEADS)
    ids = jnp.concatenate([dec_segments[:, 0], enc_segments[:, 0]], axis=1)
    ids = rows_for_layer(ids)
    self_add, cross_add = score_terms(table, ids[:, :TOKENS], ids[:, TOKENS:])
    ends = jnp.stack([layer_in[:, 0].reshape(ALL_TOKENS), cotangent[:, 0].reshape(ALL_TOKENS)])
    ends = rows_for_layer(ends)
    rows_in, given = ends[0], ends[1]
    enc = rows_for_layer(encoder[:, 0].reshape(ALL_STATES))
    weight, rows_in, given, enc, self_add, cross_add, gains = lax.optimization_barrier(
        (weight, rows_in, given, enc, self_add, cross_add, gains)
    )
    first, ck, cv = run_first(rows_in, enc, self_add, cross_add, gains, weight)
    current = jnp.where(layer == 0, rows_in, between_layers(first, 1))
    result, *saved = run_second(current, ck, cv, self_add, cross_add, gains, weight)
    saved = [ck, cv] + saved
    grad_first = run_chain(given, current, gains, saved, weight)
    incoming = jnp.where(layer == 1, given, between_layers(grad_first, -1))
    stream, gain_three, keep, send = run_hidden(incoming, gains, saved, weight)
    received = flip_core(send)
    stream, gain_two, *records = run_cross(stream, gains, saved, weight)
    wide_sum = add_halves(keep, received)
    wide_sum, stream = lax.optimization_barrier((wide_sum, stream))
    wide_part = scatter(wide_sum, first_rings)
    grad_input, gain_one, grad_scores, grad_enc, keep, send = run_self(
        stream, current, gains, enc, saved, records, weight
    )
    square_part = scatter(add_halves(keep, flip_core(send)), first_rings)
    grad_gains = jnp.concatenate([gain_one, gain_two, gain_three], axis=0)
    diagonal_sums = gather_distance(grad_scores.reshape(HEADS, TOKENS, TOKENS))
    grad_table = jnp.dot(bucket_onehot(TOKENS), diagonal_sums.T, precision=highest)
    little = jnp.zeros((8, WIDE), jnp.float32)
    little = little.at[:3].set(grad_gains)
    little = little.at[3, : BUCKETS * HEADS].set(grad_table.reshape(-1))
    for axis, bits in (("section", (1,)), ("fsdp", (1, 2, 4, 8)), ("rep", (2,))):
        for bit in bits:
            pairs = [(index, index ^ bit) for index in range(lax.axis_size(axis))]
            little = little + lax.ppermute(little, axis, pairs)
    little = jnp.where(at_home, little, beside(little))
    own_gains = lax.dynamic_slice(little, (0, part_index * ROWS_OWN), (3, ROWS_OWN))
    own_table = lax.dynamic_slice(little, (3, part_index * 2 * HEADS), (1, 2 * HEADS))
    outs = rows_back(jnp.stack([result, grad_input]))
    wide_part, square_part, own_gains, own_table, outs = lax.optimization_barrier(
        (wide_part, square_part, own_gains, own_table, outs)
    )
    partial = scatter(jnp.concatenate([wide_part, square_part], axis=1), second_rings)
    encoder_total = grad_enc.astype(jnp.float32) + beside(grad_enc).astype(jnp.float32)
    encoder_total = from_home(encoder_total)
    own_table = own_table.reshape(2, HEADS)
    results = (
        outs[0].reshape(1, BATCHES, 1, TOKENS, WIDE),
        outs[1].reshape(1, BATCHES, 1, TOKENS, WIDE),
        encoder_total.reshape(BATCHES, 1, STATES, WIDE),
        own_gains[None],
        own_table[None],
    )
    partial, results = lax.optimization_barrier((partial, results))
    up = [(p, (p + 1) % planes) for p in range(planes)]
    down = [(p, (p - 1) % planes) for p in range(planes)]
    above = lax.ppermute(partial, "rep", down).astype(jnp.float32)
    below = lax.ppermute(partial, "rep", up).astype(jnp.float32)
    other_layer = low(above + below)
    cut = ATT // 2
    own_layer = jnp.concatenate(
        [
            lax.ppermute(other_layer[:, :cut], "rep", down),
            lax.ppermute(other_layer[:, cut:], "rep", up),
        ],
        axis=1,
    )
    mine = jnp.where(at_home, own_layer, other_layer)
    theirs = flip_core(jnp.where(at_home, other_layer, own_layer))
    first_part = jnp.where(first_core, mine, theirs).astype(jnp.float32)
    second_part = jnp.where(first_core, theirs, mine).astype(jnp.float32)
    query, kv, out, *others = [member[None] for member in unpack(first_part, second_part)]
    return (*results[:4], query, kv, out, results[4], *others)


def solution(mesh):
    return jax.shard_map(
        shards,
        mesh=mesh,
        in_specs=(
            P(None, ("fsdp", "rep"), None, None),
            P(None, ("fsdp", "rep"), None, None),
            P(None, ("fsdp", "rep"), None, None),
            P(None, ("fsdp", "rep"), None),
            P(None, ("fsdp", "rep"), None),
            P("section", None, "fsdp"),
            P("section", "fsdp", None),
            P("section", "fsdp", None, None),
            P("section", "fsdp", None),
            P("section", "fsdp", None),
            P("section", "fsdp", None),
            P("section", "fsdp", None, None),
            P("section", "fsdp", None),
            P("section", "fsdp", None, None),
            P("section", "fsdp", None),
        ),
        out_specs=(
            P("section", None, ("fsdp", "rep"), None, None),
            P("section", None, ("fsdp", "rep"), None, None),
            P(None, ("fsdp", "rep"), None, None),
            P("section", None, "fsdp"),
            P("section", "fsdp", None),
            P("section", "fsdp", None, None),
            P("section", "fsdp", None),
            P("section", "fsdp", None),
            P("section", "fsdp", None),
            P("section", "fsdp", None, None),
            P("section", "fsdp", None),
            P("section", "fsdp", None, None),
            P("section", "fsdp", None),
        ),
        check_vma=False,
    )
```

```python
import jax
import jax.numpy as jnp
import numpy as np
from jax import lax
from jax.experimental import pallas as pl
from jax.experimental.pallas import tpu as pltpu
from jax.sharding import PartitionSpec as P

HEADS = 12
HEAD = 64
BUCKETS = 32
MAX_DIST = 128
PARTS = 16
GELU_SCALE = float(np.sqrt(2.0 / np.pi))


epsilon = 1e-06
highest = lax.Precision.HIGHEST


def bucket_row(length):
    distance = np.arange(length)
    half_count = BUCKETS // 2
    scaled = (
        np.log(np.maximum(distance, half_count) / half_count)
        / np.log(MAX_DIST / half_count)
        * (BUCKETS - half_count)
    )
    far_bucket = np.minimum(half_count + np.floor(scaled).astype(np.int32), BUCKETS - 1)
    return np.where(distance < half_count, distance, far_bucket).astype(np.int32)


def bucket_onehot(length):
    return (bucket_row(length)[None, :] == np.arange(BUCKETS)[:, None]).astype(np.float32)


def spread_distance(by_distance):
    head_count, length = by_distance.shape
    padded_row = jnp.concatenate(
        [jnp.zeros((head_count, length - 1), jnp.float32), by_distance], axis=1
    )
    tiled = jnp.tile(padded_row, (1, length))
    tiled = jnp.concatenate([tiled, jnp.zeros((head_count, length), jnp.float32)], axis=1)
    return tiled.reshape(head_count, length, 2 * length)[:, :, :length][:, :, ::-1]


def gather_distance(grid):
    head_count, length, _ = grid.shape
    flipped = jnp.concatenate(
        [grid[:, :, ::-1], jnp.zeros((head_count, length, length), jnp.float32)], axis=2
    )
    flat = flipped.reshape(head_count, 2 * length * length)[:, : length * (2 * length - 1)]
    return jnp.sum(flat.reshape(head_count, length, 2 * length - 1), axis=1)[:, length - 1 :]


ROWS_OWN = 48
TOKENS = 64
WIDE = 768
FF = 2048
GROUP = 256
GROUPS = 3
BATCHES = 2
STATES = 256
CHUNK = 512
CHUNKS = FF // CHUNK
ATT = 6144
ALL_TOKENS = (BATCHES * TOKENS, WIDE)
ALL_STATES = (BATCHES * STATES, WIDE)
HIDDEN = (BATCHES * TOKENS, FF)
VMEM_BYTES = 60 * 1024 * 1024
FULL = (PARTS, ROWS_OWN, WIDE)
GATED = (PARTS, ROWS_OWN, FF)
DOWN = (PARTS, FF // PARTS, WIDE)
RING = 4
LATE_HIDDEN = [name + str(index) for index in range(1, CHUNKS) for name in ("gate", "up")]
DOWN_PIECES = [(piece, block) for piece in range(GROUPS) for block in range(8)]


def product(left, right, along_left=1, along_right=0):
    return lax.dot_general(
        left,
        right,
        (((along_left,), (along_right,)), ((), ())),
        preferred_element_type=jnp.float32,
    )


def low(value):
    return value.astype(jnp.bfloat16)


def same_head():
    row = lax.broadcasted_iota(jnp.int32, (GROUP, GROUP), 0) // HEAD
    lane = lax.broadcasted_iota(jnp.int32, (GROUP, GROUP), 1) // HEAD
    return jnp.where(row == lane, 1.0, 0.0)


def spread_heads(block, own_low):
    return jnp.concatenate([block] * 4, axis=0) * own_low


def fold_heads(block, own):
    kept = block * own
    return kept[:64] + kept[64:128] + kept[128:192] + kept[192:]


def scale_of(value):
    return lax.rsqrt(jnp.mean(value * value, axis=-1, keepdims=True) + epsilon)


def norm_back(grad, value, gain):
    scale = scale_of(value)
    carried = grad * gain
    mean = jnp.mean(value * carried, axis=-1, keepdims=True)
    grad_value = carried * scale - value * (scale * scale * scale) * mean
    grad_gain = jnp.sum(grad * value * scale, axis=0, keepdims=True)
    return grad_value, grad_gain


def square(ref):
    return ref[...].reshape(WIDE, WIDE)


def down_at(ref, piece, block):
    return ref.at[:, 1, pl.ds(16 * piece, 16), pl.ds(2 * FF + GROUP * block, GROUP)]


def rows_at(ref, piece, block):
    return ref.at[:, pl.ds(16 * block, 16), pl.ds(GROUP * piece, GROUP)]


def softmax_rows(scores):
    raised = jnp.exp(scores - jnp.max(scores, axis=-1, keepdims=True))
    return raised / jnp.sum(raised, axis=-1, keepdims=True)


def gelu_parts(gate):
    cube = gate * gate * gate
    bent = jnp.tanh(GELU_SCALE * (gate + 0.044715 * cube))
    half = 0.5 * (1.0 + bent)
    slope = half + 0.5 * gate * (1.0 - bent * bent) * GELU_SCALE * (
        1.0 + 3.0 * 0.044715 * gate * gate
    )
    return gate * half, slope


def weight_copies(weight, slots, sems):
    copies = {}
    for place, (name, column) in enumerate(
        (("q", 0), ("k", 1), ("v", 2), ("o", 3), ("cq", 4), ("ck", 5), ("cv", 6), ("co", 7))
    ):
        if name in slots:
            source = weight.at[:, 0, :, pl.ds(WIDE * column, WIDE)]
            copies[name] = [pltpu.make_async_copy(source, slots[name], sems.at[place])]
    for place, (name, column) in enumerate((("gate", 0), ("up", FF))):
        if name in slots:
            for index in range(CHUNKS):
                start = CHUNK * index
                source = weight.at[:, 1, :, pl.ds(column + start, CHUNK)]
                target = slots[name].at[:, :, pl.ds(start, CHUNK)]
                sem = sems.at[8 + CHUNKS * place + index]
                copies[name + str(index)] = [pltpu.make_async_copy(source, target, sem)]
    if "down" in slots:
        copies["down"] = [
            pltpu.make_async_copy(
                down_at(weight, piece, block),
                rows_at(slots["down"], piece, block),
                sems.at[8 + 2 * CHUNKS + place],
            )
            for place, (piece, block) in enumerate(DOWN_PIECES)
        ]
    return copies


def begin(copies, names):
    for name in names:
        for copy in copies[name]:
            copy.start()


def finish(copies, name):
    for copy in copies[name]:
        copy.wait()


def forward_body(
    keys_given,
    x_ref,
    enc_ref,
    self_add_ref,
    cross_add_ref,
    gains_ref,
    weight,
    out_ref,
    n1_ref,
    q_ref,
    k_ref,
    v_ref,
    p_ref,
    o_ref,
    a2_ref,
    n2_ref,
    cq_ref,
    ck_ref,
    cv_ref,
    cp_ref,
    co_ref,
    a3_ref,
    n3_ref,
    gate_ref,
    up_ref,
    hid_ref,
    wq,
    wk,
    wv,
    wo,
    wcq,
    wck,
    wcv,
    wco,
    wg,
    wu,
    wd,
    sems,
):
    slots = dict(q=wq, k=wk, v=wv, o=wo, cq=wcq, co=wco, gate=wg, up=wu, down=wd)
    if not keys_given:
        slots.update(ck=wck, cv=wcv)
    copies = weight_copies(weight, slots, sems)
    if not keys_given:
        begin(copies, ("ck", "cv"))
    begin(copies, ("q", "k", "v", "o", "cq", "co", "gate0", "up0", "down", *LATE_HIDDEN))
    own = same_head()
    own_low = low(own)
    stream = x_ref[...].astype(jnp.float32)
    normed = low(stream * scale_of(stream) * gains_ref[0:1])
    n1_ref[...] = normed
    if not keys_given:
        for name, held_weight, target in (("ck", wck, ck_ref), ("cv", wcv, cv_ref)):
            finish(copies, name)
            for row in range(BATCHES):
                part = pl.ds(STATES * row, STATES)
                target[part] = low(product(enc_ref[part], square(held_weight)))
    finish(copies, "q")
    q_ref[...] = low(product(normed, square(wq)))
    finish(copies, "k")
    k_ref[...] = low(product(normed, square(wk)))
    finish(copies, "v")
    v_ref[...] = low(product(normed, square(wv)))
    for row in range(BATCHES):
        part = pl.ds(TOKENS * row, TOKENS)
        for group in range(GROUPS):
            lanes = pl.ds(GROUP * group, GROUP)
            spread = spread_heads(q_ref[part, lanes], own_low)
            scores = product(spread, k_ref[part, lanes], 1, 1) + self_add_ref[row, lanes]
            chance = softmax_rows(scores)
            p_ref[row, lanes] = chance
            mixed = product(low(chance), v_ref[part, lanes])
            o_ref[part, lanes] = low(fold_heads(mixed, own))
    finish(copies, "o")
    stream = stream + product(o_ref[...], square(wo))
    a2_ref[...] = stream
    normed = low(stream * scale_of(stream) * gains_ref[1:2])
    n2_ref[...] = normed
    finish(copies, "cq")
    cq_ref[...] = low(product(normed, square(wcq)))
    for row in range(BATCHES):
        part = pl.ds(TOKENS * row, TOKENS)
        keys = pl.ds(STATES * row, STATES)
        add = jnp.concatenate([cross_add_ref[row]] * 4, axis=0)
        for group in range(GROUPS):
            lanes = pl.ds(GROUP * group, GROUP)
            spread = spread_heads(cq_ref[part, lanes], own_low)
            scores = product(spread, ck_ref[keys, lanes], 1, 1) + add
            chance = softmax_rows(scores)
            cp_ref[row, lanes] = chance
            mixed = product(low(chance), cv_ref[keys, lanes])
            co_ref[part, lanes] = low(fold_heads(mixed, own))
    finish(copies, "co")
    stream = a2_ref[...] + product(co_ref[...], square(wco))
    a3_ref[...] = stream
    n3_ref[...] = low(stream * scale_of(stream) * gains_ref[2:3])
    total = a3_ref[...]
    for index in range(CHUNKS):
        lanes = pl.ds(index * CHUNK, CHUNK)
        rows = n3_ref[...]
        finish(copies, "gate" + str(index))
        gate = product(rows, wg[:, :, lanes].reshape(WIDE, CHUNK))
        finish(copies, "up" + str(index))
        up = product(rows, wu[:, :, lanes].reshape(WIDE, CHUNK))
        gate_ref[:, lanes] = gate
        up_ref[:, lanes] = up
        bent = 0.5 * (1.0 + jnp.tanh(GELU_SCALE * (gate + 0.044715 * (gate * gate * gate))))
        hidden = low(gate * bent * up)
        hid_ref[:, lanes] = hidden
        if index == 0:
            finish(copies, "down")
        total = total + product(hidden, wd[pl.ds(4 * index, 4)].reshape(CHUNK, WIDE))
    out_ref[...] = low(total)


def first_kernel(
    x_ref, enc_ref, self_add_ref, cross_add_ref, gains_ref, weight, out_ref, ck_ref, cv_ref, *rest
):
    (n1, q, k, v, p, o, a2, n2, cq, cp, co, a3, n3, gate, up, hid, *scratch) = rest
    forward_body(
        False,
        x_ref, enc_ref, self_add_ref, cross_add_ref, gains_ref, weight, out_ref,
        n1, q, k, v, p, o, a2, n2, cq, ck_ref, cv_ref, cp, co, a3, n3, gate, up, hid, *scratch,
    )


def turn_kernel(
    x_ref, ck_ref, cv_ref, self_add_ref, cross_add_ref, gains_ref, c_ref, weight,
    out_ref, da_ref, *rest,
):
    saved_out, saved, rest = rest[:16], rest[16:32], rest[32:]
    dc_ref, dcq_ref, dck_ref, dcv_ref, dself_ref, dq_ref, dk_ref, dv_ref, *rest = rest
    wq, wk, wv, wo, wcq, wco, wg, wu, wd, sems, out_sems = rest
    n1, q, k, v, p, o, a2, n2, cq, cp, co, a3, n3, gate, up, hid = saved
    forward_body(
        True,
        x_ref, None, self_add_ref, cross_add_ref, gains_ref, weight, out_ref,
        n1, q, k, v, p, o, a2, n2, cq, ck_ref, cv_ref, cp, co, a3, n3, gate, up, hid,
        wq, wk, wv, wo, wcq, None, None, wco, wg, wu, wd, sems,
    )
    sent = [
        pltpu.make_async_copy(source, target, out_sems.at[place])
        for place, (source, target) in enumerate(zip(saved, saved_out))
    ]
    for copy in sent:
        copy.start()

    def finish_weight(name):
        return None

    def emit(index, lanes, dgate, dup):
        return None

    stream, _ = hidden_back(finish_weight, emit, c_ref, a3, gains_ref, gate, up, wg, wu, wd)
    stream, _ = cross_back(
        stream, finish_weight, gains_ref, a2, cq, ck_ref, cv_ref, cp, wcq, wco,
        dc_ref, dcq_ref, dck_ref, dcv_ref,
    )
    stream, _ = self_back(
        stream, finish_weight, gains_ref, x_ref, q, k, v, p, wq, wk, wv, wo,
        dself_ref, dq_ref, dk_ref, dv_ref, None,
    )
    da_ref[...] = low(stream)
    for copy in sent:
        copy.wait()


def core_is(part):
    return lax.axis_index("section") == part


def push(source, keep, send, part, window, sem):
    @pl.when(core_is(part))
    def _():
        pltpu.make_async_copy(source, keep.at[window], sem).start()

    @pl.when(jnp.logical_not(core_is(part)))
    def _():
        pltpu.make_async_copy(source, send.at[window], sem).start()

    return pltpu.make_async_copy(source, keep.at[window], sem)


def columns(start, width):
    return (slice(None), slice(None), slice(None), pl.ds(start, width))


def put_square(slot, part, lanes, value):
    value = value.reshape(RING, RING, ROWS_OWN, value.shape[-1])
    if part == 1:
        slot[:, :, :, lanes] = value
    else:
        for place in range(RING):
            slot[:, place, :, lanes] = value[place]


def hidden_back(finish_weight, emit, c_ref, a3_ref, gains_ref, gate_ref, up_ref, wg, wu, wd):
    total = jnp.zeros(ALL_TOKENS, jnp.float32)
    finish_weight("down")
    for index in range(CHUNKS):
        lanes = pl.ds(index * CHUNK, CHUNK)
        grad = product(c_ref[...], wd[pl.ds(4 * index, 4)].reshape(CHUNK, WIDE), 1, 1)
        bent, slope = gelu_parts(gate_ref[:, lanes])
        dgate = low(grad * up_ref[:, lanes] * slope)
        dup = low(grad * bent)
        finish_weight("gate" + str(index))
        total = total + product(dgate, wg[:, :, lanes].reshape(WIDE, CHUNK), 1, 1)
        finish_weight("up" + str(index))
        total = total + product(dup, wu[:, :, lanes].reshape(WIDE, CHUNK), 1, 1)
        emit(index, lanes, dgate, dup)
    back, dgain = norm_back(total, a3_ref[...], gains_ref[2:3])
    return c_ref[...].astype(jnp.float32) + back, dgain


def cross_back(
    stream, finish_weight, gains_ref, a2_ref, cq_ref, ck_ref, cv_ref, cp_ref, wcq, wco,
    dc_ref, dcq_ref, dck_ref, dcv_ref,
):
    own = same_head()
    own_low = low(own)
    dc_ref[...] = low(stream)
    finish_weight("co")
    datt = low(product(dc_ref[...], square(wco), 1, 1))
    for row in range(BATCHES):
        part = pl.ds(TOKENS * row, TOKENS)
        keys = pl.ds(STATES * row, STATES)
        for group in range(GROUPS):
            lanes = pl.ds(GROUP * group, GROUP)
            left = GROUP * group
            dout = spread_heads(
                datt[TOKENS * row : TOKENS * (row + 1), left : left + GROUP], own_low
            )
            spread = spread_heads(cq_ref[part, lanes], own_low)
            chance = cp_ref[row, lanes]
            dchance = product(dout, cv_ref[keys, lanes], 1, 1)
            dcv_ref[keys, lanes] = low(product(low(chance), dout, 0, 0))
            inner = jnp.sum(chance * dchance, axis=-1, keepdims=True)
            dscore = low(chance * (dchance - inner))
            dcq_ref[part, lanes] = low(fold_heads(product(dscore, ck_ref[keys, lanes]), own))
            dck_ref[keys, lanes] = low(product(dscore, spread, 0, 0))
    finish_weight("cq")
    grad = product(dcq_ref[...], square(wcq), 1, 1)
    back, dgain = norm_back(grad, a2_ref[...], gains_ref[1:2])
    return stream + back, dgain


def self_back(
    stream, finish_weight, gains_ref, x_ref, q_ref, k_ref, v_ref, p_ref, wq, wk, wv, wo,
    dself_ref, dq_ref, dk_ref, dv_ref, dscore_ref,
):
    own = same_head()
    own_low = low(own)
    dself_ref[...] = low(stream)
    finish_weight("o")
    datt = low(product(dself_ref[...], square(wo), 1, 1))
    for row in range(BATCHES):
        part = pl.ds(TOKENS * row, TOKENS)
        for group in range(GROUPS):
            lanes = pl.ds(GROUP * group, GROUP)
            left = GROUP * group
            dout = spread_heads(
                datt[TOKENS * row : TOKENS * (row + 1), left : left + GROUP], own_low
            )
            spread = spread_heads(q_ref[part, lanes], own_low)
            chance = p_ref[row, lanes]
            dchance = product(dout, v_ref[part, lanes], 1, 1)
            dv_ref[part, lanes] = low(product(low(chance), dout, 0, 0))
            inner = jnp.sum(chance * dchance, axis=-1, keepdims=True)
            dscore = low(chance * (dchance - inner))
            if dscore_ref is not None:
                if row == 0:
                    dscore_ref[lanes] = dscore.astype(jnp.float32)
                else:
                    dscore_ref[lanes] += dscore.astype(jnp.float32)
            dq_ref[part, lanes] = low(fold_heads(product(dscore, k_ref[part, lanes]), own))
            dk_ref[part, lanes] = low(product(dscore, spread, 0, 0))
    finish_weight("q")
    grad = product(dq_ref[...], square(wq), 1, 1)
    finish_weight("k")
    grad = grad + product(dk_ref[...], square(wk), 1, 1)
    finish_weight("v")
    grad = grad + product(dv_ref[...], square(wv), 1, 1)
    back, dgain = norm_back(grad, x_ref[...].astype(jnp.float32), gains_ref[0:1])
    return stream + back, dgain


def hidden_kernel(
    c_ref, a3_ref, gains_ref, gate_ref, up_ref, n3_ref, hid_ref, weight,
    stream_ref, dgain_ref, keep, send,
    wg, wu, wd, gg, gu, gd0, gd1, sems, out_sems,
):
    copies = weight_copies(weight, dict(gate=wg, up=wu, down=wd), sems)
    begin(copies, ("down", "gate0", "up0", *LATE_HIDDEN))
    sent = []

    def finish_weight(name):
        finish(copies, name)

    for index in range(RING):
        lanes = pl.ds(index * CHUNK, CHUNK)
        grad = low(product(hid_ref[:, lanes], c_ref[...], 0, 0))
        grad = grad.reshape(RING, FF // PARTS, WIDE)
        gd0[:, index] = grad[:, : FF // PARTS // 2]
        gd1[index] = grad[:, FF // PARTS // 2 :]
    for part, tall in enumerate((gd0, gd1)):
        for piece in range(GROUPS):
            for block in range(4):
                source = tall.at[:, :, pl.ds(16 * block, 16), pl.ds(GROUP * piece, GROUP)]
                window = (
                    slice(None),
                    slice(None),
                    pl.ds(16 * piece, 16),
                    pl.ds(FF + GROUP * block, GROUP),
                )
                sent.append(push(source, keep, send, part, window, out_sems.at[len(sent)]))

    def emit(index, lanes, dgate, dup):
        for part, slot, grad in ((0, gg, dgate), (1, gu, dup)):
            put_square(slot, part, lanes, low(product(n3_ref[...], grad, 0, 0)))
            window = columns(index * CHUNK, CHUNK)
            sent.append(
                push(slot.at[window], keep, send, part, window, out_sems.at[len(sent)])
            )

    stream, dgain = hidden_back(
        finish_weight, emit, c_ref, a3_ref, gains_ref, gate_ref, up_ref, wg, wu, wd
    )
    stream_ref[...] = stream
    dgain_ref[...] = dgain
    for copy in sent:
        copy.wait()


def cross_kernel(
    stream_ref, gains_ref, a2_ref, cq_ref, ck_ref, cv_ref, cp_ref, weight,
    next_ref, dgain_ref, dc_ref, dcq_ref, dck_ref, dcv_ref,
    wcq, wco, sems,
):
    copies = weight_copies(weight, dict(cq=wcq, co=wco), sems)
    begin(copies, ("co", "cq"))

    def finish_weight(name):
        finish(copies, name)

    stream, dgain = cross_back(
        stream_ref[...], finish_weight, gains_ref, a2_ref, cq_ref, ck_ref, cv_ref, cp_ref,
        wcq, wco, dc_ref, dcq_ref, dck_ref, dcv_ref,
    )
    next_ref[...] = stream
    dgain_ref[...] = dgain


def self_kernel(
    stream_ref, x_ref, gains_ref, q_ref, k_ref, v_ref, p_ref,
    enc_ref, n1_ref, o_ref, n2_ref, co_ref, dc_ref, dcq_ref, dck_ref, dcv_ref, weight,
    da_ref, dgain_ref, dscore_ref, denc_ref, keep, send,
    dself_ref, dq_ref, dk_ref, dv_ref,
    wq, wk, wv, wo, wck, wcv, g0, g1, g2, g3, g4, g5, g6, g7, sems, out_sems,
):
    slots = dict(q=wq, k=wk, v=wv, o=wo, ck=wck, cv=wcv)
    copies = weight_copies(weight, slots, sems)
    begin(copies, ("o", "q", "k", "v", "ck", "cv"))

    def finish_weight(name):
        finish(copies, name)

    sent = []

    def emit(slot, part, column, left, right):
        put_square(slot, part, slice(None), low(product(left[...], right[...], 0, 0)))
        window = columns(WIDE * column, WIDE)
        sent.append(push(slot, keep, send, part, window, out_sems.at[len(sent)]))

    emit(g0, 0, 0, co_ref, dc_ref)
    emit(g1, 0, 1, n2_ref, dcq_ref)
    emit(g2, 1, 0, enc_ref, dck_ref)
    emit(g3, 1, 1, enc_ref, dcv_ref)
    stream, dgain = self_back(
        stream_ref[...], finish_weight, gains_ref, x_ref, q_ref, k_ref, v_ref, p_ref,
        wq, wk, wv, wo, dself_ref, dq_ref, dk_ref, dv_ref, dscore_ref,
    )
    da_ref[...] = low(stream)
    dgain_ref[...] = dgain
    emit(g4, 0, 2, o_ref, dself_ref)
    emit(g5, 0, 3, n1_ref, dq_ref)
    emit(g6, 1, 2, n1_ref, dk_ref)
    emit(g7, 1, 3, n1_ref, dv_ref)
    finish(copies, "ck")
    finish(copies, "cv")
    for row in range(BATCHES):
        keys = pl.ds(STATES * row, STATES)
        denc_ref[keys] = low(
            product(dck_ref[keys], square(wck), 1, 1) + product(dcv_ref[keys], square(wcv), 1, 1)
        )
    for copy in sent:
        copy.wait()


def in_vmem(count):
    return [pl.BlockSpec(memory_space=pltpu.VMEM)] * count


def held(*shapes):
    return [pltpu.VMEM(shape, jnp.bfloat16) for shape in shapes]


def shape_of(dims, kind=jnp.bfloat16):
    return jax.ShapeDtypeStruct(dims, kind)


params = pltpu.CompilerParams(vmem_limit_bytes=VMEM_BYTES)


ANYWHERE = pl.BlockSpec(memory_space=pl.ANY)
DMAS = pltpu.SemaphoreType.DMA((40,))
SAVED = (
    (ALL_TOKENS, jnp.bfloat16),
    (ALL_TOKENS, jnp.bfloat16),
    (ALL_TOKENS, jnp.bfloat16),
    (ALL_TOKENS, jnp.bfloat16),
    ((BATCHES, WIDE, TOKENS), jnp.float32),
    (ALL_TOKENS, jnp.bfloat16),
    (ALL_TOKENS, jnp.float32),
    (ALL_TOKENS, jnp.bfloat16),
    (ALL_TOKENS, jnp.bfloat16),
    ((BATCHES, WIDE, STATES), jnp.float32),
    (ALL_TOKENS, jnp.bfloat16),
    (ALL_TOKENS, jnp.float32),
    (ALL_TOKENS, jnp.bfloat16),
    (HIDDEN, jnp.float32),
    (HIDDEN, jnp.float32),
    (HIDDEN, jnp.bfloat16),
)


def run_first(x, enc, self_add, cross_add, gains, weight):
    outs = [shape_of(ALL_TOKENS), shape_of(ALL_STATES), shape_of(ALL_STATES)]
    return pl.pallas_call(
        first_kernel,
        out_shape=outs,
        in_specs=in_vmem(5) + [pl.BlockSpec(memory_space=pl.ANY)],
        out_specs=in_vmem(len(outs)),
        scratch_shapes=[pltpu.VMEM(dims, kind) for dims, kind in SAVED]
        + held(*[FULL] * 8, GATED, GATED, DOWN)
        + [pltpu.SemaphoreType.DMA((40,))],
        compiler_params=params,
        name="first_forward",
    )(x, enc, self_add, cross_add, gains, weight)


def run_turn(x, ck, cv, self_add, cross_add, gains, cotangent, weight):
    saved = [shape_of(dims, kind) for dims, kind in SAVED]
    return pl.pallas_call(
        turn_kernel,
        out_shape=[shape_of(ALL_TOKENS)] * 2 + saved,
        in_specs=in_vmem(7) + [ANYWHERE],
        out_specs=in_vmem(2) + [ANYWHERE] * len(saved),
        scratch_shapes=[pltpu.VMEM(dims, kind) for dims, kind in SAVED]
        + held(ALL_TOKENS, ALL_TOKENS, ALL_STATES, ALL_STATES, *[ALL_TOKENS] * 4)
        + held(*[FULL] * 6, GATED, GATED, DOWN)
        + [DMAS, DMAS],
        compiler_params=params,
        name="forward_and_back",
    )(x, ck, cv, self_add, cross_add, gains, cotangent, weight)


HALF = (RING, RING, ROWS_OWN, ATT // 2)
RINGED = (RING, RING, ROWS_OWN, WIDE)
RINGED_WIDE = (RING, RING, ROWS_OWN, FF)
RINGED_TALL = (RING, RING, FF // PARTS // 2, WIDE)


def run_hidden(cotangent, gains, saved, weight):
    (ck, cv, n1, q, k, v, p, o, a2, n2, cq, cp, co, a3, n3, gate, up, hid) = saved
    return pl.pallas_call(
        hidden_kernel,
        out_shape=[
            shape_of(ALL_TOKENS, jnp.float32),
            shape_of((1, WIDE), jnp.float32),
            shape_of(HALF),
            shape_of(HALF),
        ],
        in_specs=in_vmem(7) + [ANYWHERE],
        out_specs=in_vmem(2) + [ANYWHERE, ANYWHERE],
        scratch_shapes=held(
            GATED, GATED, DOWN, RINGED_WIDE, RINGED_WIDE, RINGED_TALL, RINGED_TALL
        )
        + [DMAS, DMAS],
        compiler_params=params,
        name="hidden_backward",
    )(cotangent, a3, gains, gate, up, n3, hid, weight)


def run_cross(stream, gains, saved, weight):
    (ck, cv, n1, q, k, v, p, o, a2, n2, cq, cp, co, a3, n3, gate, up, hid) = saved
    return pl.pallas_call(
        cross_kernel,
        out_shape=[
            shape_of(ALL_TOKENS, jnp.float32),
            shape_of((1, WIDE), jnp.float32),
            shape_of(ALL_TOKENS),
            shape_of(ALL_TOKENS),
            shape_of(ALL_STATES),
            shape_of(ALL_STATES),
        ],
        in_specs=in_vmem(7) + [ANYWHERE],
        out_specs=in_vmem(6),
        scratch_shapes=held(FULL, FULL) + [DMAS],
        compiler_params=params,
        name="cross_backward",
    )(stream, gains, a2, cq, ck, cv, cp, weight)


def run_self(stream, x, gains, enc, saved, records, weight):
    (ck, cv, n1, q, k, v, p, o, a2, n2, cq, cp, co, a3, n3, gate, up, hid) = saved
    return pl.pallas_call(
        self_kernel,
        out_shape=[
            shape_of(ALL_TOKENS),
            shape_of((1, WIDE), jnp.float32),
            shape_of((WIDE, TOKENS), jnp.float32),
            shape_of(ALL_STATES),
            shape_of(HALF),
            shape_of(HALF),
        ],
        in_specs=in_vmem(16) + [ANYWHERE],
        out_specs=in_vmem(4) + [ANYWHERE, ANYWHERE],
        scratch_shapes=held(*[ALL_TOKENS] * 4, *[FULL] * 6, *[RINGED] * 8) + [DMAS, DMAS],
        compiler_params=params,
        name="self_backward",
    )(stream, x, gains, q, k, v, p, enc, n1, o, n2, co, *records, weight)


def pack_kernel(
    query_ref, kv_ref, out_ref, c_query_ref, c_kv_ref, c_out_ref, in_ref, ffn_ref, kept, given
):
    def attention(target):
        start = 0
        for ref in (query_ref, kv_ref, out_ref, c_query_ref, c_kv_ref, c_out_ref):
            if len(ref.shape) == 3:
                pair = ref[...].astype(jnp.float32)
                members = [low(pair[:, 0, :]), low(pair[:, 1, :])]
            else:
                members = [ref[...]]
            for member in members:
                target[:, start : start + WIDE] = member
                start += WIDE

    def hidden(target):
        pair = in_ref[...].astype(jnp.float32)
        target[:, :FF] = low(pair[:, 0, :])
        target[:, FF : 2 * FF] = low(pair[:, 1, :])
        for piece, block in DOWN_PIECES:
            lanes = pl.ds(2 * FF + GROUP * block, GROUP)
            target[pl.ds(16 * piece, 16), lanes] = ffn_ref[
                pl.ds(16 * block, 16), pl.ds(GROUP * piece, GROUP)
            ]

    @pl.when(core_is(0))
    def _():
        attention(kept)
        hidden(given)

    @pl.when(core_is(1))
    def _():
        hidden(kept)
        attention(given)


def run_pack(members):
    return pl.pallas_call(
        pack_kernel,
        out_shape=[shape_of((ROWS_OWN, ATT))] * 2,
        in_specs=in_vmem(8),
        out_specs=in_vmem(2),
        compiler_params=params,
        name="pack_weights",
    )(*members)


def add_kernel(left, right, total):
    total[...] = low(left[...].astype(jnp.float32) + right[...].astype(jnp.float32))


def add_halves(keep, received):
    dims = (WIDE, ATT // 2)
    spec = pl.BlockSpec((128, ATT // 2), lambda place: (place, 0))
    return pl.pallas_call(
        add_kernel,
        out_shape=shape_of(dims),
        grid=(6,),
        in_specs=[spec, spec],
        out_specs=spec,
        compiler_params=params,
        name="add_halves",
    )(keep.reshape(dims), received.reshape(dims))


def unpack_kernel(
    mine, theirs, query_ref, kv_ref, out_ref, c_query_ref, c_kv_ref, c_out_ref, in_ref, ffn_ref
):
    def write(first, second):
        def square_at(part, place):
            start = ATT // 2 + WIDE * place
            return part[:, start : start + WIDE].astype(jnp.float32)

        c_out_ref[...] = square_at(first, 0)
        c_query_ref[...] = square_at(first, 1)
        out_ref[...] = square_at(first, 2)
        query_ref[...] = square_at(first, 3)
        c_kv_ref[:, 0, :] = square_at(second, 0)
        c_kv_ref[:, 1, :] = square_at(second, 1)
        kv_ref[:, 0, :] = square_at(second, 2)
        kv_ref[:, 1, :] = square_at(second, 3)
        for index, part in enumerate((first, second)):
            in_ref[:, index, :] = part[:, :FF].astype(jnp.float32)
            for piece in range(GROUPS):
                for block in range(4):
                    rows = pl.ds(64 * index + 16 * block, 16)
                    taken = part[pl.ds(16 * piece, 16), pl.ds(FF + GROUP * block, GROUP)]
                    ffn_ref[rows, pl.ds(GROUP * piece, GROUP)] = taken.astype(jnp.float32)

    @pl.when(core_is(0))
    def _():
        write(mine, theirs)

    @pl.when(core_is(1))
    def _():
        write(theirs, mine)


def run_unpack(mine, theirs):
    wide = jnp.float32
    square_dims, pair_dims = (ROWS_OWN, WIDE), (ROWS_OWN, 2, WIDE)
    outs = [square_dims, pair_dims, square_dims, square_dims, pair_dims, square_dims]
    outs += [(ROWS_OWN, 2, FF), (FF // PARTS, WIDE)]
    return pl.pallas_call(
        unpack_kernel,
        out_shape=[shape_of(dims, wide) for dims in outs],
        in_specs=in_vmem(2),
        out_specs=in_vmem(8),
        compiler_params=params,
        name="unpack_gradients",
    )(mine, theirs)


def score_terms(table, dec_ids, enc_ids):
    positions = jnp.arange(TOKENS)
    by_distance = jnp.dot(table.astype(jnp.float32).T, bucket_onehot(TOKENS), precision=highest)
    bias = spread_distance(by_distance)
    allowed = (dec_ids[:, :, None] == dec_ids[:, None, :]) & (
        positions[None, :] <= positions[:, None]
    )
    self_add = jnp.where(allowed[:, None], bias[None], -jnp.inf)
    cross_add = jnp.where(dec_ids[:, :, None] == enc_ids[:, None, :], 0.0, -jnp.inf)
    return self_add.reshape(BATCHES, WIDE, TOKENS), cross_add


def shards(
    layer_in,
    cotangent,
    encoder,
    dec_segments,
    enc_segments,
    norm_gains,
    self_query,
    self_kv,
    self_out,
    rel_bias,
    cross_query,
    cross_kv,
    cross_out,
    ffn_in,
    ffn_out,
):
    core = lax.axis_index("section")
    part_index = lax.axis_index("fsdp")
    plane = lax.axis_index("rep")
    planes = lax.axis_size("rep")
    layer = lax.rem(plane, 2)
    first_core = core == 0
    at_home = core == layer

    def place(core_index, plane_index):
        return core_index * planes + plane_index

    def flip_core(value):
        return lax.ppermute(value, "section", [(0, 1), (1, 0)])

    def from_home(value):
        pairs = [(place(p % 2, p), place(1 - p % 2, p)) for p in range(planes)]
        return jnp.where(at_home, value, lax.ppermute(value, ("section", "rep"), pairs))

    def beside(value):
        return lax.ppermute(value, "rep", [(p, p ^ 1) for p in range(planes)])

    def rows_for_layer(value):
        pairs = [(place(p % 2, p), place(p % 2, p ^ 1)) for p in range(planes)]
        return jnp.where(at_home, value, lax.ppermute(value, ("section", "rep"), pairs))

    def rows_back(value):
        pairs = [(place(1 - p % 2, p), place(p % 2, p ^ 1)) for p in range(planes)]
        return jnp.where(at_home, value, lax.ppermute(value, ("section", "rep"), pairs))

    def between_layers(value, steps):
        pairs = [(p, p + steps) for p in range(planes) if p % 2 == (steps < 0)]
        return lax.ppermute(value, "rep", pairs)

    along_z = [[RING * x + z for z in range(RING)] for x in range(RING)]
    along_x = [[RING * x + z for x in range(RING)] for z in range(RING)]
    first_rings = along_z + [[PARTS + d for d in ring] for ring in along_x]
    second_rings = along_x + [[PARTS + d for d in ring] for ring in along_z]

    def scatter(value, rings):
        return lax.psum_scatter(
            value, ("section", "fsdp"), scatter_dimension=0, axis_index_groups=rings, tiled=True
        )

    kept, given_away = run_pack(
        [
            member[0]
            for member in (
                self_query,
                self_kv,
                self_out,
                cross_query,
                cross_kv,
                cross_out,
                ffn_in,
                ffn_out,
            )
        ]
    )
    half = jnp.where(at_home, kept, flip_core(given_away))
    weight = lax.all_gather(half, ("fsdp", "section"), axis=0, tiled=True)
    weight = weight.reshape(PARTS, 2, ROWS_OWN, ATT)
    small = jnp.zeros((8, 128), jnp.bfloat16)
    small = small.at[:3, :ROWS_OWN].set(norm_gains[0])
    small = small.at[3:5, :HEADS].set(rel_bias[0])
    small = lax.all_gather(from_home(small), "fsdp", axis=0, tiled=False)
    gains = small[:, :3, :ROWS_OWN].transpose(1, 0, 2).reshape(3, WIDE).astype(jnp.float32)
    table = small[:, 3:5, :HEADS].reshape(BUCKETS, HEADS)
    ids = jnp.concatenate([dec_segments[:, 0], enc_segments[:, 0]], axis=1)
    ids = rows_for_layer(ids)
    self_add, cross_add = score_terms(table, ids[:, :TOKENS], ids[:, TOKENS:])
    ends = jnp.stack([layer_in[:, 0].reshape(ALL_TOKENS), cotangent[:, 0].reshape(ALL_TOKENS)])
    ends = rows_for_layer(ends)
    rows_in, given = ends[0], ends[1]
    enc = rows_for_layer(encoder[:, 0].reshape(ALL_STATES))
    weight, rows_in, given, enc, self_add, cross_add, gains = lax.optimization_barrier(
        (weight, rows_in, given, enc, self_add, cross_add, gains)
    )
    first, ck, cv = run_first(rows_in, enc, self_add, cross_add, gains, weight)
    current = jnp.where(layer == 0, rows_in, between_layers(first, 1))
    result, grad_first, *saved = run_turn(
        current, ck, cv, self_add, cross_add, gains, given, weight
    )
    saved = [ck, cv] + saved
    incoming = jnp.where(layer == 1, given, between_layers(grad_first, -1))
    stream, gain_three, keep, send = run_hidden(incoming, gains, saved, weight)
    received = flip_core(send)
    stream, gain_two, *records = run_cross(stream, gains, saved, weight)
    wide_sum = add_halves(keep, received)
    wide_sum, stream = lax.optimization_barrier((wide_sum, stream))
    wide_part = scatter(wide_sum, first_rings)
    grad_input, gain_one, grad_scores, grad_enc, keep, send = run_self(
        stream, current, gains, enc, saved, records, weight
    )
    square_part = scatter(add_halves(keep, flip_core(send)), first_rings)
    grad_gains = jnp.concatenate([gain_one, gain_two, gain_three], axis=0)
    diagonal_sums = gather_distance(grad_scores.reshape(HEADS, TOKENS, TOKENS))
    grad_table = jnp.dot(bucket_onehot(TOKENS), diagonal_sums.T, precision=highest)
    little = jnp.zeros((8, WIDE), jnp.float32)
    little = little.at[:3].set(grad_gains)
    little = little.at[3, : BUCKETS * HEADS].set(grad_table.reshape(-1))
    for axis, bits in (("section", (1,)), ("fsdp", (1, 2, 4, 8)), ("rep", (2,))):
        for bit in bits:
            pairs = [(index, index ^ bit) for index in range(lax.axis_size(axis))]
            little = little + lax.ppermute(little, axis, pairs)
    little = jnp.where(at_home, little, beside(little))
    own_gains = lax.dynamic_slice(little, (0, part_index * ROWS_OWN), (3, ROWS_OWN))
    own_table = lax.dynamic_slice(little, (3, part_index * 2 * HEADS), (1, 2 * HEADS))
    outs = rows_back(jnp.stack([result, grad_input]))
    other_enc = beside(grad_enc)
    wide_part, square_part, own_gains, own_table, outs, other_enc = lax.optimization_barrier(
        (wide_part, square_part, own_gains, own_table, outs, other_enc)
    )
    partial = scatter(jnp.concatenate([wide_part, square_part], axis=1), second_rings)
    encoder_total = grad_enc.astype(jnp.float32) + other_enc.astype(jnp.float32)
    encoder_total = from_home(encoder_total)
    own_table = own_table.reshape(2, HEADS)
    results = (
        outs[0].reshape(1, BATCHES, 1, TOKENS, WIDE),
        outs[1].reshape(1, BATCHES, 1, TOKENS, WIDE),
        encoder_total.reshape(BATCHES, 1, STATES, WIDE),
        own_gains[None],
        own_table[None],
    )
    partial, results = lax.optimization_barrier((partial, results))
    up = [(p, (p + 1) % planes) for p in range(planes)]
    down = [(p, (p - 1) % planes) for p in range(planes)]
    across = [(p, (p + 2) % planes) for p in range(planes)]
    cut = ATT // 2
    outer = (plane == 0) | (plane == planes - 1)
    lower = plane < 2
    rising = lax.ppermute(jnp.where(outer, partial[:, :cut], partial[:, cut:]), "rep", up)
    falling = lax.ppermute(jnp.where(outer, partial[:, cut:], partial[:, :cut]), "rep", down)
    here = low(rising.astype(jnp.float32) + falling.astype(jnp.float32))
    below = lax.ppermute(here, "rep", up)
    above = lax.ppermute(here, "rep", down)
    beyond = lax.ppermute(here, "rep", across)
    own_layer = (jnp.where(outer, above, below), jnp.where(outer, below, above))
    other_layer = (jnp.where(lower, here, beyond), jnp.where(lower, beyond, here))
    pairs = list(zip(own_layer, other_layer))
    mine = jnp.concatenate([jnp.where(at_home, own, other) for own, other in pairs], axis=1)
    away = jnp.concatenate([jnp.where(at_home, other, own) for own, other in pairs], axis=1)
    query, kv, out, *others = [member[None] for member in run_unpack(mine, flip_core(away))]
    return (*results[:4], query, kv, out, results[4], *others)


def solution(mesh):
    return jax.shard_map(
        shards,
        mesh=mesh,
        in_specs=(
            P(None, ("fsdp", "rep"), None, None),
            P(None, ("fsdp", "rep"), None, None),
            P(None, ("fsdp", "rep"), None, None),
            P(None, ("fsdp", "rep"), None),
            P(None, ("fsdp", "rep"), None),
            P("section", None, "fsdp"),
            P("section", "fsdp", None),
            P("section", "fsdp", None, None),
            P("section", "fsdp", None),
            P("section", "fsdp", None),
            P("section", "fsdp", None),
            P("section", "fsdp", None, None),
            P("section", "fsdp", None),
            P("section", "fsdp", None, None),
            P("section", "fsdp", None),
        ),
        out_specs=(
            P("section", None, ("fsdp", "rep"), None, None),
            P("section", None, ("fsdp", "rep"), None, None),
            P(None, ("fsdp", "rep"), None, None),
            P("section", None, "fsdp"),
            P("section", "fsdp", None),
            P("section", "fsdp", None, None),
            P("section", "fsdp", None),
            P("section", "fsdp", None),
            P("section", "fsdp", None),
            P("section", "fsdp", None, None),
            P("section", "fsdp", None),
            P("section", "fsdp", None, None),
            P("section", "fsdp", None),
        ),
        check_vma=False,
    )
```

```python
import jax
import jax.numpy as jnp
import numpy as np
from jax import lax
from jax.experimental import pallas as pl
from jax.experimental.pallas import tpu as pltpu
from jax.sharding import PartitionSpec as P

HEADS = 12
HEAD = 64
BUCKETS = 32
MAX_DIST = 128
PARTS = 16
GELU_SCALE = float(np.sqrt(2.0 / np.pi))


epsilon = 1e-06
highest = lax.Precision.HIGHEST


def bucket_row(length):
    distance = np.arange(length)
    half_count = BUCKETS // 2
    scaled = (
        np.log(np.maximum(distance, half_count) / half_count)
        / np.log(MAX_DIST / half_count)
        * (BUCKETS - half_count)
    )
    far_bucket = np.minimum(half_count + np.floor(scaled).astype(np.int32), BUCKETS - 1)
    return np.where(distance < half_count, distance, far_bucket).astype(np.int32)


def bucket_onehot(length):
    return (bucket_row(length)[None, :] == np.arange(BUCKETS)[:, None]).astype(np.float32)


def spread_distance(by_distance):
    head_count, length = by_distance.shape
    padded_row = jnp.concatenate(
        [jnp.zeros((head_count, length - 1), jnp.float32), by_distance], axis=1
    )
    tiled = jnp.tile(padded_row, (1, length))
    tiled = jnp.concatenate([tiled, jnp.zeros((head_count, length), jnp.float32)], axis=1)
    return tiled.reshape(head_count, length, 2 * length)[:, :, :length][:, :, ::-1]


def gather_distance(grid):
    head_count, length, _ = grid.shape
    flipped = jnp.concatenate(
        [grid[:, :, ::-1], jnp.zeros((head_count, length, length), jnp.float32)], axis=2
    )
    flat = flipped.reshape(head_count, 2 * length * length)[:, : length * (2 * length - 1)]
    return jnp.sum(flat.reshape(head_count, length, 2 * length - 1), axis=1)[:, length - 1 :]


ROWS_OWN = 48
TOKENS = 64
WIDE = 768
FF = 2048
GROUP = 256
GROUPS = 3
BATCHES = 2
STATES = 256
CHUNK = 512
CHUNKS = FF // CHUNK
ATT = 6144
ALL_TOKENS = (BATCHES * TOKENS, WIDE)
ALL_STATES = (BATCHES * STATES, WIDE)
HIDDEN = (BATCHES * TOKENS, FF)
VMEM_BYTES = 60 * 1024 * 1024
FULL = (PARTS, ROWS_OWN, WIDE)
GATED = (PARTS, ROWS_OWN, FF)
DOWN = (PARTS, FF // PARTS, WIDE)
RING = 4
LATE_HIDDEN = [name + str(index) for index in range(1, CHUNKS) for name in ("gate", "up")]
DOWN_PIECES = [(piece, block) for piece in range(GROUPS) for block in range(8)]


def product(left, right, along_left=1, along_right=0):
    return lax.dot_general(
        left,
        right,
        (((along_left,), (along_right,)), ((), ())),
        preferred_element_type=jnp.float32,
    )


def low(value):
    return value.astype(jnp.bfloat16)


def same_head():
    row = lax.broadcasted_iota(jnp.int32, (GROUP, GROUP), 0) // HEAD
    lane = lax.broadcasted_iota(jnp.int32, (GROUP, GROUP), 1) // HEAD
    return jnp.where(row == lane, 1.0, 0.0)


def spread_heads(block, own_low):
    return jnp.concatenate([block] * 4, axis=0) * own_low


def fold_heads(block, own):
    kept = block * own
    return kept[:64] + kept[64:128] + kept[128:192] + kept[192:]


def scale_of(value):
    return lax.rsqrt(jnp.mean(value * value, axis=-1, keepdims=True) + epsilon)


def norm_back(grad, value, gain):
    scale = scale_of(value)
    carried = grad * gain
    mean = jnp.mean(value * carried, axis=-1, keepdims=True)
    grad_value = carried * scale - value * (scale * scale * scale) * mean
    grad_gain = jnp.sum(grad * value * scale, axis=0, keepdims=True)
    return grad_value, grad_gain


def square(ref):
    return ref[...].reshape(WIDE, WIDE)


def down_at(ref, piece, block):
    return ref.at[:, 1, pl.ds(16 * piece, 16), pl.ds(2 * FF + GROUP * block, GROUP)]


def rows_at(ref, piece, block):
    return ref.at[:, pl.ds(16 * block, 16), pl.ds(GROUP * piece, GROUP)]


def softmax_rows(scores):
    raised = jnp.exp(scores - jnp.max(scores, axis=-1, keepdims=True))
    return raised / jnp.sum(raised, axis=-1, keepdims=True)


def gelu_parts(gate):
    cube = gate * gate * gate
    bent = jnp.tanh(GELU_SCALE * (gate + 0.044715 * cube))
    half = 0.5 * (1.0 + bent)
    slope = half + 0.5 * gate * (1.0 - bent * bent) * GELU_SCALE * (
        1.0 + 3.0 * 0.044715 * gate * gate
    )
    return gate * half, slope


def weight_copies(weight, slots, sems):
    copies = {}
    for place, (name, column) in enumerate(
        (("q", 0), ("k", 1), ("v", 2), ("o", 3), ("cq", 4), ("ck", 5), ("cv", 6), ("co", 7))
    ):
        if name in slots:
            source = weight.at[:, 0, :, pl.ds(WIDE * column, WIDE)]
            copies[name] = [pltpu.make_async_copy(source, slots[name], sems.at[place])]
    for place, (name, column) in enumerate((("gate", 0), ("up", FF))):
        if name in slots:
            for index in range(CHUNKS):
                start = CHUNK * index
                source = weight.at[:, 1, :, pl.ds(column + start, CHUNK)]
                target = slots[name].at[:, :, pl.ds(start, CHUNK)]
                sem = sems.at[8 + CHUNKS * place + index]
                copies[name + str(index)] = [pltpu.make_async_copy(source, target, sem)]
    if "down" in slots:
        copies["down"] = [
            pltpu.make_async_copy(
                down_at(weight, piece, block),
                rows_at(slots["down"], piece, block),
                sems.at[8 + 2 * CHUNKS + place],
            )
            for place, (piece, block) in enumerate(DOWN_PIECES)
        ]
    return copies


def begin(copies, names):
    for name in names:
        for copy in copies[name]:
            copy.start()


def finish(copies, name):
    for copy in copies[name]:
        copy.wait()


def forward_body(
    keys_given,
    x_ref,
    enc_ref,
    self_add_ref,
    cross_add_ref,
    gains_ref,
    weight,
    out_ref,
    n1_ref,
    q_ref,
    k_ref,
    v_ref,
    p_ref,
    o_ref,
    a2_ref,
    n2_ref,
    cq_ref,
    ck_ref,
    cv_ref,
    cp_ref,
    co_ref,
    a3_ref,
    n3_ref,
    gate_ref,
    up_ref,
    hid_ref,
    wq,
    wk,
    wv,
    wo,
    wcq,
    wck,
    wcv,
    wco,
    wg,
    wu,
    wd,
    sems,
):
    slots = dict(q=wq, k=wk, v=wv, o=wo, cq=wcq, co=wco, gate=wg, up=wu, down=wd)
    if not keys_given:
        slots.update(ck=wck, cv=wcv)
    copies = weight_copies(weight, slots, sems)
    if not keys_given:
        begin(copies, ("ck", "cv"))
    begin(copies, ("q", "k", "v", "o", "cq", "co", "gate0", "up0", "down", *LATE_HIDDEN))
    own = same_head()
    own_low = low(own)
    stream = x_ref[...].astype(jnp.float32)
    normed = low(stream * scale_of(stream) * gains_ref[0:1])
    n1_ref[...] = normed
    if not keys_given:
        for name, held_weight, target in (("ck", wck, ck_ref), ("cv", wcv, cv_ref)):
            finish(copies, name)
            for row in range(BATCHES):
                part = pl.ds(STATES * row, STATES)
                target[part] = low(product(enc_ref[part], square(held_weight)))
    finish(copies, "q")
    q_ref[...] = low(product(normed, square(wq)))
    finish(copies, "k")
    k_ref[...] = low(product(normed, square(wk)))
    finish(copies, "v")
    v_ref[...] = low(product(normed, square(wv)))
    for row in range(BATCHES):
        part = pl.ds(TOKENS * row, TOKENS)
        for group in range(GROUPS):
            lanes = pl.ds(GROUP * group, GROUP)
            spread = spread_heads(q_ref[part, lanes], own_low)
            scores = product(spread, k_ref[part, lanes], 1, 1) + self_add_ref[row, lanes]
            chance = softmax_rows(scores)
            p_ref[row, lanes] = chance
            mixed = product(low(chance), v_ref[part, lanes])
            o_ref[part, lanes] = low(fold_heads(mixed, own))
    finish(copies, "o")
    stream = stream + product(o_ref[...], square(wo))
    a2_ref[...] = stream
    normed = low(stream * scale_of(stream) * gains_ref[1:2])
    n2_ref[...] = normed
    finish(copies, "cq")
    cq_ref[...] = low(product(normed, square(wcq)))
    for row in range(BATCHES):
        part = pl.ds(TOKENS * row, TOKENS)
        keys = pl.ds(STATES * row, STATES)
        add = jnp.concatenate([cross_add_ref[row]] * 4, axis=0)
        for group in range(GROUPS):
            lanes = pl.ds(GROUP * group, GROUP)
            spread = spread_heads(cq_ref[part, lanes], own_low)
            scores = product(spread, ck_ref[keys, lanes], 1, 1) + add
            chance = softmax_rows(scores)
            cp_ref[row, lanes] = chance
            mixed = product(low(chance), cv_ref[keys, lanes])
            co_ref[part, lanes] = low(fold_heads(mixed, own))
    finish(copies, "co")
    stream = a2_ref[...] + product(co_ref[...], square(wco))
    a3_ref[...] = stream
    n3_ref[...] = low(stream * scale_of(stream) * gains_ref[2:3])
    total = a3_ref[...]
    for index in range(CHUNKS):
        lanes = pl.ds(index * CHUNK, CHUNK)
        rows = n3_ref[...]
        finish(copies, "gate" + str(index))
        gate = product(rows, wg[:, :, lanes].reshape(WIDE, CHUNK))
        finish(copies, "up" + str(index))
        up = product(rows, wu[:, :, lanes].reshape(WIDE, CHUNK))
        gate_ref[:, lanes] = gate
        up_ref[:, lanes] = up
        bent = 0.5 * (1.0 + jnp.tanh(GELU_SCALE * (gate + 0.044715 * (gate * gate * gate))))
        hidden = low(gate * bent * up)
        hid_ref[:, lanes] = hidden
        if index == 0:
            finish(copies, "down")
        total = total + product(hidden, wd[pl.ds(4 * index, 4)].reshape(CHUNK, WIDE))
    out_ref[...] = low(total)


def first_kernel(
    x_ref, enc_ref, self_add_ref, cross_add_ref, gains_ref, weight, out_ref, ck_ref, cv_ref, *rest
):
    (n1, q, k, v, p, o, a2, n2, cq, cp, co, a3, n3, gate, up, hid, *scratch) = rest
    forward_body(
        False,
        x_ref, enc_ref, self_add_ref, cross_add_ref, gains_ref, weight, out_ref,
        n1, q, k, v, p, o, a2, n2, cq, ck_ref, cv_ref, cp, co, a3, n3, gate, up, hid, *scratch,
    )


def turn_kernel(
    x_ref, ck_ref, cv_ref, self_add_ref, cross_add_ref, gains_ref, c_ref, weight,
    out_ref, da_ref, *rest,
):
    saved_out, saved, rest = rest[:16], rest[16:32], rest[32:]
    dc_ref, dcq_ref, dck_ref, dcv_ref, dself_ref, dq_ref, dk_ref, dv_ref, *rest = rest
    wq, wk, wv, wo, wcq, wco, wg, wu, wd, sems, out_sems = rest
    n1, q, k, v, p, o, a2, n2, cq, cp, co, a3, n3, gate, up, hid = saved
    forward_body(
        True,
        x_ref, None, self_add_ref, cross_add_ref, gains_ref, weight, out_ref,
        n1, q, k, v, p, o, a2, n2, cq, ck_ref, cv_ref, cp, co, a3, n3, gate, up, hid,
        wq, wk, wv, wo, wcq, None, None, wco, wg, wu, wd, sems,
    )
    sent = [
        pltpu.make_async_copy(source, target, out_sems.at[place])
        for place, (source, target) in enumerate(zip(saved, saved_out))
    ]
    for copy in sent:
        copy.start()

    def finish_weight(name):
        return None

    def emit(index, lanes, dgate, dup):
        return None

    stream, _ = hidden_back(finish_weight, emit, c_ref, a3, gains_ref, gate, up, wg, wu, wd)
    stream, _ = cross_back(
        stream, finish_weight, gains_ref, a2, cq, ck_ref, cv_ref, cp, wcq, wco,
        dc_ref, dcq_ref, dck_ref, dcv_ref,
    )
    stream, _ = self_back(
        stream, finish_weight, gains_ref, x_ref, q, k, v, p, wq, wk, wv, wo,
        dself_ref, dq_ref, dk_ref, dv_ref, None,
    )
    da_ref[...] = low(stream)
    for copy in sent:
        copy.wait()


def core_is(part):
    return lax.axis_index("section") == part


def push(source, keep, send, part, window, sem):
    @pl.when(core_is(part))
    def _():
        pltpu.make_async_copy(source, keep.at[window], sem).start()

    @pl.when(jnp.logical_not(core_is(part)))
    def _():
        pltpu.make_async_copy(source, send.at[window], sem).start()

    return pltpu.make_async_copy(source, keep.at[window], sem)


def columns(start, width):
    return (slice(None), slice(None), slice(None), pl.ds(start, width))


def put_square(slot, part, lanes, value):
    value = value.reshape(RING, RING, ROWS_OWN, value.shape[-1])
    if part == 1:
        slot[:, :, :, lanes] = value
    else:
        for place in range(RING):
            slot[:, place, :, lanes] = value[place]


def hidden_back(finish_weight, emit, c_ref, a3_ref, gains_ref, gate_ref, up_ref, wg, wu, wd):
    total = jnp.zeros(ALL_TOKENS, jnp.float32)
    finish_weight("down")
    for index in range(CHUNKS):
        lanes = pl.ds(index * CHUNK, CHUNK)
        grad = product(c_ref[...], wd[pl.ds(4 * index, 4)].reshape(CHUNK, WIDE), 1, 1)
        bent, slope = gelu_parts(gate_ref[:, lanes])
        dgate = low(grad * up_ref[:, lanes] * slope)
        dup = low(grad * bent)
        finish_weight("gate" + str(index))
        total = total + product(dgate, wg[:, :, lanes].reshape(WIDE, CHUNK), 1, 1)
        finish_weight("up" + str(index))
        total = total + product(dup, wu[:, :, lanes].reshape(WIDE, CHUNK), 1, 1)
        emit(index, lanes, dgate, dup)
    back, dgain = norm_back(total, a3_ref[...], gains_ref[2:3])
    return c_ref[...].astype(jnp.float32) + back, dgain


def cross_back(
    stream, finish_weight, gains_ref, a2_ref, cq_ref, ck_ref, cv_ref, cp_ref, wcq, wco,
    dc_ref, dcq_ref, dck_ref, dcv_ref,
):
    own = same_head()
    own_low = low(own)
    dc_ref[...] = low(stream)
    finish_weight("co")
    datt = low(product(dc_ref[...], square(wco), 1, 1))
    for row in range(BATCHES):
        part = pl.ds(TOKENS * row, TOKENS)
        keys = pl.ds(STATES * row, STATES)
        for group in range(GROUPS):
            lanes = pl.ds(GROUP * group, GROUP)
            left = GROUP * group
            dout = spread_heads(
                datt[TOKENS * row : TOKENS * (row + 1), left : left + GROUP], own_low
            )
            spread = spread_heads(cq_ref[part, lanes], own_low)
            chance = cp_ref[row, lanes]
            dchance = product(dout, cv_ref[keys, lanes], 1, 1)
            dcv_ref[keys, lanes] = low(product(low(chance), dout, 0, 0))
            inner = jnp.sum(chance * dchance, axis=-1, keepdims=True)
            dscore = low(chance * (dchance - inner))
            dcq_ref[part, lanes] = low(fold_heads(product(dscore, ck_ref[keys, lanes]), own))
            dck_ref[keys, lanes] = low(product(dscore, spread, 0, 0))
    finish_weight("cq")
    grad = product(dcq_ref[...], square(wcq), 1, 1)
    back, dgain = norm_back(grad, a2_ref[...], gains_ref[1:2])
    return stream + back, dgain


def self_back(
    stream, finish_weight, gains_ref, x_ref, q_ref, k_ref, v_ref, p_ref, wq, wk, wv, wo,
    dself_ref, dq_ref, dk_ref, dv_ref, dscore_ref,
):
    own = same_head()
    own_low = low(own)
    dself_ref[...] = low(stream)
    finish_weight("o")
    datt = low(product(dself_ref[...], square(wo), 1, 1))
    for row in range(BATCHES):
        part = pl.ds(TOKENS * row, TOKENS)
        for group in range(GROUPS):
            lanes = pl.ds(GROUP * group, GROUP)
            left = GROUP * group
            dout = spread_heads(
                datt[TOKENS * row : TOKENS * (row + 1), left : left + GROUP], own_low
            )
            spread = spread_heads(q_ref[part, lanes], own_low)
            chance = p_ref[row, lanes]
            dchance = product(dout, v_ref[part, lanes], 1, 1)
            dv_ref[part, lanes] = low(product(low(chance), dout, 0, 0))
            inner = jnp.sum(chance * dchance, axis=-1, keepdims=True)
            dscore = low(chance * (dchance - inner))
            if dscore_ref is not None:
                if row == 0:
                    dscore_ref[lanes] = dscore.astype(jnp.float32)
                else:
                    dscore_ref[lanes] += dscore.astype(jnp.float32)
            dq_ref[part, lanes] = low(fold_heads(product(dscore, k_ref[part, lanes]), own))
            dk_ref[part, lanes] = low(product(dscore, spread, 0, 0))
    finish_weight("q")
    grad = product(dq_ref[...], square(wq), 1, 1)
    finish_weight("k")
    grad = grad + product(dk_ref[...], square(wk), 1, 1)
    finish_weight("v")
    grad = grad + product(dv_ref[...], square(wv), 1, 1)
    back, dgain = norm_back(grad, x_ref[...].astype(jnp.float32), gains_ref[0:1])
    return stream + back, dgain


def hidden_kernel(
    c_ref, a3_ref, gains_ref, gate_ref, up_ref, n3_ref, hid_ref, weight,
    stream_ref, dgain_ref, keep, send,
    wg, wu, wd, gg, gu, gd0, gd1, sems, out_sems,
):
    copies = weight_copies(weight, dict(gate=wg, up=wu, down=wd), sems)
    begin(copies, ("down", "gate0", "up0", *LATE_HIDDEN))
    sent = []

    def finish_weight(name):
        finish(copies, name)

    for index in range(RING):
        lanes = pl.ds(index * CHUNK, CHUNK)
        grad = low(product(hid_ref[:, lanes], c_ref[...], 0, 0))
        grad = grad.reshape(RING, FF // PARTS, WIDE)
        gd0[:, index] = grad[:, : FF // PARTS // 2]
        gd1[index] = grad[:, FF // PARTS // 2 :]
    for part, tall in enumerate((gd0, gd1)):
        for piece in range(GROUPS):
            for block in range(4):
                source = tall.at[:, :, pl.ds(16 * block, 16), pl.ds(GROUP * piece, GROUP)]
                window = (
                    slice(None),
                    slice(None),
                    pl.ds(16 * piece, 16),
                    pl.ds(FF + GROUP * block, GROUP),
                )
                sent.append(push(source, keep, send, part, window, out_sems.at[len(sent)]))

    def emit(index, lanes, dgate, dup):
        for part, slot, grad in ((0, gg, dgate), (1, gu, dup)):
            put_square(slot, part, lanes, low(product(n3_ref[...], grad, 0, 0)))
            window = columns(index * CHUNK, CHUNK)
            sent.append(
                push(slot.at[window], keep, send, part, window, out_sems.at[len(sent)])
            )

    stream, dgain = hidden_back(
        finish_weight, emit, c_ref, a3_ref, gains_ref, gate_ref, up_ref, wg, wu, wd
    )
    stream_ref[...] = stream
    dgain_ref[...] = dgain
    for copy in sent:
        copy.wait()


def cross_kernel(
    stream_ref, gains_ref, a2_ref, cq_ref, ck_ref, cv_ref, cp_ref, weight,
    next_ref, dgain_ref, dc_ref, dcq_ref, dck_ref, dcv_ref,
    wcq, wco, sems,
):
    copies = weight_copies(weight, dict(cq=wcq, co=wco), sems)
    begin(copies, ("co", "cq"))

    def finish_weight(name):
        finish(copies, name)

    stream, dgain = cross_back(
        stream_ref[...], finish_weight, gains_ref, a2_ref, cq_ref, ck_ref, cv_ref, cp_ref,
        wcq, wco, dc_ref, dcq_ref, dck_ref, dcv_ref,
    )
    next_ref[...] = stream
    dgain_ref[...] = dgain


def self_kernel(
    stream_ref, x_ref, gains_ref, q_ref, k_ref, v_ref, p_ref,
    enc_ref, n1_ref, o_ref, n2_ref, co_ref, dc_ref, dcq_ref, dck_ref, dcv_ref, weight,
    da_ref, dgain_ref, dscore_ref, denc_ref, keep, send,
    dself_ref, dq_ref, dk_ref, dv_ref,
    wq, wk, wv, wo, wck, wcv, g0, g1, g2, g3, g4, g5, g6, g7, sems, out_sems,
):
    slots = dict(q=wq, k=wk, v=wv, o=wo, ck=wck, cv=wcv)
    copies = weight_copies(weight, slots, sems)
    begin(copies, ("o", "q", "k", "v", "ck", "cv"))

    def finish_weight(name):
        finish(copies, name)

    sent = []

    def emit(slot, part, column, left, right):
        put_square(slot, part, slice(None), low(product(left[...], right[...], 0, 0)))
        window = columns(WIDE * column, WIDE)
        sent.append(push(slot, keep, send, part, window, out_sems.at[len(sent)]))

    emit(g0, 0, 0, co_ref, dc_ref)
    emit(g1, 0, 1, n2_ref, dcq_ref)
    emit(g2, 1, 0, enc_ref, dck_ref)
    emit(g3, 1, 1, enc_ref, dcv_ref)
    stream, dgain = self_back(
        stream_ref[...], finish_weight, gains_ref, x_ref, q_ref, k_ref, v_ref, p_ref,
        wq, wk, wv, wo, dself_ref, dq_ref, dk_ref, dv_ref, dscore_ref,
    )
    da_ref[...] = low(stream)
    dgain_ref[...] = dgain
    emit(g4, 0, 2, o_ref, dself_ref)
    emit(g5, 0, 3, n1_ref, dq_ref)
    emit(g6, 1, 2, n1_ref, dk_ref)
    emit(g7, 1, 3, n1_ref, dv_ref)
    finish(copies, "ck")
    finish(copies, "cv")
    for row in range(BATCHES):
        keys = pl.ds(STATES * row, STATES)
        denc_ref[keys] = low(
            product(dck_ref[keys], square(wck), 1, 1) + product(dcv_ref[keys], square(wcv), 1, 1)
        )
    for copy in sent:
        copy.wait()


def in_vmem(count):
    return [pl.BlockSpec(memory_space=pltpu.VMEM)] * count


def held(*shapes):
    return [pltpu.VMEM(shape, jnp.bfloat16) for shape in shapes]


def shape_of(dims, kind=jnp.bfloat16):
    return jax.ShapeDtypeStruct(dims, kind)


params = pltpu.CompilerParams(vmem_limit_bytes=VMEM_BYTES)


ANYWHERE = pl.BlockSpec(memory_space=pl.ANY)
DMAS = pltpu.SemaphoreType.DMA((40,))
SAVED = (
    (ALL_TOKENS, jnp.bfloat16),
    (ALL_TOKENS, jnp.bfloat16),
    (ALL_TOKENS, jnp.bfloat16),
    (ALL_TOKENS, jnp.bfloat16),
    ((BATCHES, WIDE, TOKENS), jnp.float32),
    (ALL_TOKENS, jnp.bfloat16),
    (ALL_TOKENS, jnp.float32),
    (ALL_TOKENS, jnp.bfloat16),
    (ALL_TOKENS, jnp.bfloat16),
    ((BATCHES, WIDE, STATES), jnp.float32),
    (ALL_TOKENS, jnp.bfloat16),
    (ALL_TOKENS, jnp.float32),
    (ALL_TOKENS, jnp.bfloat16),
    (HIDDEN, jnp.float32),
    (HIDDEN, jnp.float32),
    (HIDDEN, jnp.bfloat16),
)


def run_first(x, enc, self_add, cross_add, gains, weight):
    outs = [shape_of(ALL_TOKENS), shape_of(ALL_STATES), shape_of(ALL_STATES)]
    return pl.pallas_call(
        first_kernel,
        out_shape=outs,
        in_specs=in_vmem(5) + [pl.BlockSpec(memory_space=pl.ANY)],
        out_specs=in_vmem(len(outs)),
        scratch_shapes=[pltpu.VMEM(dims, kind) for dims, kind in SAVED]
        + held(*[FULL] * 8, GATED, GATED, DOWN)
        + [pltpu.SemaphoreType.DMA((40,))],
        compiler_params=params,
        name="first_forward",
    )(x, enc, self_add, cross_add, gains, weight)


def run_turn(x, ck, cv, self_add, cross_add, gains, cotangent, weight):
    saved = [shape_of(dims, kind) for dims, kind in SAVED]
    return pl.pallas_call(
        turn_kernel,
        out_shape=[shape_of(ALL_TOKENS)] * 2 + saved,
        in_specs=in_vmem(7) + [ANYWHERE],
        out_specs=in_vmem(2) + [ANYWHERE] * len(saved),
        scratch_shapes=[pltpu.VMEM(dims, kind) for dims, kind in SAVED]
        + held(ALL_TOKENS, ALL_TOKENS, ALL_STATES, ALL_STATES, *[ALL_TOKENS] * 4)
        + held(*[FULL] * 6, GATED, GATED, DOWN)
        + [DMAS, DMAS],
        compiler_params=params,
        name="forward_and_back",
    )(x, ck, cv, self_add, cross_add, gains, cotangent, weight)


HALF = (RING, RING, ROWS_OWN, ATT // 2)
RINGED = (RING, RING, ROWS_OWN, WIDE)
RINGED_WIDE = (RING, RING, ROWS_OWN, FF)
RINGED_TALL = (RING, RING, FF // PARTS // 2, WIDE)


def run_hidden(cotangent, gains, saved, weight):
    (ck, cv, n1, q, k, v, p, o, a2, n2, cq, cp, co, a3, n3, gate, up, hid) = saved
    return pl.pallas_call(
        hidden_kernel,
        out_shape=[
            shape_of(ALL_TOKENS, jnp.float32),
            shape_of((1, WIDE), jnp.float32),
            shape_of(HALF),
            shape_of(HALF),
        ],
        in_specs=in_vmem(7) + [ANYWHERE],
        out_specs=in_vmem(2) + [ANYWHERE, ANYWHERE],
        scratch_shapes=held(
            GATED, GATED, DOWN, RINGED_WIDE, RINGED_WIDE, RINGED_TALL, RINGED_TALL
        )
        + [DMAS, DMAS],
        compiler_params=params,
        name="hidden_backward",
    )(cotangent, a3, gains, gate, up, n3, hid, weight)


def run_cross(stream, gains, saved, weight):
    (ck, cv, n1, q, k, v, p, o, a2, n2, cq, cp, co, a3, n3, gate, up, hid) = saved
    return pl.pallas_call(
        cross_kernel,
        out_shape=[
            shape_of(ALL_TOKENS, jnp.float32),
            shape_of((1, WIDE), jnp.float32),
            shape_of(ALL_TOKENS),
            shape_of(ALL_TOKENS),
            shape_of(ALL_STATES),
            shape_of(ALL_STATES),
        ],
        in_specs=in_vmem(7) + [ANYWHERE],
        out_specs=in_vmem(6),
        scratch_shapes=held(FULL, FULL) + [DMAS],
        compiler_params=params,
        name="cross_backward",
    )(stream, gains, a2, cq, ck, cv, cp, weight)


def run_self(stream, x, gains, enc, saved, records, weight):
    (ck, cv, n1, q, k, v, p, o, a2, n2, cq, cp, co, a3, n3, gate, up, hid) = saved
    return pl.pallas_call(
        self_kernel,
        out_shape=[
            shape_of(ALL_TOKENS),
            shape_of((1, WIDE), jnp.float32),
            shape_of((WIDE, TOKENS), jnp.float32),
            shape_of(ALL_STATES),
            shape_of(HALF),
            shape_of(HALF),
        ],
        in_specs=in_vmem(16) + [ANYWHERE],
        out_specs=in_vmem(4) + [ANYWHERE, ANYWHERE],
        scratch_shapes=held(*[ALL_TOKENS] * 4, *[FULL] * 6, *[RINGED] * 8) + [DMAS, DMAS],
        compiler_params=params,
        name="self_backward",
    )(stream, x, gains, q, k, v, p, enc, n1, o, n2, co, *records, weight)


def pack_kernel(
    query_ref, kv_ref, out_ref, c_query_ref, c_kv_ref, c_out_ref, in_ref, ffn_ref, kept, given
):
    def attention(target):
        start = 0
        for ref in (query_ref, kv_ref, out_ref, c_query_ref, c_kv_ref, c_out_ref):
            if len(ref.shape) == 3:
                pair = ref[...].astype(jnp.float32)
                members = [low(pair[:, 0, :]), low(pair[:, 1, :])]
            else:
                members = [ref[...]]
            for member in members:
                target[:, start : start + WIDE] = member
                start += WIDE

    def hidden(target):
        pair = in_ref[...].astype(jnp.float32)
        target[:, :FF] = low(pair[:, 0, :])
        target[:, FF : 2 * FF] = low(pair[:, 1, :])
        for piece, block in DOWN_PIECES:
            lanes = pl.ds(2 * FF + GROUP * block, GROUP)
            target[pl.ds(16 * piece, 16), lanes] = ffn_ref[
                pl.ds(16 * block, 16), pl.ds(GROUP * piece, GROUP)
            ]

    @pl.when(core_is(0))
    def _():
        attention(kept)
        hidden(given)

    @pl.when(core_is(1))
    def _():
        hidden(kept)
        attention(given)


def run_pack(members):
    return pl.pallas_call(
        pack_kernel,
        out_shape=[shape_of((ROWS_OWN, ATT))] * 2,
        in_specs=in_vmem(8),
        out_specs=in_vmem(2),
        compiler_params=params,
        name="pack_weights",
    )(*members)


def add_kernel(left, right, total):
    total[...] = low(left[...].astype(jnp.float32) + right[...].astype(jnp.float32))


def add_halves(keep, received):
    dims = (WIDE, ATT // 2)
    spec = pl.BlockSpec((64, ATT // 2), lambda place: (place, 0))
    return pl.pallas_call(
        add_kernel,
        out_shape=shape_of(dims),
        grid=(12,),
        in_specs=[spec, spec],
        out_specs=spec,
        compiler_params=params,
        name="add_halves",
    )(keep.reshape(dims), received.reshape(dims))


def unpack_kernel(
    mine, theirs, query_ref, kv_ref, out_ref, c_query_ref, c_kv_ref, c_out_ref, in_ref, ffn_ref
):
    def write(first, second):
        def square_at(part, place):
            start = ATT // 2 + WIDE * place
            return part[:, start : start + WIDE].astype(jnp.float32)

        c_out_ref[...] = square_at(first, 0)
        c_query_ref[...] = square_at(first, 1)
        out_ref[...] = square_at(first, 2)
        query_ref[...] = square_at(first, 3)
        c_kv_ref[:, 0, :] = square_at(second, 0)
        c_kv_ref[:, 1, :] = square_at(second, 1)
        kv_ref[:, 0, :] = square_at(second, 2)
        kv_ref[:, 1, :] = square_at(second, 3)
        for index, part in enumerate((first, second)):
            in_ref[:, index, :] = part[:, :FF].astype(jnp.float32)
            for piece in range(GROUPS):
                for block in range(4):
                    rows = pl.ds(64 * index + 16 * block, 16)
                    taken = part[pl.ds(16 * piece, 16), pl.ds(FF + GROUP * block, GROUP)]
                    ffn_ref[rows, pl.ds(GROUP * piece, GROUP)] = taken.astype(jnp.float32)

    @pl.when(core_is(0))
    def _():
        write(mine, theirs)

    @pl.when(core_is(1))
    def _():
        write(theirs, mine)


def run_unpack(mine, theirs):
    wide = jnp.float32
    square_dims, pair_dims = (ROWS_OWN, WIDE), (ROWS_OWN, 2, WIDE)
    outs = [square_dims, pair_dims, square_dims, square_dims, pair_dims, square_dims]
    outs += [(ROWS_OWN, 2, FF), (FF // PARTS, WIDE)]
    return pl.pallas_call(
        unpack_kernel,
        out_shape=[shape_of(dims, wide) for dims in outs],
        in_specs=in_vmem(2),
        out_specs=in_vmem(8),
        compiler_params=pltpu.CompilerParams(vmem_limit_bytes=10 * 1024 * 1024),
        name="unpack_gradients",
    )(mine, theirs)


def score_terms(table, dec_ids, enc_ids):
    positions = jnp.arange(TOKENS)
    by_distance = jnp.dot(table.astype(jnp.float32).T, bucket_onehot(TOKENS), precision=highest)
    bias = spread_distance(by_distance)
    allowed = (dec_ids[:, :, None] == dec_ids[:, None, :]) & (
        positions[None, :] <= positions[:, None]
    )
    self_add = jnp.where(allowed[:, None], bias[None], -jnp.inf)
    cross_add = jnp.where(dec_ids[:, :, None] == enc_ids[:, None, :], 0.0, -jnp.inf)
    return self_add.reshape(BATCHES, WIDE, TOKENS), cross_add


def shards(
    layer_in,
    cotangent,
    encoder,
    dec_segments,
    enc_segments,
    norm_gains,
    self_query,
    self_kv,
    self_out,
    rel_bias,
    cross_query,
    cross_kv,
    cross_out,
    ffn_in,
    ffn_out,
):
    core = lax.axis_index("section")
    part_index = lax.axis_index("fsdp")
    plane = lax.axis_index("rep")
    planes = lax.axis_size("rep")
    layer = lax.rem(plane, 2)
    first_core = core == 0
    at_home = core == layer

    def place(core_index, plane_index):
        return core_index * planes + plane_index

    def flip_core(value):
        return lax.ppermute(value, "section", [(0, 1), (1, 0)])

    def from_home(value):
        pairs = [(place(p % 2, p), place(1 - p % 2, p)) for p in range(planes)]
        return jnp.where(at_home, value, lax.ppermute(value, ("section", "rep"), pairs))

    def beside(value):
        return lax.ppermute(value, "rep", [(p, p ^ 1) for p in range(planes)])

    def to_home(value):
        pairs = [(place(1 - p % 2, p), place(1 - p % 2, p ^ 1)) for p in range(planes)]
        return lax.ppermute(value, ("section", "rep"), pairs)

    def rows_for_layer(value):
        pairs = [(place(p % 2, p), place(p % 2, p ^ 1)) for p in range(planes)]
        return jnp.where(at_home, value, lax.ppermute(value, ("section", "rep"), pairs))

    def rows_back(value):
        pairs = [(place(1 - p % 2, p), place(p % 2, p ^ 1)) for p in range(planes)]
        return jnp.where(at_home, value, lax.ppermute(value, ("section", "rep"), pairs))

    def between_layers(value, steps):
        pairs = [(p, p + steps) for p in range(planes) if p % 2 == (steps < 0)]
        return lax.ppermute(value, "rep", pairs)

    along_z = [[RING * x + z for z in range(RING)] for x in range(RING)]
    along_x = [[RING * x + z for x in range(RING)] for z in range(RING)]
    first_rings = along_z + [[PARTS + d for d in ring] for ring in along_x]
    second_rings = along_x + [[PARTS + d for d in ring] for ring in along_z]

    def scatter(value, rings):
        return lax.psum_scatter(
            value, ("section", "fsdp"), scatter_dimension=0, axis_index_groups=rings, tiled=True
        )

    kept, given_away = run_pack(
        [
            member[0]
            for member in (
                self_query,
                self_kv,
                self_out,
                cross_query,
                cross_kv,
                cross_out,
                ffn_in,
                ffn_out,
            )
        ]
    )
    half = jnp.where(at_home, kept, flip_core(given_away))
    weight = lax.all_gather(half, ("fsdp", "section"), axis=0, tiled=True)
    weight = weight.reshape(PARTS, 2, ROWS_OWN, ATT)
    small = jnp.zeros((8, 128), jnp.bfloat16)
    small = small.at[:3, :ROWS_OWN].set(norm_gains[0])
    small = small.at[3:5, :HEADS].set(rel_bias[0])
    small = lax.all_gather(from_home(small), "fsdp", axis=0, tiled=False)
    gains = small[:, :3, :ROWS_OWN].transpose(1, 0, 2).reshape(3, WIDE).astype(jnp.float32)
    table = small[:, 3:5, :HEADS].reshape(BUCKETS, HEADS)
    ids = jnp.concatenate([dec_segments[:, 0], enc_segments[:, 0]], axis=1)
    ids = rows_for_layer(ids)
    self_add, cross_add = score_terms(table, ids[:, :TOKENS], ids[:, TOKENS:])
    ends = jnp.stack([layer_in[:, 0].reshape(ALL_TOKENS), cotangent[:, 0].reshape(ALL_TOKENS)])
    ends = rows_for_layer(ends)
    rows_in, given = ends[0], ends[1]
    enc = rows_for_layer(encoder[:, 0].reshape(ALL_STATES))
    weight, rows_in, given, enc, self_add, cross_add, gains = lax.optimization_barrier(
        (weight, rows_in, given, enc, self_add, cross_add, gains)
    )
    first, ck, cv = run_first(rows_in, enc, self_add, cross_add, gains, weight)
    current = jnp.where(layer == 0, rows_in, between_layers(first, 1))
    result, grad_first, *saved = run_turn(
        current, ck, cv, self_add, cross_add, gains, given, weight
    )
    saved = [ck, cv] + saved
    incoming = jnp.where(layer == 1, given, between_layers(grad_first, -1))
    stream, gain_three, keep, send = run_hidden(incoming, gains, saved, weight)
    received = flip_core(send)
    stream, gain_two, *records = run_cross(stream, gains, saved, weight)
    wide_sum = add_halves(keep, received)
    wide_sum, stream = lax.optimization_barrier((wide_sum, stream))
    wide_part = scatter(wide_sum, first_rings)
    grad_input, gain_one, grad_scores, grad_enc, keep, send = run_self(
        stream, current, gains, enc, saved, records, weight
    )
    square_part = scatter(add_halves(keep, flip_core(send)), first_rings)
    grad_gains = jnp.concatenate([gain_one, gain_two, gain_three], axis=0)
    diagonal_sums = gather_distance(grad_scores.reshape(HEADS, TOKENS, TOKENS))
    grad_table = jnp.dot(bucket_onehot(TOKENS), diagonal_sums.T, precision=highest)
    little = jnp.zeros((8, WIDE), jnp.float32)
    little = little.at[:3].set(grad_gains)
    little = little.at[3, : BUCKETS * HEADS].set(grad_table.reshape(-1))

    def add_pairs(value, axis, bits):
        for bit in bits:
            pairs = [(index, index ^ bit) for index in range(lax.axis_size(axis))]
            value = value + lax.ppermute(value, axis, pairs)
        return value

    little = add_pairs(add_pairs(little, "section", (1,)), "fsdp", (1, 2, 4, 8))
    outs = rows_back(jnp.stack([result, grad_input]))
    wide_part, square_part, little, outs, grad_enc = lax.optimization_barrier(
        (wide_part, square_part, little, outs, grad_enc)
    )
    partial = scatter(jnp.concatenate([wide_part, square_part], axis=1), second_rings)
    other_enc = to_home(grad_enc)
    little = add_pairs(little, "rep", (2,))
    little = jnp.where(at_home, little, beside(little))
    own_gains = lax.dynamic_slice(little, (0, part_index * ROWS_OWN), (3, ROWS_OWN))
    own_table = lax.dynamic_slice(little, (3, part_index * 2 * HEADS), (1, 2 * HEADS))
    encoder_total = grad_enc.astype(jnp.float32) + other_enc.astype(jnp.float32)
    encoder_total = from_home(encoder_total)
    own_table = own_table.reshape(2, HEADS)
    results = (
        outs[0].reshape(1, BATCHES, 1, TOKENS, WIDE),
        outs[1].reshape(1, BATCHES, 1, TOKENS, WIDE),
        encoder_total.reshape(BATCHES, 1, STATES, WIDE),
        own_gains[None],
        own_table[None],
    )
    partial, results = lax.optimization_barrier((partial, results))
    up = [(p, (p + 1) % planes) for p in range(planes)]
    down = [(p, (p - 1) % planes) for p in range(planes)]
    across = [(p, (p + 2) % planes) for p in range(planes)]
    cut = ATT // 2
    outer = (plane == 0) | (plane == planes - 1)
    lower = plane < 2
    rising = lax.ppermute(jnp.where(outer, partial[:, :cut], partial[:, cut:]), "rep", up)
    falling = lax.ppermute(jnp.where(outer, partial[:, cut:], partial[:, :cut]), "rep", down)
    here = low(rising.astype(jnp.float32) + falling.astype(jnp.float32))
    below = lax.ppermute(here, "rep", up)
    above = lax.ppermute(here, "rep", down)
    beyond = lax.ppermute(here, "rep", across)
    own_layer = (jnp.where(outer, above, below), jnp.where(outer, below, above))
    other_layer = (jnp.where(lower, here, beyond), jnp.where(lower, beyond, here))
    pairs = list(zip(own_layer, other_layer))
    mine = jnp.concatenate([jnp.where(at_home, own, other) for own, other in pairs], axis=1)
    away = jnp.concatenate([jnp.where(at_home, other, own) for own, other in pairs], axis=1)
    query, kv, out, *others = [member[None] for member in run_unpack(mine, flip_core(away))]
    return (*results[:4], query, kv, out, results[4], *others)


def solution(mesh):
    return jax.shard_map(
        shards,
        mesh=mesh,
        in_specs=(
            P(None, ("fsdp", "rep"), None, None),
            P(None, ("fsdp", "rep"), None, None),
            P(None, ("fsdp", "rep"), None, None),
            P(None, ("fsdp", "rep"), None),
            P(None, ("fsdp", "rep"), None),
            P("section", None, "fsdp"),
            P("section", "fsdp", None),
            P("section", "fsdp", None, None),
            P("section", "fsdp", None),
            P("section", "fsdp", None),
            P("section", "fsdp", None),
            P("section", "fsdp", None, None),
            P("section", "fsdp", None),
            P("section", "fsdp", None, None),
            P("section", "fsdp", None),
        ),
        out_specs=(
            P("section", None, ("fsdp", "rep"), None, None),
            P("section", None, ("fsdp", "rep"), None, None),
            P(None, ("fsdp", "rep"), None, None),
            P("section", None, "fsdp"),
            P("section", "fsdp", None),
            P("section", "fsdp", None, None),
            P("section", "fsdp", None),
            P("section", "fsdp", None),
            P("section", "fsdp", None),
            P("section", "fsdp", None, None),
            P("section", "fsdp", None),
            P("section", "fsdp", None, None),
            P("section", "fsdp", None),
        ),
        check_vma=False,
    )
```

```python
import jax
import jax.numpy as jnp
import numpy as np
from jax import lax
from jax.experimental import pallas as pl
from jax.experimental.pallas import tpu as pltpu
from jax.sharding import PartitionSpec as P

HEADS = 12
HEAD = 64
BUCKETS = 32
MAX_DIST = 128
PARTS = 16
GELU_SCALE = float(np.sqrt(2.0 / np.pi))


epsilon = 1e-06
highest = lax.Precision.HIGHEST


def bucket_row(length):
    distance = np.arange(length)
    half_count = BUCKETS // 2
    scaled = (
        np.log(np.maximum(distance, half_count) / half_count)
        / np.log(MAX_DIST / half_count)
        * (BUCKETS - half_count)
    )
    far_bucket = np.minimum(half_count + np.floor(scaled).astype(np.int32), BUCKETS - 1)
    return np.where(distance < half_count, distance, far_bucket).astype(np.int32)


def bucket_onehot(length):
    return (bucket_row(length)[None, :] == np.arange(BUCKETS)[:, None]).astype(np.float32)


def spread_distance(by_distance):
    head_count, length = by_distance.shape
    padded_row = jnp.concatenate(
        [jnp.zeros((head_count, length - 1), jnp.float32), by_distance], axis=1
    )
    tiled = jnp.tile(padded_row, (1, length))
    tiled = jnp.concatenate([tiled, jnp.zeros((head_count, length), jnp.float32)], axis=1)
    return tiled.reshape(head_count, length, 2 * length)[:, :, :length][:, :, ::-1]


def gather_distance(grid):
    head_count, length, _ = grid.shape
    flipped = jnp.concatenate(
        [grid[:, :, ::-1], jnp.zeros((head_count, length, length), jnp.float32)], axis=2
    )
    flat = flipped.reshape(head_count, 2 * length * length)[:, : length * (2 * length - 1)]
    return jnp.sum(flat.reshape(head_count, length, 2 * length - 1), axis=1)[:, length - 1 :]


ROWS_OWN = 48
TOKENS = 64
WIDE = 768
FF = 2048
GROUP = 256
GROUPS = 3
BATCHES = 2
STATES = 256
CHUNK = 512
CHUNKS = FF // CHUNK
ATT = 6144
ALL_TOKENS = (BATCHES * TOKENS, WIDE)
ALL_STATES = (BATCHES * STATES, WIDE)
HIDDEN = (BATCHES * TOKENS, FF)
VMEM_BYTES = 60 * 1024 * 1024
FULL = (PARTS, ROWS_OWN, WIDE)
GATED = (PARTS, ROWS_OWN, FF)
DOWN = (PARTS, FF // PARTS, WIDE)
RING = 4
LATE_HIDDEN = [name + str(index) for index in range(1, CHUNKS) for name in ("gate", "up")]
DOWN_PIECES = [(piece, block) for piece in range(GROUPS) for block in range(8)]


def product(left, right, along_left=1, along_right=0):
    return lax.dot_general(
        left,
        right,
        (((along_left,), (along_right,)), ((), ())),
        preferred_element_type=jnp.float32,
    )


def low(value):
    return value.astype(jnp.bfloat16)


def same_head():
    row = lax.broadcasted_iota(jnp.int32, (GROUP, GROUP), 0) // HEAD
    lane = lax.broadcasted_iota(jnp.int32, (GROUP, GROUP), 1) // HEAD
    return jnp.where(row == lane, 1.0, 0.0)


def spread_heads(block, own_low):
    return jnp.concatenate([block] * 4, axis=0) * own_low


def fold_heads(block, own):
    kept = block * own
    return kept[:64] + kept[64:128] + kept[128:192] + kept[192:]


def scale_of(value):
    return lax.rsqrt(jnp.mean(value * value, axis=-1, keepdims=True) + epsilon)


def norm_back(grad, value, gain):
    scale = scale_of(value)
    carried = grad * gain
    mean = jnp.mean(value * carried, axis=-1, keepdims=True)
    grad_value = carried * scale - value * (scale * scale * scale) * mean
    grad_gain = jnp.sum(grad * value * scale, axis=0, keepdims=True)
    return grad_value, grad_gain


def square(ref):
    return ref[...].reshape(WIDE, WIDE)


def down_at(ref, piece, block):
    return ref.at[:, 1, pl.ds(16 * piece, 16), pl.ds(2 * FF + GROUP * block, GROUP)]


def rows_at(ref, piece, block):
    return ref.at[:, pl.ds(16 * block, 16), pl.ds(GROUP * piece, GROUP)]


def softmax_rows(scores):
    raised = jnp.exp(scores - jnp.max(scores, axis=-1, keepdims=True))
    return raised / jnp.sum(raised, axis=-1, keepdims=True)


def gelu_parts(gate):
    cube = gate * gate * gate
    bent = jnp.tanh(GELU_SCALE * (gate + 0.044715 * cube))
    half = 0.5 * (1.0 + bent)
    slope = half + 0.5 * gate * (1.0 - bent * bent) * GELU_SCALE * (
        1.0 + 3.0 * 0.044715 * gate * gate
    )
    return gate * half, slope


def weight_copies(weight, slots, sems):
    copies = {}
    for place, (name, column) in enumerate(
        (("q", 0), ("k", 1), ("v", 2), ("o", 3), ("cq", 4), ("ck", 5), ("cv", 6), ("co", 7))
    ):
        if name in slots:
            source = weight.at[:, 0, :, pl.ds(WIDE * column, WIDE)]
            copies[name] = [pltpu.make_async_copy(source, slots[name], sems.at[place])]
    for place, (name, column) in enumerate((("gate", 0), ("up", FF))):
        if name in slots:
            for index in range(CHUNKS):
                start = CHUNK * index
                source = weight.at[:, 1, :, pl.ds(column + start, CHUNK)]
                target = slots[name].at[:, :, pl.ds(start, CHUNK)]
                sem = sems.at[8 + CHUNKS * place + index]
                copies[name + str(index)] = [pltpu.make_async_copy(source, target, sem)]
    if "down" in slots:
        copies["down"] = [
            pltpu.make_async_copy(
                down_at(weight, piece, block),
                rows_at(slots["down"], piece, block),
                sems.at[8 + 2 * CHUNKS + place],
            )
            for place, (piece, block) in enumerate(DOWN_PIECES)
        ]
    return copies


def begin(copies, names):
    for name in names:
        for copy in copies[name]:
            copy.start()


def finish(copies, name):
    for copy in copies[name]:
        copy.wait()


def forward_body(
    keys_given,
    x_ref,
    enc_ref,
    self_add_ref,
    cross_add_ref,
    gains_ref,
    weight,
    out_ref,
    n1_ref,
    q_ref,
    k_ref,
    v_ref,
    p_ref,
    o_ref,
    a2_ref,
    n2_ref,
    cq_ref,
    ck_ref,
    cv_ref,
    cp_ref,
    co_ref,
    a3_ref,
    n3_ref,
    gate_ref,
    up_ref,
    hid_ref,
    wq,
    wk,
    wv,
    wo,
    wcq,
    wck,
    wcv,
    wco,
    wg,
    wu,
    wd,
    sems,
):
    slots = dict(q=wq, k=wk, v=wv, o=wo, cq=wcq, co=wco, gate=wg, up=wu, down=wd)
    if not keys_given:
        slots.update(ck=wck, cv=wcv)
    copies = weight_copies(weight, slots, sems)
    if not keys_given:
        begin(copies, ("ck", "cv"))
    begin(copies, ("q", "k", "v", "o", "cq", "co", "gate0", "up0", "down", *LATE_HIDDEN))
    own = same_head()
    own_low = low(own)
    stream = x_ref[...].astype(jnp.float32)
    normed = low(stream * scale_of(stream) * gains_ref[0:1])
    n1_ref[...] = normed
    if not keys_given:
        for name, held_weight, target in (("ck", wck, ck_ref), ("cv", wcv, cv_ref)):
            finish(copies, name)
            for row in range(BATCHES):
                part = pl.ds(STATES * row, STATES)
                target[part] = low(product(enc_ref[part], square(held_weight)))
    finish(copies, "q")
    q_ref[...] = low(product(normed, square(wq)))
    finish(copies, "k")
    k_ref[...] = low(product(normed, square(wk)))
    finish(copies, "v")
    v_ref[...] = low(product(normed, square(wv)))
    for row in range(BATCHES):
        part = pl.ds(TOKENS * row, TOKENS)
        for group in range(GROUPS):
            lanes = pl.ds(GROUP * group, GROUP)
            spread = spread_heads(q_ref[part, lanes], own_low)
            scores = product(spread, k_ref[part, lanes], 1, 1) + self_add_ref[row, lanes]
            chance = softmax_rows(scores)
            p_ref[row, lanes] = chance
            mixed = product(low(chance), v_ref[part, lanes])
            o_ref[part, lanes] = low(fold_heads(mixed, own))
    finish(copies, "o")
    stream = stream + product(o_ref[...], square(wo))
    a2_ref[...] = stream
    normed = low(stream * scale_of(stream) * gains_ref[1:2])
    n2_ref[...] = normed
    finish(copies, "cq")
    cq_ref[...] = low(product(normed, square(wcq)))
    for row in range(BATCHES):
        part = pl.ds(TOKENS * row, TOKENS)
        keys = pl.ds(STATES * row, STATES)
        add = jnp.concatenate([cross_add_ref[row]] * 4, axis=0)
        for group in range(GROUPS):
            lanes = pl.ds(GROUP * group, GROUP)
            spread = spread_heads(cq_ref[part, lanes], own_low)
            scores = product(spread, ck_ref[keys, lanes], 1, 1) + add
            chance = softmax_rows(scores)
            cp_ref[row, lanes] = chance
            mixed = product(low(chance), cv_ref[keys, lanes])
            co_ref[part, lanes] = low(fold_heads(mixed, own))
    finish(copies, "co")
    stream = a2_ref[...] + product(co_ref[...], square(wco))
    a3_ref[...] = stream
    n3_ref[...] = low(stream * scale_of(stream) * gains_ref[2:3])
    total = a3_ref[...]
    for index in range(CHUNKS):
        lanes = pl.ds(index * CHUNK, CHUNK)
        rows = n3_ref[...]
        finish(copies, "gate" + str(index))
        gate = product(rows, wg[:, :, lanes].reshape(WIDE, CHUNK))
        finish(copies, "up" + str(index))
        up = product(rows, wu[:, :, lanes].reshape(WIDE, CHUNK))
        gate_ref[:, lanes] = gate
        up_ref[:, lanes] = up
        bent = 0.5 * (1.0 + jnp.tanh(GELU_SCALE * (gate + 0.044715 * (gate * gate * gate))))
        hidden = low(gate * bent * up)
        hid_ref[:, lanes] = hidden
        if index == 0:
            finish(copies, "down")
        total = total + product(hidden, wd[pl.ds(4 * index, 4)].reshape(CHUNK, WIDE))
    out_ref[...] = low(total)


def first_kernel(
    x_ref, enc_ref, self_add_ref, cross_add_ref, gains_ref, weight, out_ref, ck_ref, cv_ref, *rest
):
    (n1, q, k, v, p, o, a2, n2, cq, cp, co, a3, n3, gate, up, hid, *scratch) = rest
    forward_body(
        False,
        x_ref, enc_ref, self_add_ref, cross_add_ref, gains_ref, weight, out_ref,
        n1, q, k, v, p, o, a2, n2, cq, ck_ref, cv_ref, cp, co, a3, n3, gate, up, hid, *scratch,
    )


def turn_kernel(
    x_ref, ck_ref, cv_ref, self_add_ref, cross_add_ref, gains_ref, c_ref, weight,
    out_ref, da_ref, *rest,
):
    saved_out, saved, rest = rest[:16], rest[16:32], rest[32:]
    dc_ref, dcq_ref, dck_ref, dcv_ref, dself_ref, dq_ref, dk_ref, dv_ref, *rest = rest
    wq, wk, wv, wo, wcq, wco, wg, wu, wd, sems, out_sems = rest
    n1, q, k, v, p, o, a2, n2, cq, cp, co, a3, n3, gate, up, hid = saved
    forward_body(
        True,
        x_ref, None, self_add_ref, cross_add_ref, gains_ref, weight, out_ref,
        n1, q, k, v, p, o, a2, n2, cq, ck_ref, cv_ref, cp, co, a3, n3, gate, up, hid,
        wq, wk, wv, wo, wcq, None, None, wco, wg, wu, wd, sems,
    )
    sent = [
        pltpu.make_async_copy(source, target, out_sems.at[place])
        for place, (source, target) in enumerate(zip(saved, saved_out))
    ]
    for copy in sent:
        copy.start()

    def finish_weight(name):
        return None

    def emit(index, lanes, dgate, dup):
        return None

    stream, _ = hidden_back(finish_weight, emit, c_ref, a3, gains_ref, gate, up, wg, wu, wd)
    stream, _ = cross_back(
        stream, finish_weight, gains_ref, a2, cq, ck_ref, cv_ref, cp, wcq, wco,
        dc_ref, dcq_ref, dck_ref, dcv_ref,
    )
    stream, _ = self_back(
        stream, finish_weight, gains_ref, x_ref, q, k, v, p, wq, wk, wv, wo,
        dself_ref, dq_ref, dk_ref, dv_ref, None,
    )
    da_ref[...] = low(stream)
    for copy in sent:
        copy.wait()


def core_is(part):
    return lax.axis_index("section") == part


def push(source, keep, send, part, window, sem):
    @pl.when(core_is(part))
    def _():
        pltpu.make_async_copy(source, keep.at[window], sem).start()

    @pl.when(jnp.logical_not(core_is(part)))
    def _():
        pltpu.make_async_copy(source, send.at[window], sem).start()

    return pltpu.make_async_copy(source, keep.at[window], sem)


def columns(start, width):
    return (slice(None), slice(None), slice(None), pl.ds(start, width))


def put_square(slot, part, lanes, value):
    value = value.reshape(RING, RING, ROWS_OWN, value.shape[-1])
    if part == 1:
        slot[:, :, :, lanes] = value
    else:
        for place in range(RING):
            slot[:, place, :, lanes] = value[place]


def hidden_back(finish_weight, emit, c_ref, a3_ref, gains_ref, gate_ref, up_ref, wg, wu, wd):
    total = jnp.zeros(ALL_TOKENS, jnp.float32)
    finish_weight("down")
    for index in range(CHUNKS):
        lanes = pl.ds(index * CHUNK, CHUNK)
        grad = product(c_ref[...], wd[pl.ds(4 * index, 4)].reshape(CHUNK, WIDE), 1, 1)
        bent, slope = gelu_parts(gate_ref[:, lanes])
        dgate = low(grad * up_ref[:, lanes] * slope)
        dup = low(grad * bent)
        finish_weight("gate" + str(index))
        total = total + product(dgate, wg[:, :, lanes].reshape(WIDE, CHUNK), 1, 1)
        finish_weight("up" + str(index))
        total = total + product(dup, wu[:, :, lanes].reshape(WIDE, CHUNK), 1, 1)
        emit(index, lanes, dgate, dup)
    back, dgain = norm_back(total, a3_ref[...], gains_ref[2:3])
    return c_ref[...].astype(jnp.float32) + back, dgain


def cross_back(
    stream, finish_weight, gains_ref, a2_ref, cq_ref, ck_ref, cv_ref, cp_ref, wcq, wco,
    dc_ref, dcq_ref, dck_ref, dcv_ref,
):
    own = same_head()
    own_low = low(own)
    dc_ref[...] = low(stream)
    finish_weight("co")
    datt = low(product(dc_ref[...], square(wco), 1, 1))
    for row in range(BATCHES):
        part = pl.ds(TOKENS * row, TOKENS)
        keys = pl.ds(STATES * row, STATES)
        for group in range(GROUPS):
            lanes = pl.ds(GROUP * group, GROUP)
            left = GROUP * group
            dout = spread_heads(
                datt[TOKENS * row : TOKENS * (row + 1), left : left + GROUP], own_low
            )
            spread = spread_heads(cq_ref[part, lanes], own_low)
            chance = cp_ref[row, lanes]
            dchance = product(dout, cv_ref[keys, lanes], 1, 1)
            dcv_ref[keys, lanes] = low(product(low(chance), dout, 0, 0))
            inner = jnp.sum(chance * dchance, axis=-1, keepdims=True)
            dscore = low(chance * (dchance - inner))
            dcq_ref[part, lanes] = low(fold_heads(product(dscore, ck_ref[keys, lanes]), own))
            dck_ref[keys, lanes] = low(product(dscore, spread, 0, 0))
    finish_weight("cq")
    grad = product(dcq_ref[...], square(wcq), 1, 1)
    back, dgain = norm_back(grad, a2_ref[...], gains_ref[1:2])
    return stream + back, dgain


def self_back(
    stream, finish_weight, gains_ref, x_ref, q_ref, k_ref, v_ref, p_ref, wq, wk, wv, wo,
    dself_ref, dq_ref, dk_ref, dv_ref, dscore_ref,
):
    own = same_head()
    own_low = low(own)
    dself_ref[...] = low(stream)
    finish_weight("o")
    datt = low(product(dself_ref[...], square(wo), 1, 1))
    for row in range(BATCHES):
        part = pl.ds(TOKENS * row, TOKENS)
        for group in range(GROUPS):
            lanes = pl.ds(GROUP * group, GROUP)
            left = GROUP * group
            dout = spread_heads(
                datt[TOKENS * row : TOKENS * (row + 1), left : left + GROUP], own_low
            )
            spread = spread_heads(q_ref[part, lanes], own_low)
            chance = p_ref[row, lanes]
            dchance = product(dout, v_ref[part, lanes], 1, 1)
            dv_ref[part, lanes] = low(product(low(chance), dout, 0, 0))
            inner = jnp.sum(chance * dchance, axis=-1, keepdims=True)
            dscore = low(chance * (dchance - inner))
            if dscore_ref is not None:
                if row == 0:
                    dscore_ref[lanes] = dscore.astype(jnp.float32)
                else:
                    dscore_ref[lanes] += dscore.astype(jnp.float32)
            dq_ref[part, lanes] = low(fold_heads(product(dscore, k_ref[part, lanes]), own))
            dk_ref[part, lanes] = low(product(dscore, spread, 0, 0))
    finish_weight("q")
    grad = product(dq_ref[...], square(wq), 1, 1)
    finish_weight("k")
    grad = grad + product(dk_ref[...], square(wk), 1, 1)
    finish_weight("v")
    grad = grad + product(dv_ref[...], square(wv), 1, 1)
    back, dgain = norm_back(grad, x_ref[...].astype(jnp.float32), gains_ref[0:1])
    return stream + back, dgain


def hidden_kernel(
    c_ref, a3_ref, gains_ref, gate_ref, up_ref, n3_ref, hid_ref, weight,
    stream_ref, dgain_ref, keep, send,
    wg, wu, wd, gg, gu, gd0, gd1, sems, out_sems,
):
    copies = weight_copies(weight, dict(gate=wg, up=wu, down=wd), sems)
    begin(copies, ("down", "gate0", "up0", *LATE_HIDDEN))
    sent = []

    def finish_weight(name):
        finish(copies, name)

    for index in range(RING):
        lanes = pl.ds(index * CHUNK, CHUNK)
        grad = low(product(hid_ref[:, lanes], c_ref[...], 0, 0))
        grad = grad.reshape(RING, FF // PARTS, WIDE)
        gd0[:, index] = grad[:, : FF // PARTS // 2]
        gd1[index] = grad[:, FF // PARTS // 2 :]
    for part, tall in enumerate((gd0, gd1)):
        for piece in range(GROUPS):
            for block in range(4):
                source = tall.at[:, :, pl.ds(16 * block, 16), pl.ds(GROUP * piece, GROUP)]
                window = (
                    slice(None),
                    slice(None),
                    pl.ds(16 * piece, 16),
                    pl.ds(FF + GROUP * block, GROUP),
                )
                sent.append(push(source, keep, send, part, window, out_sems.at[len(sent)]))

    def emit(index, lanes, dgate, dup):
        for part, slot, grad in ((0, gg, dgate), (1, gu, dup)):
            put_square(slot, part, lanes, low(product(n3_ref[...], grad, 0, 0)))
            window = columns(index * CHUNK, CHUNK)
            sent.append(
                push(slot.at[window], keep, send, part, window, out_sems.at[len(sent)])
            )

    stream, dgain = hidden_back(
        finish_weight, emit, c_ref, a3_ref, gains_ref, gate_ref, up_ref, wg, wu, wd
    )
    stream_ref[...] = stream
    dgain_ref[...] = dgain
    for copy in sent:
        copy.wait()


def cross_kernel(
    stream_ref, gains_ref, a2_ref, cq_ref, ck_ref, cv_ref, cp_ref, weight,
    next_ref, dgain_ref, dc_ref, dcq_ref, dck_ref, dcv_ref,
    wcq, wco, sems,
):
    copies = weight_copies(weight, dict(cq=wcq, co=wco), sems)
    begin(copies, ("co", "cq"))

    def finish_weight(name):
        finish(copies, name)

    stream, dgain = cross_back(
        stream_ref[...], finish_weight, gains_ref, a2_ref, cq_ref, ck_ref, cv_ref, cp_ref,
        wcq, wco, dc_ref, dcq_ref, dck_ref, dcv_ref,
    )
    next_ref[...] = stream
    dgain_ref[...] = dgain


def self_kernel(
    stream_ref, x_ref, gains_ref, q_ref, k_ref, v_ref, p_ref,
    enc_ref, n1_ref, o_ref, n2_ref, co_ref, dc_ref, dcq_ref, dck_ref, dcv_ref, weight,
    da_ref, dgain_ref, dscore_ref, denc_ref, keep, send,
    dself_ref, dq_ref, dk_ref, dv_ref,
    wq, wk, wv, wo, wck, wcv, g0, g1, g2, g3, g4, g5, g6, g7, sems, out_sems,
):
    slots = dict(q=wq, k=wk, v=wv, o=wo, ck=wck, cv=wcv)
    copies = weight_copies(weight, slots, sems)
    begin(copies, ("o", "q", "k", "v", "ck", "cv"))

    def finish_weight(name):
        finish(copies, name)

    sent = []

    def emit(slot, part, column, left, right):
        put_square(slot, part, slice(None), low(product(left[...], right[...], 0, 0)))
        window = columns(WIDE * column, WIDE)
        sent.append(push(slot, keep, send, part, window, out_sems.at[len(sent)]))

    emit(g0, 0, 0, co_ref, dc_ref)
    emit(g1, 0, 1, n2_ref, dcq_ref)
    emit(g2, 1, 0, enc_ref, dck_ref)
    emit(g3, 1, 1, enc_ref, dcv_ref)
    stream, dgain = self_back(
        stream_ref[...], finish_weight, gains_ref, x_ref, q_ref, k_ref, v_ref, p_ref,
        wq, wk, wv, wo, dself_ref, dq_ref, dk_ref, dv_ref, dscore_ref,
    )
    da_ref[...] = low(stream)
    dgain_ref[...] = dgain
    emit(g4, 0, 2, o_ref, dself_ref)
    emit(g5, 0, 3, n1_ref, dq_ref)
    emit(g6, 1, 2, n1_ref, dk_ref)
    emit(g7, 1, 3, n1_ref, dv_ref)
    finish(copies, "ck")
    finish(copies, "cv")
    for row in range(BATCHES):
        keys = pl.ds(STATES * row, STATES)
        denc_ref[keys] = low(
            product(dck_ref[keys], square(wck), 1, 1) + product(dcv_ref[keys], square(wcv), 1, 1)
        )
    for copy in sent:
        copy.wait()


def in_vmem(count):
    return [pl.BlockSpec(memory_space=pltpu.VMEM)] * count


def held(*shapes):
    return [pltpu.VMEM(shape, jnp.bfloat16) for shape in shapes]


def shape_of(dims, kind=jnp.bfloat16):
    return jax.ShapeDtypeStruct(dims, kind)


params = pltpu.CompilerParams(vmem_limit_bytes=VMEM_BYTES)


ANYWHERE = pl.BlockSpec(memory_space=pl.ANY)
DMAS = pltpu.SemaphoreType.DMA((40,))
SAVED = (
    (ALL_TOKENS, jnp.bfloat16),
    (ALL_TOKENS, jnp.bfloat16),
    (ALL_TOKENS, jnp.bfloat16),
    (ALL_TOKENS, jnp.bfloat16),
    ((BATCHES, WIDE, TOKENS), jnp.float32),
    (ALL_TOKENS, jnp.bfloat16),
    (ALL_TOKENS, jnp.float32),
    (ALL_TOKENS, jnp.bfloat16),
    (ALL_TOKENS, jnp.bfloat16),
    ((BATCHES, WIDE, STATES), jnp.float32),
    (ALL_TOKENS, jnp.bfloat16),
    (ALL_TOKENS, jnp.float32),
    (ALL_TOKENS, jnp.bfloat16),
    (HIDDEN, jnp.float32),
    (HIDDEN, jnp.float32),
    (HIDDEN, jnp.bfloat16),
)


def run_first(x, enc, self_add, cross_add, gains, weight):
    outs = [shape_of(ALL_TOKENS), shape_of(ALL_STATES), shape_of(ALL_STATES)]
    return pl.pallas_call(
        first_kernel,
        out_shape=outs,
        in_specs=in_vmem(5) + [pl.BlockSpec(memory_space=pl.ANY)],
        out_specs=in_vmem(len(outs)),
        scratch_shapes=[pltpu.VMEM(dims, kind) for dims, kind in SAVED]
        + held(*[FULL] * 8, GATED, GATED, DOWN)
        + [pltpu.SemaphoreType.DMA((40,))],
        compiler_params=params,
        name="first_forward",
    )(x, enc, self_add, cross_add, gains, weight)


def run_turn(x, ck, cv, self_add, cross_add, gains, cotangent, weight):
    saved = [shape_of(dims, kind) for dims, kind in SAVED]
    return pl.pallas_call(
        turn_kernel,
        out_shape=[shape_of(ALL_TOKENS)] * 2 + saved,
        in_specs=in_vmem(7) + [ANYWHERE],
        out_specs=in_vmem(2) + [ANYWHERE] * len(saved),
        scratch_shapes=[pltpu.VMEM(dims, kind) for dims, kind in SAVED]
        + held(ALL_TOKENS, ALL_TOKENS, ALL_STATES, ALL_STATES, *[ALL_TOKENS] * 4)
        + held(*[FULL] * 6, GATED, GATED, DOWN)
        + [DMAS, DMAS],
        compiler_params=params,
        name="forward_and_back",
    )(x, ck, cv, self_add, cross_add, gains, cotangent, weight)


HALF = (RING, RING, ROWS_OWN, ATT // 2)
RINGED = (RING, RING, ROWS_OWN, WIDE)
RINGED_WIDE = (RING, RING, ROWS_OWN, FF)
RINGED_TALL = (RING, RING, FF // PARTS // 2, WIDE)


def run_hidden(cotangent, gains, saved, weight):
    (ck, cv, n1, q, k, v, p, o, a2, n2, cq, cp, co, a3, n3, gate, up, hid) = saved
    return pl.pallas_call(
        hidden_kernel,
        out_shape=[
            shape_of(ALL_TOKENS, jnp.float32),
            shape_of((1, WIDE), jnp.float32),
            shape_of(HALF),
            shape_of(HALF),
        ],
        in_specs=in_vmem(7) + [ANYWHERE],
        out_specs=in_vmem(2) + [ANYWHERE, ANYWHERE],
        scratch_shapes=held(
            GATED, GATED, DOWN, RINGED_WIDE, RINGED_WIDE, RINGED_TALL, RINGED_TALL
        )
        + [DMAS, DMAS],
        compiler_params=params,
        name="hidden_backward",
    )(cotangent, a3, gains, gate, up, n3, hid, weight)


def run_cross(stream, gains, saved, weight):
    (ck, cv, n1, q, k, v, p, o, a2, n2, cq, cp, co, a3, n3, gate, up, hid) = saved
    return pl.pallas_call(
        cross_kernel,
        out_shape=[
            shape_of(ALL_TOKENS, jnp.float32),
            shape_of((1, WIDE), jnp.float32),
            shape_of(ALL_TOKENS),
            shape_of(ALL_TOKENS),
            shape_of(ALL_STATES),
            shape_of(ALL_STATES),
        ],
        in_specs=in_vmem(7) + [ANYWHERE],
        out_specs=in_vmem(6),
        scratch_shapes=held(FULL, FULL) + [DMAS],
        compiler_params=params,
        name="cross_backward",
    )(stream, gains, a2, cq, ck, cv, cp, weight)


def run_self(stream, x, gains, enc, saved, records, weight):
    (ck, cv, n1, q, k, v, p, o, a2, n2, cq, cp, co, a3, n3, gate, up, hid) = saved
    return pl.pallas_call(
        self_kernel,
        out_shape=[
            shape_of(ALL_TOKENS),
            shape_of((1, WIDE), jnp.float32),
            shape_of((WIDE, TOKENS), jnp.float32),
            shape_of(ALL_STATES),
            shape_of(HALF),
            shape_of(HALF),
        ],
        in_specs=in_vmem(16) + [ANYWHERE],
        out_specs=in_vmem(4) + [ANYWHERE, ANYWHERE],
        scratch_shapes=held(*[ALL_TOKENS] * 4, *[FULL] * 6, *[RINGED] * 8) + [DMAS, DMAS],
        compiler_params=params,
        name="self_backward",
    )(stream, x, gains, q, k, v, p, enc, n1, o, n2, co, *records, weight)


def pack_kernel(
    query_ref, kv_ref, out_ref, c_query_ref, c_kv_ref, c_out_ref, in_ref, ffn_ref, kept, given
):
    def attention(target):
        start = 0
        for ref in (query_ref, kv_ref, out_ref, c_query_ref, c_kv_ref, c_out_ref):
            if len(ref.shape) == 3:
                pair = ref[...].astype(jnp.float32)
                members = [low(pair[:, 0, :]), low(pair[:, 1, :])]
            else:
                members = [ref[...]]
            for member in members:
                target[:, start : start + WIDE] = member
                start += WIDE

    def hidden(target):
        pair = in_ref[...].astype(jnp.float32)
        target[:, :FF] = low(pair[:, 0, :])
        target[:, FF : 2 * FF] = low(pair[:, 1, :])
        for piece, block in DOWN_PIECES:
            lanes = pl.ds(2 * FF + GROUP * block, GROUP)
            target[pl.ds(16 * piece, 16), lanes] = ffn_ref[
                pl.ds(16 * block, 16), pl.ds(GROUP * piece, GROUP)
            ]

    @pl.when(core_is(0))
    def _():
        attention(kept)
        hidden(given)

    @pl.when(core_is(1))
    def _():
        hidden(kept)
        attention(given)


def run_pack(members):
    return pl.pallas_call(
        pack_kernel,
        out_shape=[shape_of((ROWS_OWN, ATT))] * 2,
        in_specs=in_vmem(8),
        out_specs=in_vmem(2),
        compiler_params=params,
        name="pack_weights",
    )(*members)


def add_kernel(left, right, total):
    total[...] = low(left[...].astype(jnp.float32) + right[...].astype(jnp.float32))


def add_halves(keep, received):
    dims = (WIDE, ATT // 2)
    spec = pl.BlockSpec((256, ATT // 2), lambda place: (place, 0))
    return pl.pallas_call(
        add_kernel,
        out_shape=shape_of(dims),
        grid=(3,),
        in_specs=[spec, spec],
        out_specs=spec,
        compiler_params=params,
        name="add_halves",
    )(keep.reshape(dims), received.reshape(dims))


def unpack_kernel(
    mine, theirs, query_ref, kv_ref, out_ref, c_query_ref, c_kv_ref, c_out_ref, in_ref, ffn_ref
):
    def write(first, second):
        def square_at(part, place):
            start = ATT // 2 + WIDE * place
            return part[:, start : start + WIDE].astype(jnp.float32)

        c_out_ref[...] = square_at(first, 0)
        c_query_ref[...] = square_at(first, 1)
        out_ref[...] = square_at(first, 2)
        query_ref[...] = square_at(first, 3)
        c_kv_ref[:, 0, :] = square_at(second, 0)
        c_kv_ref[:, 1, :] = square_at(second, 1)
        kv_ref[:, 0, :] = square_at(second, 2)
        kv_ref[:, 1, :] = square_at(second, 3)
        for index, part in enumerate((first, second)):
            in_ref[:, index, :] = part[:, :FF].astype(jnp.float32)
            for piece in range(GROUPS):
                for block in range(4):
                    rows = pl.ds(64 * index + 16 * block, 16)
                    taken = part[pl.ds(16 * piece, 16), pl.ds(FF + GROUP * block, GROUP)]
                    ffn_ref[rows, pl.ds(GROUP * piece, GROUP)] = taken.astype(jnp.float32)

    @pl.when(core_is(0))
    def _():
        write(mine, theirs)

    @pl.when(core_is(1))
    def _():
        write(theirs, mine)


def run_unpack(mine, theirs):
    wide = jnp.float32
    square_dims, pair_dims = (ROWS_OWN, WIDE), (ROWS_OWN, 2, WIDE)
    outs = [square_dims, pair_dims, square_dims, square_dims, pair_dims, square_dims]
    outs += [(ROWS_OWN, 2, FF), (FF // PARTS, WIDE)]
    return pl.pallas_call(
        unpack_kernel,
        out_shape=[shape_of(dims, wide) for dims in outs],
        in_specs=in_vmem(2),
        out_specs=in_vmem(8),
        compiler_params=pltpu.CompilerParams(vmem_limit_bytes=10 * 1024 * 1024),
        name="unpack_gradients",
    )(mine, theirs)


def score_terms(table, dec_ids, enc_ids):
    positions = jnp.arange(TOKENS)
    by_distance = jnp.dot(table.astype(jnp.float32).T, bucket_onehot(TOKENS), precision=highest)
    bias = spread_distance(by_distance)
    allowed = (dec_ids[:, :, None] == dec_ids[:, None, :]) & (
        positions[None, :] <= positions[:, None]
    )
    self_add = jnp.where(allowed[:, None], bias[None], -jnp.inf)
    cross_add = jnp.where(dec_ids[:, :, None] == enc_ids[:, None, :], 0.0, -jnp.inf)
    return self_add.reshape(BATCHES, WIDE, TOKENS), cross_add


def shards(
    layer_in,
    cotangent,
    encoder,
    dec_segments,
    enc_segments,
    norm_gains,
    self_query,
    self_kv,
    self_out,
    rel_bias,
    cross_query,
    cross_kv,
    cross_out,
    ffn_in,
    ffn_out,
):
    core = lax.axis_index("section")
    part_index = lax.axis_index("fsdp")
    plane = lax.axis_index("rep")
    planes = lax.axis_size("rep")
    layer = lax.rem(plane, 2)
    first_core = core == 0
    at_home = core == layer

    def place(core_index, plane_index):
        return core_index * planes + plane_index

    def flip_core(value):
        return lax.ppermute(value, "section", [(0, 1), (1, 0)])

    def from_home(value):
        pairs = [(place(p % 2, p), place(1 - p % 2, p)) for p in range(planes)]
        return jnp.where(at_home, value, lax.ppermute(value, ("section", "rep"), pairs))

    def beside(value):
        return lax.ppermute(value, "rep", [(p, p ^ 1) for p in range(planes)])

    def to_home(value):
        pairs = [(place(1 - p % 2, p), place(1 - p % 2, p ^ 1)) for p in range(planes)]
        return lax.ppermute(value, ("section", "rep"), pairs)

    def rows_for_layer(value):
        pairs = [(place(p % 2, p), place(p % 2, p ^ 1)) for p in range(planes)]
        return jnp.where(at_home, value, lax.ppermute(value, ("section", "rep"), pairs))

    def rows_back(value):
        pairs = [(place(1 - p % 2, p), place(p % 2, p ^ 1)) for p in range(planes)]
        return jnp.where(at_home, value, lax.ppermute(value, ("section", "rep"), pairs))

    def between_layers(value, steps):
        pairs = [(p, p + steps) for p in range(planes) if p % 2 == (steps < 0)]
        return lax.ppermute(value, "rep", pairs)

    along_z = [[RING * x + z for z in range(RING)] for x in range(RING)]
    along_x = [[RING * x + z for x in range(RING)] for z in range(RING)]
    first_rings = along_z + [[PARTS + d for d in ring] for ring in along_x]
    second_rings = along_x + [[PARTS + d for d in ring] for ring in along_z]

    def scatter(value, rings):
        return lax.psum_scatter(
            value, ("section", "fsdp"), scatter_dimension=0, axis_index_groups=rings, tiled=True
        )

    kept, given_away = run_pack(
        [
            member[0]
            for member in (
                self_query,
                self_kv,
                self_out,
                cross_query,
                cross_kv,
                cross_out,
                ffn_in,
                ffn_out,
            )
        ]
    )
    half = jnp.where(at_home, kept, flip_core(given_away))
    weight = lax.all_gather(half, ("fsdp", "section"), axis=0, tiled=True)
    weight = weight.reshape(PARTS, 2, ROWS_OWN, ATT)
    small = jnp.zeros((8, 128), jnp.bfloat16)
    small = small.at[:3, :ROWS_OWN].set(norm_gains[0])
    small = small.at[3:5, :HEADS].set(rel_bias[0])
    small = lax.all_gather(from_home(small), "fsdp", axis=0, tiled=False)
    gains = small[:, :3, :ROWS_OWN].transpose(1, 0, 2).reshape(3, WIDE).astype(jnp.float32)
    table = small[:, 3:5, :HEADS].reshape(BUCKETS, HEADS)
    ids = jnp.concatenate([dec_segments[:, 0], enc_segments[:, 0]], axis=1)
    ids = rows_for_layer(ids)
    self_add, cross_add = score_terms(table, ids[:, :TOKENS], ids[:, TOKENS:])
    ends = jnp.stack([layer_in[:, 0].reshape(ALL_TOKENS), cotangent[:, 0].reshape(ALL_TOKENS)])
    ends = rows_for_layer(ends)
    rows_in, given = ends[0], ends[1]
    enc = rows_for_layer(encoder[:, 0].reshape(ALL_STATES))
    weight, rows_in, given, enc, self_add, cross_add, gains = lax.optimization_barrier(
        (weight, rows_in, given, enc, self_add, cross_add, gains)
    )
    first, ck, cv = run_first(rows_in, enc, self_add, cross_add, gains, weight)
    current = jnp.where(layer == 0, rows_in, between_layers(first, 1))
    result, grad_first, *saved = run_turn(
        current, ck, cv, self_add, cross_add, gains, given, weight
    )
    saved = [ck, cv] + saved
    incoming = jnp.where(layer == 1, given, between_layers(grad_first, -1))
    stream, gain_three, keep, send = run_hidden(incoming, gains, saved, weight)
    received = flip_core(send)
    stream, gain_two, *records = run_cross(stream, gains, saved, weight)
    wide_sum = add_halves(keep, received)
    wide_sum, stream = lax.optimization_barrier((wide_sum, stream))
    wide_part = scatter(wide_sum, first_rings)
    grad_input, gain_one, grad_scores, grad_enc, keep, send = run_self(
        stream, current, gains, enc, saved, records, weight
    )
    square_part = scatter(add_halves(keep, flip_core(send)), first_rings)
    grad_gains = jnp.concatenate([gain_one, gain_two, gain_three], axis=0)
    diagonal_sums = gather_distance(grad_scores.reshape(HEADS, TOKENS, TOKENS))
    grad_table = jnp.dot(bucket_onehot(TOKENS), diagonal_sums.T, precision=highest)
    little = jnp.zeros((8, WIDE), jnp.float32)
    little = little.at[:3].set(grad_gains)
    little = little.at[3, : BUCKETS * HEADS].set(grad_table.reshape(-1))

    def add_pairs(value, axis, bits):
        for bit in bits:
            pairs = [(index, index ^ bit) for index in range(lax.axis_size(axis))]
            value = value + lax.ppermute(value, axis, pairs)
        return value

    little = add_pairs(add_pairs(little, "section", (1,)), "fsdp", (1, 2, 4, 8))
    outs = rows_back(jnp.stack([result, grad_input]))
    wide_part, square_part, little, outs, other_enc = lax.optimization_barrier(
        (wide_part, square_part, little, outs, to_home(grad_enc))
    )
    partial = scatter(jnp.concatenate([wide_part, square_part], axis=1), second_rings)
    little = add_pairs(little, "rep", (2,))
    little = jnp.where(at_home, little, beside(little))
    own_gains = lax.dynamic_slice(little, (0, part_index * ROWS_OWN), (3, ROWS_OWN))
    own_table = lax.dynamic_slice(little, (3, part_index * 2 * HEADS), (1, 2 * HEADS))
    encoder_total = grad_enc.astype(jnp.float32) + other_enc.astype(jnp.float32)
    encoder_total = from_home(encoder_total)
    own_table = own_table.reshape(2, HEADS)
    results = (
        outs[0].reshape(1, BATCHES, 1, TOKENS, WIDE),
        outs[1].reshape(1, BATCHES, 1, TOKENS, WIDE),
        encoder_total.reshape(BATCHES, 1, STATES, WIDE),
        own_gains[None],
        own_table[None],
    )
    partial, results = lax.optimization_barrier((partial, results))
    up = [(p, (p + 1) % planes) for p in range(planes)]
    down = [(p, (p - 1) % planes) for p in range(planes)]
    across = [(p, (p + 2) % planes) for p in range(planes)]
    cut = ATT // 2
    outer = (plane == 0) | (plane == planes - 1)
    lower = plane < 2
    rising = lax.ppermute(jnp.where(outer, partial[:, :cut], partial[:, cut:]), "rep", up)
    falling = lax.ppermute(jnp.where(outer, partial[:, cut:], partial[:, :cut]), "rep", down)
    here = low(rising.astype(jnp.float32) + falling.astype(jnp.float32))
    below = lax.ppermute(here, "rep", up)
    above = lax.ppermute(here, "rep", down)
    beyond = lax.ppermute(here, "rep", across)
    own_layer = (jnp.where(outer, above, below), jnp.where(outer, below, above))
    other_layer = (jnp.where(lower, here, beyond), jnp.where(lower, beyond, here))
    pairs = list(zip(own_layer, other_layer))
    mine = jnp.concatenate([jnp.where(at_home, own, other) for own, other in pairs], axis=1)
    away = jnp.concatenate([jnp.where(at_home, other, own) for own, other in pairs], axis=1)
    query, kv, out, *others = [member[None] for member in run_unpack(mine, flip_core(away))]
    return (*results[:4], query, kv, out, results[4], *others)


def solution(mesh):
    return jax.shard_map(
        shards,
        mesh=mesh,
        in_specs=(
            P(None, ("fsdp", "rep"), None, None),
            P(None, ("fsdp", "rep"), None, None),
            P(None, ("fsdp", "rep"), None, None),
            P(None, ("fsdp", "rep"), None),
            P(None, ("fsdp", "rep"), None),
            P("section", None, "fsdp"),
            P("section", "fsdp", None),
            P("section", "fsdp", None, None),
            P("section", "fsdp", None),
            P("section", "fsdp", None),
            P("section", "fsdp", None),
            P("section", "fsdp", None, None),
            P("section", "fsdp", None),
            P("section", "fsdp", None, None),
            P("section", "fsdp", None),
        ),
        out_specs=(
            P("section", None, ("fsdp", "rep"), None, None),
            P("section", None, ("fsdp", "rep"), None, None),
            P(None, ("fsdp", "rep"), None, None),
            P("section", None, "fsdp"),
            P("section", "fsdp", None),
            P("section", "fsdp", None, None),
            P("section", "fsdp", None),
            P("section", "fsdp", None),
            P("section", "fsdp", None),
            P("section", "fsdp", None, None),
            P("section", "fsdp", None),
            P("section", "fsdp", None, None),
            P("section", "fsdp", None),
        ),
        check_vma=False,
    )
```

```python
import jax
import jax.numpy as jnp
import numpy as np
from jax import lax
from jax.experimental import pallas as pl
from jax.experimental.pallas import tpu as pltpu
from jax.sharding import PartitionSpec as P

HEADS = 12
HEAD = 64
BUCKETS = 32
MAX_DIST = 128
PARTS = 16
GELU_SCALE = float(np.sqrt(2.0 / np.pi))


epsilon = 1e-06
highest = lax.Precision.HIGHEST


def bucket_row(length):
    distance = np.arange(length)
    half_count = BUCKETS // 2
    scaled = (
        np.log(np.maximum(distance, half_count) / half_count)
        / np.log(MAX_DIST / half_count)
        * (BUCKETS - half_count)
    )
    far_bucket = np.minimum(half_count + np.floor(scaled).astype(np.int32), BUCKETS - 1)
    return np.where(distance < half_count, distance, far_bucket).astype(np.int32)


def bucket_onehot(length):
    return (bucket_row(length)[None, :] == np.arange(BUCKETS)[:, None]).astype(np.float32)


def spread_distance(by_distance):
    head_count, length = by_distance.shape
    padded_row = jnp.concatenate(
        [jnp.zeros((head_count, length - 1), jnp.float32), by_distance], axis=1
    )
    tiled = jnp.tile(padded_row, (1, length))
    tiled = jnp.concatenate([tiled, jnp.zeros((head_count, length), jnp.float32)], axis=1)
    return tiled.reshape(head_count, length, 2 * length)[:, :, :length][:, :, ::-1]


def gather_distance(grid):
    head_count, length, _ = grid.shape
    flipped = jnp.concatenate(
        [grid[:, :, ::-1], jnp.zeros((head_count, length, length), jnp.float32)], axis=2
    )
    flat = flipped.reshape(head_count, 2 * length * length)[:, : length * (2 * length - 1)]
    return jnp.sum(flat.reshape(head_count, length, 2 * length - 1), axis=1)[:, length - 1 :]


ROWS_OWN = 48
TOKENS = 64
WIDE = 768
FF = 2048
GROUP = 256
GROUPS = 3
BATCHES = 2
STATES = 256
CHUNK = 512
TALL = FF // PARTS // 2
SHARE = FF + 4 * WIDE
SMALL = 16
CHUNKS = FF // CHUNK
ATT = 6144
ALL_TOKENS = (BATCHES * TOKENS, WIDE)
ALL_STATES = (BATCHES * STATES, WIDE)
HIDDEN = (BATCHES * TOKENS, FF)
VMEM_BYTES = 60 * 1024 * 1024
FULL = (PARTS, ROWS_OWN, WIDE)
GATED = (PARTS, ROWS_OWN, FF)
DOWN = (PARTS, FF // PARTS, WIDE)
RING = 4
LATE_HIDDEN = [name + str(index) for index in range(1, CHUNKS) for name in ("gate", "up")]


def product(left, right, along_left=1, along_right=0):
    return lax.dot_general(
        left,
        right,
        (((along_left,), (along_right,)), ((), ())),
        preferred_element_type=jnp.float32,
    )


def low(value):
    return value.astype(jnp.bfloat16)


def same_head():
    row = lax.broadcasted_iota(jnp.int32, (GROUP, GROUP), 0) // HEAD
    lane = lax.broadcasted_iota(jnp.int32, (GROUP, GROUP), 1) // HEAD
    return jnp.where(row == lane, 1.0, 0.0)


def spread_heads(block, own_low):
    return jnp.concatenate([block] * 4, axis=0) * own_low


def fold_heads(block, own):
    kept = block * own
    return kept[:64] + kept[64:128] + kept[128:192] + kept[192:]


def scale_of(value):
    return lax.rsqrt(jnp.mean(value * value, axis=-1, keepdims=True) + epsilon)


def norm_back(grad, value, gain):
    scale = scale_of(value)
    carried = grad * gain
    mean = jnp.mean(value * carried, axis=-1, keepdims=True)
    grad_value = carried * scale - value * (scale * scale * scale) * mean
    grad_gain = jnp.sum(grad * value * scale, axis=0, keepdims=True)
    return grad_value, grad_gain


def square(ref):
    return ref[...].reshape(WIDE, WIDE)


class Either:
    def __init__(self, part, near, far):
        self.part, self.near, self.far = part, near, far

    def start(self):
        @pl.when(core_is(self.part))
        def _():
            self.near.start()

        @pl.when(jnp.logical_not(core_is(self.part)))
        def _():
            self.far.start()

    def wait(self):
        self.near.wait()


def softmax_rows(scores):
    raised = jnp.exp(scores - jnp.max(scores, axis=-1, keepdims=True))
    return raised / jnp.sum(raised, axis=-1, keepdims=True)


def gelu_parts(gate):
    cube = gate * gate * gate
    bent = jnp.tanh(GELU_SCALE * (gate + 0.044715 * cube))
    half = 0.5 * (1.0 + bent)
    slope = half + 0.5 * gate * (1.0 - bent * bent) * GELU_SCALE * (
        1.0 + 3.0 * 0.044715 * gate * gate
    )
    return gate * half, slope


def down_copies(near, far, slot, sems):
    device = lax.axis_index("fsdp")
    here_x, here_z = lax.div(device, RING), lax.rem(device, RING)
    copies = []
    for part in range(2):
        for back_z in range(RING):
            for back_x in range(RING):
                from_x = lax.rem(here_x - back_x + RING, RING)
                from_z = lax.rem(here_z - back_z + RING, RING)
                target = slot.at[from_x * RING + from_z, pl.ds(TALL * part, TALL)]
                sem = sems.at[8 + 2 * CHUNKS + len(copies)]
                pair = [
                    pltpu.make_async_copy(
                        source.at[back_z, back_x, pl.ds(0, TALL)], target, sem
                    )
                    for source in (near, far)
                ]
                copies.append(Either(part, *pair))
    return copies


def weight_copies(weight, slots, sems, sides=None):
    copies = {}
    for place, name in enumerate(("q", "k", "v", "o", "cq", "ck", "cv", "co")):
        if name in slots:
            lanes = pl.ds(FF + WIDE * (place % 4), WIDE)
            source = weight.at[:, place // 4, :, lanes]
            copies[name] = [pltpu.make_async_copy(source, slots[name], sems.at[place])]
    for place, name in enumerate(("gate", "up")):
        if name in slots:
            for index in range(CHUNKS):
                lanes = pl.ds(CHUNK * index, CHUNK)
                source = weight.at[:, place, :, lanes]
                target = slots[name].at[:, :, lanes]
                sem = sems.at[8 + CHUNKS * place + index]
                copies[name + str(index)] = [pltpu.make_async_copy(source, target, sem)]
    if "down" in slots:
        copies["down"] = down_copies(*sides, slots["down"], sems)
    return copies


def begin(copies, names):
    for name in names:
        for copy in copies[name]:
            copy.start()


def finish(copies, name):
    for copy in copies[name]:
        copy.wait()


def forward_body(
    keys_given,
    x_ref,
    enc_ref,
    self_add_ref,
    cross_add_ref,
    gains_ref,
    weight,
    out_ref,
    n1_ref,
    q_ref,
    k_ref,
    v_ref,
    p_ref,
    o_ref,
    a2_ref,
    n2_ref,
    cq_ref,
    ck_ref,
    cv_ref,
    cp_ref,
    co_ref,
    a3_ref,
    n3_ref,
    gate_ref,
    up_ref,
    hid_ref,
    wq,
    wk,
    wv,
    wo,
    wcq,
    wck,
    wcv,
    wco,
    wg,
    wu,
    wd,
    sems,
):
    slots = dict(q=wq, k=wk, v=wv, o=wo, cq=wcq, co=wco, gate=wg, up=wu, down=wd)
    if not keys_given:
        slots.update(ck=wck, cv=wcv)
    copies = weight_copies(weight[0], slots, sems, weight[1:])
    if not keys_given:
        begin(copies, ("ck", "cv"))
    begin(copies, ("q", "k", "v", "o", "cq", "co", "gate0", "up0", "down", *LATE_HIDDEN))
    own = same_head()
    own_low = low(own)
    stream = x_ref[...].astype(jnp.float32)
    normed = low(stream * scale_of(stream) * gains_ref[0:1])
    n1_ref[...] = normed
    if not keys_given:
        for name, held_weight, target in (("ck", wck, ck_ref), ("cv", wcv, cv_ref)):
            finish(copies, name)
            for row in range(BATCHES):
                part = pl.ds(STATES * row, STATES)
                target[part] = low(product(enc_ref[part], square(held_weight)))
    finish(copies, "q")
    q_ref[...] = low(product(normed, square(wq)))
    finish(copies, "k")
    k_ref[...] = low(product(normed, square(wk)))
    finish(copies, "v")
    v_ref[...] = low(product(normed, square(wv)))
    for row in range(BATCHES):
        part = pl.ds(TOKENS * row, TOKENS)
        for group in range(GROUPS):
            lanes = pl.ds(GROUP * group, GROUP)
            spread = spread_heads(q_ref[part, lanes], own_low)
            scores = product(spread, k_ref[part, lanes], 1, 1) + self_add_ref[row, lanes]
            chance = softmax_rows(scores)
            p_ref[row, lanes] = chance
            mixed = product(low(chance), v_ref[part, lanes])
            o_ref[part, lanes] = low(fold_heads(mixed, own))
    finish(copies, "o")
    stream = stream + product(o_ref[...], square(wo))
    a2_ref[...] = stream
    normed = low(stream * scale_of(stream) * gains_ref[1:2])
    n2_ref[...] = normed
    finish(copies, "cq")
    cq_ref[...] = low(product(normed, square(wcq)))
    for row in range(BATCHES):
        part = pl.ds(TOKENS * row, TOKENS)
        keys = pl.ds(STATES * row, STATES)
        add = jnp.concatenate([cross_add_ref[row]] * 4, axis=0)
        for group in range(GROUPS):
            lanes = pl.ds(GROUP * group, GROUP)
            spread = spread_heads(cq_ref[part, lanes], own_low)
            scores = product(spread, ck_ref[keys, lanes], 1, 1) + add
            chance = softmax_rows(scores)
            cp_ref[row, lanes] = chance
            mixed = product(low(chance), cv_ref[keys, lanes])
            co_ref[part, lanes] = low(fold_heads(mixed, own))
    finish(copies, "co")
    stream = a2_ref[...] + product(co_ref[...], square(wco))
    a3_ref[...] = stream
    n3_ref[...] = low(stream * scale_of(stream) * gains_ref[2:3])
    total = a3_ref[...]
    for index in range(CHUNKS):
        lanes = pl.ds(index * CHUNK, CHUNK)
        rows = n3_ref[...]
        finish(copies, "gate" + str(index))
        gate = product(rows, wg[:, :, lanes].reshape(WIDE, CHUNK))
        finish(copies, "up" + str(index))
        up = product(rows, wu[:, :, lanes].reshape(WIDE, CHUNK))
        gate_ref[:, lanes] = gate
        up_ref[:, lanes] = up
        bent = 0.5 * (1.0 + jnp.tanh(GELU_SCALE * (gate + 0.044715 * (gate * gate * gate))))
        hidden = low(gate * bent * up)
        hid_ref[:, lanes] = hidden
        if index == 0:
            finish(copies, "down")
        total = total + product(hidden, wd[pl.ds(4 * index, 4)].reshape(CHUNK, WIDE))
    out_ref[...] = low(total)


def first_kernel(
    x_ref, enc_ref, self_add_ref, cross_add_ref, gains_ref, weight, near, far,
    out_ref, ck_ref, cv_ref, *rest,
):
    (n1, q, k, v, p, o, a2, n2, cq, cp, co, a3, n3, gate, up, hid, *scratch) = rest
    forward_body(
        False,
        x_ref, enc_ref, self_add_ref, cross_add_ref, gains_ref, (weight, near, far), out_ref,
        n1, q, k, v, p, o, a2, n2, cq, ck_ref, cv_ref, cp, co, a3, n3, gate, up, hid, *scratch,
    )


def turn_kernel(
    x_ref, ck_ref, cv_ref, self_add_ref, cross_add_ref, gains_ref, c_ref, weight, near, far,
    out_ref, da_ref, *rest,
):
    saved_out, saved, rest = rest[:16], rest[16:32], rest[32:]
    dc_ref, dcq_ref, dck_ref, dcv_ref, dself_ref, dq_ref, dk_ref, dv_ref, *rest = rest
    wq, wk, wv, wo, wcq, wco, wg, wu, wd, sems, out_sems = rest
    n1, q, k, v, p, o, a2, n2, cq, cp, co, a3, n3, gate, up, hid = saved
    forward_body(
        True,
        x_ref, None, self_add_ref, cross_add_ref, gains_ref, (weight, near, far), out_ref,
        n1, q, k, v, p, o, a2, n2, cq, ck_ref, cv_ref, cp, co, a3, n3, gate, up, hid,
        wq, wk, wv, wo, wcq, None, None, wco, wg, wu, wd, sems,
    )
    sent = [
        pltpu.make_async_copy(source, target, out_sems.at[place])
        for place, (source, target) in enumerate(zip(saved, saved_out))
    ]
    for copy in sent:
        copy.start()

    def finish_weight(name):
        return None

    def emit(index, lanes, dgate, dup):
        return None

    stream, _ = hidden_back(finish_weight, emit, c_ref, a3, gains_ref, gate, up, wg, wu, wd)
    stream, _ = cross_back(
        stream, finish_weight, gains_ref, a2, cq, ck_ref, cv_ref, cp, wcq, wco,
        dc_ref, dcq_ref, dck_ref, dcv_ref,
    )
    stream, _ = self_back(
        stream, finish_weight, gains_ref, x_ref, q, k, v, p, wq, wk, wv, wo,
        dself_ref, dq_ref, dk_ref, dv_ref, None,
    )
    da_ref[...] = low(stream)
    for copy in sent:
        copy.wait()


def core_is(part):
    return lax.axis_index("section") == part


def push(source, keep, send, part, window, sem):
    @pl.when(core_is(part))
    def _():
        pltpu.make_async_copy(source, keep.at[window], sem).start()

    @pl.when(jnp.logical_not(core_is(part)))
    def _():
        pltpu.make_async_copy(source, send.at[window], sem).start()

    return pltpu.make_async_copy(source, keep.at[window], sem)


def columns(start, width):
    return (slice(None), slice(None), slice(None), pl.ds(start, width))


def put_square(slot, part, lanes, value):
    value = value.reshape(RING, RING, ROWS_OWN, value.shape[-1])
    if part == 1:
        slot[:, :, :, lanes] = value
    else:
        for place in range(RING):
            slot[:, place, :, lanes] = value[place]


def hidden_back(finish_weight, emit, c_ref, a3_ref, gains_ref, gate_ref, up_ref, wg, wu, wd):
    total = jnp.zeros(ALL_TOKENS, jnp.float32)
    finish_weight("down")
    for index in range(CHUNKS):
        lanes = pl.ds(index * CHUNK, CHUNK)
        grad = product(c_ref[...], wd[pl.ds(4 * index, 4)].reshape(CHUNK, WIDE), 1, 1)
        bent, slope = gelu_parts(gate_ref[:, lanes])
        dgate = low(grad * up_ref[:, lanes] * slope)
        dup = low(grad * bent)
        finish_weight("gate" + str(index))
        total = total + product(dgate, wg[:, :, lanes].reshape(WIDE, CHUNK), 1, 1)
        finish_weight("up" + str(index))
        total = total + product(dup, wu[:, :, lanes].reshape(WIDE, CHUNK), 1, 1)
        emit(index, lanes, dgate, dup)
    back, dgain = norm_back(total, a3_ref[...], gains_ref[2:3])
    return c_ref[...].astype(jnp.float32) + back, dgain


def cross_back(
    stream, finish_weight, gains_ref, a2_ref, cq_ref, ck_ref, cv_ref, cp_ref, wcq, wco,
    dc_ref, dcq_ref, dck_ref, dcv_ref,
):
    own = same_head()
    own_low = low(own)
    dc_ref[...] = low(stream)
    finish_weight("co")
    datt = low(product(dc_ref[...], square(wco), 1, 1))
    for row in range(BATCHES):
        part = pl.ds(TOKENS * row, TOKENS)
        keys = pl.ds(STATES * row, STATES)
        for group in range(GROUPS):
            lanes = pl.ds(GROUP * group, GROUP)
            left = GROUP * group
            dout = spread_heads(
                datt[TOKENS * row : TOKENS * (row + 1), left : left + GROUP], own_low
            )
            spread = spread_heads(cq_ref[part, lanes], own_low)
            chance = cp_ref[row, lanes]
            dchance = product(dout, cv_ref[keys, lanes], 1, 1)
            dcv_ref[keys, lanes] = low(product(low(chance), dout, 0, 0))
            inner = jnp.sum(chance * dchance, axis=-1, keepdims=True)
            dscore = low(chance * (dchance - inner))
            dcq_ref[part, lanes] = low(fold_heads(product(dscore, ck_ref[keys, lanes]), own))
            dck_ref[keys, lanes] = low(product(dscore, spread, 0, 0))
    finish_weight("cq")
    grad = product(dcq_ref[...], square(wcq), 1, 1)
    back, dgain = norm_back(grad, a2_ref[...], gains_ref[1:2])
    return stream + back, dgain


def self_back(
    stream, finish_weight, gains_ref, x_ref, q_ref, k_ref, v_ref, p_ref, wq, wk, wv, wo,
    dself_ref, dq_ref, dk_ref, dv_ref, dscore_ref,
):
    own = same_head()
    own_low = low(own)
    dself_ref[...] = low(stream)
    finish_weight("o")
    datt = low(product(dself_ref[...], square(wo), 1, 1))
    for row in range(BATCHES):
        part = pl.ds(TOKENS * row, TOKENS)
        for group in range(GROUPS):
            lanes = pl.ds(GROUP * group, GROUP)
            left = GROUP * group
            dout = spread_heads(
                datt[TOKENS * row : TOKENS * (row + 1), left : left + GROUP], own_low
            )
            spread = spread_heads(q_ref[part, lanes], own_low)
            chance = p_ref[row, lanes]
            dchance = product(dout, v_ref[part, lanes], 1, 1)
            dv_ref[part, lanes] = low(product(low(chance), dout, 0, 0))
            inner = jnp.sum(chance * dchance, axis=-1, keepdims=True)
            dscore = low(chance * (dchance - inner))
            if dscore_ref is not None:
                if row == 0:
                    dscore_ref[lanes] = dscore.astype(jnp.float32)
                else:
                    dscore_ref[lanes] += dscore.astype(jnp.float32)
            dq_ref[part, lanes] = low(fold_heads(product(dscore, k_ref[part, lanes]), own))
            dk_ref[part, lanes] = low(product(dscore, spread, 0, 0))
    finish_weight("q")
    grad = product(dq_ref[...], square(wq), 1, 1)
    finish_weight("k")
    grad = grad + product(dk_ref[...], square(wk), 1, 1)
    finish_weight("v")
    grad = grad + product(dv_ref[...], square(wv), 1, 1)
    back, dgain = norm_back(grad, x_ref[...].astype(jnp.float32), gains_ref[0:1])
    return stream + back, dgain


def hidden_kernel(
    c_ref, a3_ref, gains_ref, gate_ref, up_ref, n3_ref, hid_ref, weight, near, far,
    stream_ref, dgain_ref, keep, send,
    wg, wu, wd, gg, gu, gd0, gd1, sems, out_sems,
):
    copies = weight_copies(weight, dict(gate=wg, up=wu, down=wd), sems, (near, far))
    begin(copies, ("down", "gate0", "up0", *LATE_HIDDEN))
    sent = []

    def finish_weight(name):
        finish(copies, name)

    for index in range(RING):
        lanes = pl.ds(index * CHUNK, CHUNK)
        grad = low(product(hid_ref[:, lanes], c_ref[...], 0, 0))
        grad = grad.reshape(RING, FF // PARTS, WIDE)
        gd0[:, index] = grad[:, : FF // PARTS // 2]
        gd1[index] = grad[:, FF // PARTS // 2 :]
    for part, tall in enumerate((gd0, gd1)):
        for piece in range(GROUPS):
            for block in range(4):
                source = tall.at[:, :, pl.ds(16 * block, 16), pl.ds(GROUP * piece, GROUP)]
                window = (
                    slice(None),
                    slice(None),
                    pl.ds(16 * piece, 16),
                    pl.ds(FF + GROUP * block, GROUP),
                )
                sent.append(push(source, keep, send, part, window, out_sems.at[len(sent)]))

    def emit(index, lanes, dgate, dup):
        for part, slot, grad in ((0, gg, dgate), (1, gu, dup)):
            put_square(slot, part, lanes, low(product(n3_ref[...], grad, 0, 0)))
            window = columns(index * CHUNK, CHUNK)
            sent.append(
                push(slot.at[window], keep, send, part, window, out_sems.at[len(sent)])
            )

    stream, dgain = hidden_back(
        finish_weight, emit, c_ref, a3_ref, gains_ref, gate_ref, up_ref, wg, wu, wd
    )
    stream_ref[...] = stream
    dgain_ref[...] = dgain
    for copy in sent:
        copy.wait()


def cross_kernel(
    stream_ref, gains_ref, a2_ref, cq_ref, ck_ref, cv_ref, cp_ref, weight,
    next_ref, dgain_ref, dc_ref, dcq_ref, dck_ref, dcv_ref,
    wcq, wco, sems,
):
    copies = weight_copies(weight, dict(cq=wcq, co=wco), sems)
    begin(copies, ("co", "cq"))

    def finish_weight(name):
        finish(copies, name)

    stream, dgain = cross_back(
        stream_ref[...], finish_weight, gains_ref, a2_ref, cq_ref, ck_ref, cv_ref, cp_ref,
        wcq, wco, dc_ref, dcq_ref, dck_ref, dcv_ref,
    )
    next_ref[...] = stream
    dgain_ref[...] = dgain


def self_kernel(
    stream_ref, x_ref, gains_ref, q_ref, k_ref, v_ref, p_ref,
    enc_ref, n1_ref, o_ref, n2_ref, co_ref, dc_ref, dcq_ref, dck_ref, dcv_ref, weight,
    da_ref, dgain_ref, dscore_ref, denc_ref, keep, send,
    dself_ref, dq_ref, dk_ref, dv_ref,
    wq, wk, wv, wo, wck, wcv, g0, g1, g2, g3, g4, g5, g6, g7, sems, out_sems,
):
    slots = dict(q=wq, k=wk, v=wv, o=wo, ck=wck, cv=wcv)
    copies = weight_copies(weight, slots, sems)
    begin(copies, ("o", "q", "k", "v", "ck", "cv"))

    def finish_weight(name):
        finish(copies, name)

    sent = []

    def emit(slot, part, column, left, right):
        put_square(slot, part, slice(None), low(product(left[...], right[...], 0, 0)))
        window = columns(WIDE * column, WIDE)
        sent.append(push(slot, keep, send, part, window, out_sems.at[len(sent)]))

    emit(g0, 0, 0, co_ref, dc_ref)
    emit(g1, 0, 1, n2_ref, dcq_ref)
    emit(g2, 1, 0, enc_ref, dck_ref)
    emit(g3, 1, 1, enc_ref, dcv_ref)
    stream, dgain = self_back(
        stream_ref[...], finish_weight, gains_ref, x_ref, q_ref, k_ref, v_ref, p_ref,
        wq, wk, wv, wo, dself_ref, dq_ref, dk_ref, dv_ref, dscore_ref,
    )
    da_ref[...] = low(stream)
    dgain_ref[...] = dgain
    emit(g4, 0, 2, o_ref, dself_ref)
    emit(g5, 0, 3, n1_ref, dq_ref)
    emit(g6, 1, 2, n1_ref, dk_ref)
    emit(g7, 1, 3, n1_ref, dv_ref)
    finish(copies, "ck")
    finish(copies, "cv")
    for row in range(BATCHES):
        keys = pl.ds(STATES * row, STATES)
        denc_ref[keys] = low(
            product(dck_ref[keys], square(wck), 1, 1) + product(dcv_ref[keys], square(wcv), 1, 1)
        )
    for copy in sent:
        copy.wait()


def in_vmem(count):
    return [pl.BlockSpec(memory_space=pltpu.VMEM)] * count


def held(*shapes):
    return [pltpu.VMEM(shape, jnp.bfloat16) for shape in shapes]


def shape_of(dims, kind=jnp.bfloat16):
    return jax.ShapeDtypeStruct(dims, kind)


params = pltpu.CompilerParams(vmem_limit_bytes=VMEM_BYTES)


ANYWHERE = pl.BlockSpec(memory_space=pl.ANY)
DMAS = pltpu.SemaphoreType.DMA((48,))
SAVED = (
    (ALL_TOKENS, jnp.bfloat16),
    (ALL_TOKENS, jnp.bfloat16),
    (ALL_TOKENS, jnp.bfloat16),
    (ALL_TOKENS, jnp.bfloat16),
    ((BATCHES, WIDE, TOKENS), jnp.float32),
    (ALL_TOKENS, jnp.bfloat16),
    (ALL_TOKENS, jnp.float32),
    (ALL_TOKENS, jnp.bfloat16),
    (ALL_TOKENS, jnp.bfloat16),
    ((BATCHES, WIDE, STATES), jnp.float32),
    (ALL_TOKENS, jnp.bfloat16),
    (ALL_TOKENS, jnp.float32),
    (ALL_TOKENS, jnp.bfloat16),
    (HIDDEN, jnp.float32),
    (HIDDEN, jnp.float32),
    (HIDDEN, jnp.bfloat16),
)


def run_first(x, enc, self_add, cross_add, gains, weights):
    outs = [shape_of(ALL_TOKENS), shape_of(ALL_STATES), shape_of(ALL_STATES)]
    return pl.pallas_call(
        first_kernel,
        out_shape=outs,
        in_specs=in_vmem(5) + [ANYWHERE] * 3,
        out_specs=in_vmem(len(outs)),
        scratch_shapes=[pltpu.VMEM(dims, kind) for dims, kind in SAVED]
        + held(*[FULL] * 8, GATED, GATED, DOWN)
        + [pltpu.SemaphoreType.DMA((48,))],
        compiler_params=params,
        name="first_forward",
    )(x, enc, self_add, cross_add, gains, *weights)


def run_turn(x, ck, cv, self_add, cross_add, gains, cotangent, weights):
    saved = [shape_of(dims, kind) for dims, kind in SAVED]
    return pl.pallas_call(
        turn_kernel,
        out_shape=[shape_of(ALL_TOKENS)] * 2 + saved,
        in_specs=in_vmem(7) + [ANYWHERE] * 3,
        out_specs=in_vmem(2) + [ANYWHERE] * len(saved),
        scratch_shapes=[pltpu.VMEM(dims, kind) for dims, kind in SAVED]
        + held(ALL_TOKENS, ALL_TOKENS, ALL_STATES, ALL_STATES, *[ALL_TOKENS] * 4)
        + held(*[FULL] * 6, GATED, GATED, DOWN)
        + [DMAS, DMAS],
        compiler_params=params,
        name="forward_and_back",
    )(x, ck, cv, self_add, cross_add, gains, cotangent, *weights)


HALF = (RING, RING, ROWS_OWN, ATT // 2)
RINGED = (RING, RING, ROWS_OWN, WIDE)
RINGED_WIDE = (RING, RING, ROWS_OWN, FF)
RINGED_TALL = (RING, RING, FF // PARTS // 2, WIDE)


def run_hidden(cotangent, gains, saved, weights):
    (ck, cv, n1, q, k, v, p, o, a2, n2, cq, cp, co, a3, n3, gate, up, hid) = saved
    return pl.pallas_call(
        hidden_kernel,
        out_shape=[
            shape_of(ALL_TOKENS, jnp.float32),
            shape_of((1, WIDE), jnp.float32),
            shape_of(HALF),
            shape_of(HALF),
        ],
        in_specs=in_vmem(7) + [ANYWHERE] * 3,
        out_specs=in_vmem(2) + [ANYWHERE, ANYWHERE],
        scratch_shapes=held(
            GATED, GATED, DOWN, RINGED_WIDE, RINGED_WIDE, RINGED_TALL, RINGED_TALL
        )
        + [DMAS, DMAS],
        compiler_params=params,
        name="hidden_backward",
    )(cotangent, a3, gains, gate, up, n3, hid, *weights)


def run_cross(stream, gains, saved, weight):
    (ck, cv, n1, q, k, v, p, o, a2, n2, cq, cp, co, a3, n3, gate, up, hid) = saved
    return pl.pallas_call(
        cross_kernel,
        out_shape=[
            shape_of(ALL_TOKENS, jnp.float32),
            shape_of((1, WIDE), jnp.float32),
            shape_of(ALL_TOKENS),
            shape_of(ALL_TOKENS),
            shape_of(ALL_STATES),
            shape_of(ALL_STATES),
        ],
        in_specs=in_vmem(7) + [ANYWHERE],
        out_specs=in_vmem(6),
        scratch_shapes=held(FULL, FULL) + [DMAS],
        compiler_params=params,
        name="cross_backward",
    )(stream, gains, a2, cq, ck, cv, cp, weight)


def run_self(stream, x, gains, enc, saved, records, weight):
    (ck, cv, n1, q, k, v, p, o, a2, n2, cq, cp, co, a3, n3, gate, up, hid) = saved
    return pl.pallas_call(
        self_kernel,
        out_shape=[
            shape_of(ALL_TOKENS),
            shape_of((1, WIDE), jnp.float32),
            shape_of((WIDE, TOKENS), jnp.float32),
            shape_of(ALL_STATES),
            shape_of(HALF),
            shape_of(HALF),
        ],
        in_specs=in_vmem(16) + [ANYWHERE],
        out_specs=in_vmem(4) + [ANYWHERE, ANYWHERE],
        scratch_shapes=held(*[ALL_TOKENS] * 4, *[FULL] * 6, *[RINGED] * 8) + [DMAS, DMAS],
        compiler_params=params,
        name="self_backward",
    )(stream, x, gains, q, k, v, p, enc, n1, o, n2, co, *records, weight)


def pack_kernel(
    query_ref, kv_ref, out_ref, c_query_ref, c_kv_ref, c_out_ref, in_ref, ffn_ref,
    kept, given, kept_tall, given_tall,
):
    def write(part, target, tall):
        if part == 0:
            pair, first, last = kv_ref[...].astype(jnp.float32), query_ref, out_ref
        else:
            pair, first, last = c_kv_ref[...].astype(jnp.float32), c_query_ref, c_out_ref
        members = (first[...], low(pair[:, 0, :]), low(pair[:, 1, :]), last[...])
        for place, member in enumerate(members):
            start = FF + WIDE * place
            target[:, start : start + WIDE] = member
        target[:, :FF] = low(in_ref[...].astype(jnp.float32)[:, part, :])
        tall[...] = ffn_ref[pl.ds(TALL * part, TALL)]

    for part in range(2):

        @pl.when(core_is(part))
        def _():
            write(part, kept, kept_tall)
            write(1 - part, given, given_tall)


def run_pack(members):
    return pl.pallas_call(
        pack_kernel,
        out_shape=[shape_of((ROWS_OWN, SHARE))] * 2 + [shape_of((TALL, WIDE))] * 2,
        in_specs=in_vmem(8),
        out_specs=in_vmem(4),
        compiler_params=params,
        name="pack_weights",
    )(*members)


def add_kernel(left, right, total):
    total[...] = low(left[...].astype(jnp.float32) + right[...].astype(jnp.float32))


def add_halves(keep, received):
    dims = (WIDE, ATT // 2)
    spec = pl.BlockSpec((256, ATT // 2), lambda place: (place, 0))
    return pl.pallas_call(
        add_kernel,
        out_shape=shape_of(dims),
        grid=(3,),
        in_specs=[spec, spec],
        out_specs=spec,
        compiler_params=params,
        name="add_halves",
    )(keep.reshape(dims), received.reshape(dims))


def unpack_kernel(
    mine, theirs, query_ref, kv_ref, out_ref, c_query_ref, c_kv_ref, c_out_ref, in_ref, ffn_ref
):
    def write(first, second):
        def square_at(part, place):
            start = ATT // 2 + WIDE * place
            return part[:, start : start + WIDE].astype(jnp.float32)

        c_out_ref[...] = square_at(first, 0)
        c_query_ref[...] = square_at(first, 1)
        out_ref[...] = square_at(first, 2)
        query_ref[...] = square_at(first, 3)
        c_kv_ref[:, 0, :] = square_at(second, 0)
        c_kv_ref[:, 1, :] = square_at(second, 1)
        kv_ref[:, 0, :] = square_at(second, 2)
        kv_ref[:, 1, :] = square_at(second, 3)
        for index, part in enumerate((first, second)):
            in_ref[:, index, :] = part[:, :FF].astype(jnp.float32)
            for piece in range(GROUPS):
                for block in range(4):
                    rows = pl.ds(64 * index + 16 * block, 16)
                    taken = part[pl.ds(16 * piece, 16), pl.ds(FF + GROUP * block, GROUP)]
                    ffn_ref[rows, pl.ds(GROUP * piece, GROUP)] = taken.astype(jnp.float32)

    @pl.when(core_is(0))
    def _():
        write(mine, theirs)

    @pl.when(core_is(1))
    def _():
        write(theirs, mine)


def run_unpack(mine, theirs):
    wide = jnp.float32
    square_dims, pair_dims = (ROWS_OWN, WIDE), (ROWS_OWN, 2, WIDE)
    outs = [square_dims, pair_dims, square_dims, square_dims, pair_dims, square_dims]
    outs += [(ROWS_OWN, 2, FF), (FF // PARTS, WIDE)]
    return pl.pallas_call(
        unpack_kernel,
        out_shape=[shape_of(dims, wide) for dims in outs],
        in_specs=in_vmem(2),
        out_specs=in_vmem(8),
        compiler_params=pltpu.CompilerParams(vmem_limit_bytes=10 * 1024 * 1024),
        name="unpack_gradients",
    )(mine, theirs)


def score_terms(table, dec_ids, enc_ids):
    positions = jnp.arange(TOKENS)
    by_distance = jnp.dot(table.astype(jnp.float32).T, bucket_onehot(TOKENS), precision=highest)
    bias = spread_distance(by_distance)
    allowed = (dec_ids[:, :, None] == dec_ids[:, None, :]) & (
        positions[None, :] <= positions[:, None]
    )
    self_add = jnp.where(allowed[:, None], bias[None], -jnp.inf)
    cross_add = jnp.where(dec_ids[:, :, None] == enc_ids[:, None, :], 0.0, -jnp.inf)
    return self_add.reshape(BATCHES, WIDE, TOKENS), cross_add


def shards(
    layer_in,
    cotangent,
    encoder,
    dec_segments,
    enc_segments,
    norm_gains,
    self_query,
    self_kv,
    self_out,
    rel_bias,
    cross_query,
    cross_kv,
    cross_out,
    ffn_in,
    ffn_out,
):
    core = lax.axis_index("section")
    part_index = lax.axis_index("fsdp")
    plane = lax.axis_index("rep")
    planes = lax.axis_size("rep")
    layer = lax.rem(plane, 2)
    first_core = core == 0
    at_home = core == layer

    def place(core_index, plane_index):
        return core_index * planes + plane_index

    def flip_core(value):
        return lax.ppermute(value, "section", [(0, 1), (1, 0)])

    def from_home(value):
        pairs = [(place(p % 2, p), place(1 - p % 2, p)) for p in range(planes)]
        return jnp.where(at_home, value, lax.ppermute(value, ("section", "rep"), pairs))

    def beside(value):
        return lax.ppermute(value, "rep", [(p, p ^ 1) for p in range(planes)])

    def to_home(value):
        pairs = [(place(1 - p % 2, p), place(1 - p % 2, p ^ 1)) for p in range(planes)]
        return lax.ppermute(value, ("section", "rep"), pairs)

    def rows_for_layer(value):
        pairs = [(place(p % 2, p), place(p % 2, p ^ 1)) for p in range(planes)]
        return jnp.where(at_home, value, lax.ppermute(value, ("section", "rep"), pairs))

    def rows_back(value):
        pairs = [(place(1 - p % 2, p), place(p % 2, p ^ 1)) for p in range(planes)]
        return jnp.where(at_home, value, lax.ppermute(value, ("section", "rep"), pairs))

    def between_layers(value, steps):
        pairs = [(p, p + steps) for p in range(planes) if p % 2 == (steps < 0)]
        return lax.ppermute(value, "rep", pairs)

    along_z = [[RING * x + z for z in range(RING)] for x in range(RING)]
    along_x = [[RING * x + z for x in range(RING)] for z in range(RING)]
    first_rings = along_z + [[PARTS + d for d in ring] for ring in along_x]
    second_rings = along_x + [[PARTS + d for d in ring] for ring in along_z]

    def scatter(value, rings):
        return lax.psum_scatter(
            value, ("section", "fsdp"), scatter_dimension=0, axis_index_groups=rings, tiled=True
        )

    kept, given_away, kept_tall, given_tall = run_pack(
        [
            member[0]
            for member in (
                self_query,
                self_kv,
                self_out,
                cross_query,
                cross_kv,
                cross_out,
                ffn_in,
                ffn_out,
            )
        ]
    )
    half = jnp.where(at_home, kept, flip_core(given_away))
    tall = jnp.where(at_home, kept_tall, flip_core(given_tall))
    weight = lax.all_gather(half, ("fsdp", "section"), axis=0, tiled=True)
    weight = weight.reshape(PARTS, 2, ROWS_OWN, SHARE)
    small = jnp.zeros((SMALL, WIDE), jnp.bfloat16)
    small = small.at[:3, :ROWS_OWN].set(norm_gains[0])
    small = small.at[3:5, :HEADS].set(rel_bias[0])

    def step_x(value, count):
        pairs = [
            (RING * x + z, RING * ((x + count) % RING) + z)
            for x in range(RING)
            for z in range(RING)
        ]
        return lax.ppermute(value, "fsdp", pairs)

    def step_z(value, count):
        pairs = [
            (RING * x + z, RING * x + (z + count) % RING)
            for x in range(RING)
            for z in range(RING)
        ]
        return lax.ppermute(value, "fsdp", pairs)

    block = jnp.concatenate([tall, from_home(small)], axis=0)
    line = jnp.stack([block, step_x(block, 1), step_x(block, 2), step_x(block, 3)])
    behind, ahead = step_z(line, 1), step_z(line, 3)
    middle = jnp.concatenate([step_z(behind[:2], 1), step_z(ahead[2:], 3)], axis=0)
    near = jnp.stack([line, behind, middle, ahead])
    far = flip_core(near)
    small = near[:, :, TALL : TALL + 8, :128]
    for axis, position in ((0, lax.rem(part_index, RING)), (1, lax.div(part_index, RING))):
        small = jnp.flip(small, axis)
        small = jnp.concatenate([small, small], axis=axis)
        small = lax.dynamic_slice_in_dim(small, RING - 1 - position, RING, axis)
    small = small.transpose(1, 0, 2, 3).reshape(PARTS, 8, 128)
    gains = small[:, :3, :ROWS_OWN].transpose(1, 0, 2).reshape(3, WIDE).astype(jnp.float32)
    table = small[:, 3:5, :HEADS].reshape(BUCKETS, HEADS)
    ids = jnp.concatenate([dec_segments[:, 0], enc_segments[:, 0]], axis=1)
    ids = rows_for_layer(ids)
    self_add, cross_add = score_terms(table, ids[:, :TOKENS], ids[:, TOKENS:])
    ends = jnp.stack([layer_in[:, 0].reshape(ALL_TOKENS), cotangent[:, 0].reshape(ALL_TOKENS)])
    ends = rows_for_layer(ends)
    rows_in, given = ends[0], ends[1]
    enc = rows_for_layer(encoder[:, 0].reshape(ALL_STATES))
    weight, near, far, rows_in, given, enc, self_add, cross_add, gains = lax.optimization_barrier(
        (weight, near, far, rows_in, given, enc, self_add, cross_add, gains)
    )
    weights = (weight, near, far)
    first, ck, cv = run_first(rows_in, enc, self_add, cross_add, gains, weights)
    current = jnp.where(layer == 0, rows_in, between_layers(first, 1))
    result, grad_first, *saved = run_turn(
        current, ck, cv, self_add, cross_add, gains, given, weights
    )
    saved = [ck, cv] + saved
    incoming = jnp.where(layer == 1, given, between_layers(grad_first, -1))
    stream, gain_three, keep, send = run_hidden(incoming, gains, saved, weights)
    received = flip_core(send)
    stream, gain_two, *records = run_cross(stream, gains, saved, weight)
    wide_sum = add_halves(keep, received)
    wide_sum, stream = lax.optimization_barrier((wide_sum, stream))
    wide_part = scatter(wide_sum, first_rings)
    grad_input, gain_one, grad_scores, grad_enc, keep, send = run_self(
        stream, current, gains, enc, saved, records, weight
    )
    square_part = scatter(add_halves(keep, flip_core(send)), first_rings)
    grad_gains = jnp.concatenate([gain_one, gain_two, gain_three], axis=0)
    diagonal_sums = gather_distance(grad_scores.reshape(HEADS, TOKENS, TOKENS))
    grad_table = jnp.dot(bucket_onehot(TOKENS), diagonal_sums.T, precision=highest)
    little = jnp.zeros((8, WIDE), jnp.float32)
    little = little.at[:3].set(grad_gains)
    little = little.at[3, : BUCKETS * HEADS].set(grad_table.reshape(-1))

    def add_pairs(value, axis, bits):
        for bit in bits:
            pairs = [(index, index ^ bit) for index in range(lax.axis_size(axis))]
            value = value + lax.ppermute(value, axis, pairs)
        return value

    little = add_pairs(add_pairs(little, "section", (1,)), "fsdp", (1, 2, 4, 8))
    outs = rows_back(jnp.stack([result, grad_input]))
    wide_part, square_part, little, outs, other_enc = lax.optimization_barrier(
        (wide_part, square_part, little, outs, to_home(grad_enc))
    )
    partial = scatter(jnp.concatenate([wide_part, square_part], axis=1), second_rings)
    little = add_pairs(little, "rep", (2,))
    little = jnp.where(at_home, little, beside(little))
    own_gains = lax.dynamic_slice(little, (0, part_index * ROWS_OWN), (3, ROWS_OWN))
    own_table = lax.dynamic_slice(little, (3, part_index * 2 * HEADS), (1, 2 * HEADS))
    encoder_total = grad_enc.astype(jnp.float32) + other_enc.astype(jnp.float32)
    encoder_total = from_home(encoder_total)
    own_table = own_table.reshape(2, HEADS)
    results = (
        outs[0].reshape(1, BATCHES, 1, TOKENS, WIDE),
        outs[1].reshape(1, BATCHES, 1, TOKENS, WIDE),
        encoder_total.reshape(BATCHES, 1, STATES, WIDE),
        own_gains[None],
        own_table[None],
    )
    partial, results = lax.optimization_barrier((partial, results))
    up = [(p, (p + 1) % planes) for p in range(planes)]
    down = [(p, (p - 1) % planes) for p in range(planes)]
    across = [(p, (p + 2) % planes) for p in range(planes)]
    cut = ATT // 2
    outer = (plane == 0) | (plane == planes - 1)
    lower = plane < 2
    rising = lax.ppermute(jnp.where(outer, partial[:, :cut], partial[:, cut:]), "rep", up)
    falling = lax.ppermute(jnp.where(outer, partial[:, cut:], partial[:, :cut]), "rep", down)
    here = low(rising.astype(jnp.float32) + falling.astype(jnp.float32))
    below = lax.ppermute(here, "rep", up)
    above = lax.ppermute(here, "rep", down)
    beyond = lax.ppermute(here, "rep", across)
    own_layer = (jnp.where(outer, above, below), jnp.where(outer, below, above))
    other_layer = (jnp.where(lower, here, beyond), jnp.where(lower, beyond, here))
    pairs = list(zip(own_layer, other_layer))
    mine = jnp.concatenate([jnp.where(at_home, own, other) for own, other in pairs], axis=1)
    away = jnp.concatenate([jnp.where(at_home, other, own) for own, other in pairs], axis=1)
    query, kv, out, *others = [member[None] for member in run_unpack(mine, flip_core(away))]
    return (*results[:4], query, kv, out, results[4], *others)


def solution(mesh):
    return jax.shard_map(
        shards,
        mesh=mesh,
        in_specs=(
            P(None, ("fsdp", "rep"), None, None),
            P(None, ("fsdp", "rep"), None, None),
            P(None, ("fsdp", "rep"), None, None),
            P(None, ("fsdp", "rep"), None),
            P(None, ("fsdp", "rep"), None),
            P("section", None, "fsdp"),
            P("section", "fsdp", None),
            P("section", "fsdp", None, None),
            P("section", "fsdp", None),
            P("section", "fsdp", None),
            P("section", "fsdp", None),
            P("section", "fsdp", None, None),
            P("section", "fsdp", None),
            P("section", "fsdp", None, None),
            P("section", "fsdp", None),
        ),
        out_specs=(
            P("section", None, ("fsdp", "rep"), None, None),
            P("section", None, ("fsdp", "rep"), None, None),
            P(None, ("fsdp", "rep"), None, None),
            P("section", None, "fsdp"),
            P("section", "fsdp", None),
            P("section", "fsdp", None, None),
            P("section", "fsdp", None),
            P("section", "fsdp", None),
            P("section", "fsdp", None),
            P("section", "fsdp", None, None),
            P("section", "fsdp", None),
            P("section", "fsdp", None, None),
            P("section", "fsdp", None),
        ),
        check_vma=False,
    )
```
